256 devices in a mesh: px: 32 (over z, x), py: 8 (over y, core).
Axes of the slice: x: 4, y: 4, z: 8, core: 2. Of those that a mesh axis runs over, the one named last changes fastest.
Arguments:
- corr: float32 [3, 256, 256, 256], P(None, 'px', 'py'), may hold values from -6 to 6
- solute_pot: bfloat16 [3, 256, 256, 256], P(None, 'px', 'py'), may hold values from -8 to 8
- chi: float32 [3, 3, 2, 128, 256, 256], P(None, None, None, 'py', 'px'), may hold values from -1 to 2, as said below
- site_charge: float32 [3], replicated, may hold values from -1 to 1
- home_slab: int32 [8192, 1], P(('px', 'py')), may hold values from 0 to 31; in each aligned block of 32 rows (0 to 31, 32 to 63, ...) at most 4 rows name the same one
- brick_index: int32 [8192], P(('px', 'py')), may hold values from 0 to 127
- block_slot: int32 [256, 32], P(('px', 'py')), may hold values from 0 to 31, each once within a row
- basis_values: bfloat16 [8192, 512, 128], P(('px', 'py')), may hold values from -0.25 to 0.25
- fock_in: float32 [8192, 128, 128], P(('px', 'py')), may hold values from -6 to 6
Outputs:
- corr_next: float32 [3, 256, 256, 256], P(None, 'px', 'py')
- potential: float32 [256, 256, 256], P('px', 'py')
- fock_out: float32 [8192, 128, 128], P(('px', 'py'))
The draws below stay inside these ranges and needn't reach their ends.
Inputs may be any that keep to these rules, and one draw needn't show every extreme that they name: Among the 32 fragments of one device at most 4 have the same home_slab, and in every draw some device has 4 fragments with one home_slab. `block_slot`: each row is a permutation of 0 to 31. chi at wave vector (kx, kz, ky) equals chi at ((-kx) mod 256, (-kz) mod 256, (-ky) mod 256).
All inputs are finite; a program needn't handle non-finite values.
Results may differ from the reference program's by a relative error of at most 0.0011.
Values may be sent and summed in bfloat16 or wider, within the bound.
A program may use at most 128 MiB of HBM per device.

```python
import math
import jax
import jax.numpy as jnp
import numpy as np
from jax import lax

NGRID = 256
SITES = 3
BASIS = 128
BRICK = 8
MOST = 4
FRAG_DEV = 32
FRAGS = 8192
BRICKS_DEV = 128
BCELLS = 512
N_PX = 32
N_PY = 8


def draw_chi(key, part):
    key = jax.random.fold_in(key, 11)
    shape = (SITES, SITES, NGRID, NGRID, NGRID)
    unit = jax.random.uniform(key, shape, jnp.float32)
    diag_low, diag_high, off_low, off_high = (0.3, 1.5, -0.6, 0.6)
    identity = jnp.eye(SITES, dtype=jnp.float32)[:, :, None, None, None]
    values = identity * (diag_low + (diag_high - diag_low) * unit) + (1.0 - identity) * (off_low + (off_high - off_low) * unit)
    mirrored = jnp.roll(jnp.flip(values, axis=(2, 3, 4)), 1, axis=(2, 3, 4))
    return (0.5 * (values + mirrored)).reshape(SITES, SITES, 2, NGRID // 2, NGRID, NGRID)


def place_ends(result, rng, low, top_value):
    index_at = [jax.random.randint(jax.random.fold_in(rng, axis), (), 0, length) for axis, length in enumerate(result.shape)]
    longest = result.shape.index(max(result.shape))
    next_to = index_at[:longest] + [(index_at[longest] + 1) % result.shape[longest]] + index_at[longest + 1:]
    return result.at[tuple(index_at)].set(low).at[tuple(next_to)].set(top_value)


def block_scale(rng, dims, shards, low, largest):
    factor_of, own = 1.0, jax.random.fold_in(rng, 6)
    for position, parts in shards:
        heights = jnp.exp(jax.random.uniform(jax.random.fold_in(own, position), (parts,), jnp.float32, low / len(shards), largest / len(shards)))
        factor_of = factor_of * jnp.repeat(heights, dims[position] // parts).reshape([-1 if axis == position else 1 for axis in range(len(dims))])
    return factor_of


def assign_block(own_key, own, number, rows, number_of, top, most, slope):
    ranking = jax.random.permutation(own_key, number_of)
    heavy_load, ordinary = load_shares(number_of, rows * top, most, slope, True), load_shares(number_of, rows * top, most, slope, False)
    places = jnp.arange(number_of)

    def named(tallies, turn):
        used = int((tallies > 0).sum())
        fixed = max(1, used // 4)
        passed = fixed + (places - fixed + turn * (used - fixed)) % max(1, number_of - fixed)
        return jnp.zeros((number_of,), jnp.int32).at[ranking[jnp.where(places < fixed, places, passed)]].set(jnp.asarray(tallies, jnp.int32))

    tallies = jnp.where(number % 4 == 0, named(heavy_load, number // 4), named(ordinary, number - number // 4 - 1))
    mixed = jax.random.permutation(jax.random.fold_in(own, 3), number_of)
    source_of, taker = mixed[0:number_of // 2 * 2:2], mixed[1:number_of // 2 * 2:2]
    room = jnp.minimum(tallies[source_of] - 1, most - tallies[taker]) // 2
    room = jnp.where((source_of == ranking[0]) | (taker == ranking[0]) | (tallies[taker] == 0), 0, jnp.maximum(room, 0))
    passed = jax.random.randint(jax.random.fold_in(own, 4), (number_of // 2,), 0, 1 << 20) % (room + 1)
    tallies = tallies.at[source_of].add(-passed).at[taker].add(passed)
    items = jnp.searchsorted(jnp.cumsum(tallies), jnp.arange(rows * top), side="right").astype(jnp.int32)
    table = items.reshape(top, rows).T
    table = table[jax.random.permutation(jax.random.fold_in(own, 1), rows)]
    turn = jax.random.randint(jax.random.fold_in(own, 2), (rows, 1), 0, top)
    return jnp.take_along_axis(table, (jnp.arange(top)[None, :] + turn) % top, axis=1)


def load_shares(count, total, bound, lean, full):
    portions = [(1 << 20) // math.isqrt(rank ** lean) + 1 for rank in range(1, count + 1)]
    largest = bound if full else min(bound, max(-(-total // count), total * portions[0] // sum(portions)))
    least = 1 if total - largest >= count - 1 else 0
    holding, spare = [largest] + [least] * (count - 1), total - largest - least * (count - 1)
    while spare > 0:
        free = [i for i in range(1, count) if holding[i] < largest] or [i for i in range(1, count) if holding[i] < bound]
        whole, budget = sum([portions[i] for i in free]), spare
        for i in free:
            more = min(bound - holding[i], max(1, budget * portions[i] // whole), spare)
            holding[i] = holding[i] + more
            spare = spare - more
    return np.array(holding)


def noise(stream_key, dims, spread, reach, split=(), held_as=jnp.bfloat16):
    drawn = spread * jax.random.normal(stream_key, dims, jnp.float32)
    if split:
        drawn = drawn * block_scale(stream_key, dims, split, -0.22, 0.18)
    return jnp.clip(drawn, -reach, reach).astype(held_as)


def setup_inputs(seed: int = 0) -> dict:
    key_list = jax.random.split(jax.random.key(seed), 10)
    corr = noise(key_list[0], (SITES, NGRID, NGRID, NGRID), 1.0, 6.0, ((1, 32), (2, 8)), jnp.float32)
    solute_pot = noise(key_list[1], (SITES, NGRID, NGRID, NGRID), 1.5, 8.0, ((1, 32), (2, 8)))
    chi = draw_chi(jax.random.fold_in(key_list[9], 71), 0)
    site_charge = jnp.clip(jax.random.uniform(key_list[3], (SITES,), jnp.float32, -1.0, 1.0), -1.0, 1.0)
    home_slab_keys = jax.random.split(jax.random.fold_in(key_list[4], 1), FRAGS // FRAG_DEV)
    home_slab_turns = jax.random.permutation(jax.random.fold_in(key_list[4], 3), FRAGS // FRAG_DEV)
    home_slab = jax.vmap(lambda own, number: assign_block(jax.random.fold_in(key_list[4], 2), own, number, FRAG_DEV, N_PX, 1, MOST, 2))(home_slab_keys, home_slab_turns).reshape((FRAGS, 1))
    brick_index = place_ends(jax.random.randint(key_list[5], (FRAGS,), 0, BRICKS_DEV), jax.random.fold_in(key_list[5], 1), 0, BRICKS_DEV - 1).astype(jnp.int32)
    block_slot = jax.vmap(lambda own: jax.random.permutation(own, FRAG_DEV))(jax.random.split(key_list[6], (N_PX * N_PY))).reshape((N_PX * N_PY, FRAG_DEV)).astype(jnp.int32)
    basis_values = noise(key_list[7], (FRAGS, BCELLS, BASIS), BCELLS ** -0.5, 0.25, ((0, 256),))
    fock_in = noise(key_list[8], (FRAGS, BASIS, BASIS), 1.0, 6.0, ((0, 256),), jnp.float32)
    return {"corr": corr, "solute_pot": solute_pot, "chi": chi, "site_charge": site_charge, "home_slab": home_slab, "brick_index": brick_index, "block_slot": block_slot, "basis_values": basis_values, "fock_in": fock_in}


SCREEN = 1.0
HIGH = lax.Precision.HIGHEST


def closure(corr, solute_pot):
    excess = corr - solute_pot.astype(jnp.float32)
    total_corr = jnp.where(excess > 0, excess, jnp.expm1(jnp.minimum(excess, 0.0)))
    return total_corr - corr


def signed_wave(index, length):
    shifted = (index + length // 2) % length - length // 2
    return shifted.astype(jnp.float32) * (2.0 * jnp.pi / length)


def reference(corr, solute_pot, chi, site_charge, home_slab, brick_index, block_slot, basis_values, fock_in):
    direct = closure(corr, solute_pot)
    direct_k = jnp.fft.fftn(direct, axes=(1, 2, 3))
    direct_re = jnp.real(direct_k).astype(jnp.float32)
    direct_im = jnp.imag(direct_k).astype(jnp.float32)
    total_re = []
    total_im = []
    for site_a in range(SITES):
        acc_re = jnp.zeros_like(direct_re[0])
        acc_im = jnp.zeros_like(direct_im[0])
        for site_b in range(SITES):
            factor = jnp.transpose(chi[site_a, site_b].reshape(NGRID, NGRID, NGRID), (2, 1, 0))
            acc_re = acc_re + factor * direct_re[site_b]
            acc_im = acc_im + factor * direct_im[site_b]
        total_re.append(acc_re)
        total_im.append(acc_im)
    total_re = jnp.stack(total_re)
    total_im = jnp.stack(total_im)
    ind_re = total_re - direct_re
    ind_im = total_im - direct_im
    wave_num = signed_wave(jnp.arange(NGRID, dtype=jnp.int32), NGRID)
    screened = 4.0 * jnp.pi / (wave_num[:, None, None] ** 2 + wave_num[None, :, None] ** 2
                              + wave_num[None, None, :] ** 2 + SCREEN * SCREEN)
    charges = site_charge[:, None, None, None]
    pot_re = screened * jnp.sum(charges * total_re, axis=0)
    pot_im = screened * jnp.sum(charges * total_im, axis=0)
    corr_next = jnp.real(jnp.fft.ifftn(lax.complex(ind_re, ind_im), axes=(1, 2, 3))).astype(jnp.float32)
    potential = jnp.real(jnp.fft.ifftn(lax.complex(pot_re, pot_im))).astype(jnp.float32)

    y_dev = NGRID // N_PX
    z_dev = NGRID // N_PY
    z_bricks = z_dev // BRICK
    x_bricks = NGRID // BRICK
    frag_ids = jnp.arange(FRAGS, dtype=jnp.int32)
    group = (frag_ids // FRAG_DEV) % N_PY
    brick_y = brick_index // (z_bricks * x_bricks)
    brick_z = (brick_index // x_bricks) % z_bricks
    brick_x = brick_index % x_bricks
    start_y = (home_slab[:, 0] * y_dev + brick_y * BRICK).astype(jnp.int32)
    start_z = (group * z_dev + brick_z * BRICK).astype(jnp.int32)
    start_x = (brick_x * BRICK).astype(jnp.int32)

    def sample_one(corner_y, corner_z, corner_x):
        return lax.dynamic_slice(potential, (corner_y, corner_z, corner_x), (BRICK, BRICK, BRICK)).reshape(-1)

    sampled = jax.vmap(sample_one)(start_y, start_z, start_x).astype(jnp.bfloat16)
    devices = N_PX * N_PY

    def fragment_block(inputs):
        basis, samples, slots, fock = inputs
        weighted = (basis.astype(jnp.float32) * samples.astype(jnp.float32)[:, :, None]).astype(jnp.bfloat16)
        embed = jnp.einsum("fcb,fcd->fbd", basis.astype(jnp.float32), weighted.astype(jnp.float32), precision=HIGH)
        return fock.at[slots].add(embed)

    fock_out = lax.map(fragment_block, (basis_values.reshape(devices, FRAG_DEV, BCELLS, BASIS),
                                        sampled.reshape(devices, FRAG_DEV, BCELLS),
                                        block_slot,
                                        fock_in.reshape(devices, FRAG_DEV, BASIS, BASIS)))
    return corr_next, potential, fock_out.reshape(FRAGS, BASIS, BASIS)
```

```python
import functools
import jax
import jax.numpy as jnp
import numpy as np
from jax import lax
from jax.experimental import pallas as pl
from jax.experimental.pallas import tpu as pltpu
from jax.sharding import PartitionSpec as P

BRICK = 8
MOST = 4
N = 256
PX = 32
PY = 8
SITES = 3
FIELDS = 4
R = 16
MESH = pl.DeviceIdType.MESH
F32 = jnp.float32
BF16 = jnp.bfloat16
WIRE = jnp.float32


def split(values):
    high = values.astype(BF16)
    return high, (values - high.astype(F32)).astype(BF16)


def np_split(values):
    high = values.astype(np.float32).astype(BF16)
    low = (values - high.astype(np.float64)).astype(np.float32).astype(BF16)
    return high, low


def tables():
    index = np.arange(N)
    angle = (index[:, None] * index[None, :] % N) * (2.0 * np.pi / N)
    cos, sin = np.cos(angle), np.sin(angle)
    half_re = cos[:, : N // 2].copy()
    half_im = -sin[:, : N // 2]
    half_im[:, 0] = cos[:, N // 2]
    halves = np.stack([half_re.reshape(N, PY, R), half_im.reshape(N, PY, R)], axis=2)
    spread = np.broadcast_to(halves[:, :, :, None, :], (N, PY, 2, FIELDS, R))
    spread = spread.reshape(N, PY * 128)
    return np_split(spread) + np_split(cos) + np_split(sin)


def encode(values):
    return values.astype(WIRE)


def decode(values):
    return values.astype(F32)


def dot(left, right):
    return jnp.dot(left, right, preferred_element_type=F32)


def dot_nt(left, right):
    return lax.dot_general(left, right, (((1,), (1,)), ((), ())), preferred_element_type=F32)


def dot3(product, left, right):
    return product(left[0], right[0]) + product(left[0], right[1]) + product(left[1], right[0])


def closure(corr, solute_pot):
    excess = corr - solute_pot.astype(F32)
    low = jnp.minimum(excess, 0.0)
    series = jnp.full_like(low, 1.0 / 362880.0)
    for denominator in (40320.0, 5040.0, 720.0, 120.0, 24.0, 6.0, 2.0, 1.0):
        series = series * low + 1.0 / denominator
    grown = jnp.where(low > -0.5, series * low, jnp.exp(low) - 1.0)
    return jnp.where(excess > 0, excess, grown) - corr


def field_kernel(
    corr_ref, pot_ref, chi_ref, charge_ref, xh_ref, xl_ref, ch_ref, cl_ref, sh_ref, sl_ref,
    corr_out, potential_out,
    chi0, chi1, s1, b1, s2, b2, ys, s3, b3, s4, b4,
    chi_sem, send1, recv1, send2, recv2, send3, recv3, send4, recv4,
):
    px = lax.axis_index("px")
    py = lax.axis_index("py")
    barrier = pltpu.get_barrier_semaphore()

    def greet_px(step, carry):
        pl.semaphore_signal(barrier, inc=1, device_id=(lax.rem(px + step, PX), py), device_id_type=MESH)
        return carry

    def greet_py(step, carry):
        pl.semaphore_signal(barrier, inc=1, device_id=(px, lax.rem(py + step, PY)), device_id_type=MESH)
        return carry

    lax.fori_loop(1, PX, greet_px, 0)
    lax.fori_loop(1, PY, greet_py, 0)
    chi_copy0 = pltpu.make_async_copy(chi_ref.at[:, :, 0], chi0, chi_sem.at[0])
    chi_copy1 = pltpu.make_async_copy(chi_ref.at[:, :, 1, 0], chi1, chi_sem.at[1])
    chi_copy0.start()
    chi_copy1.start()

    lane = lax.broadcasted_iota(jnp.int32, (1, 128), 1)
    lane_re = lane < 64
    lane_field = lax.rem(lane // R, FIELDS)
    lane_spec = (lax.rem(lane, R) == 0) & (py == 0)

    lane_site = jnp.concatenate([lane_field, lane_field], axis=1)

    def x_forward(yp, carry):
        parts = []
        for site in range(SITES):
            rows = closure(corr_ref[site, pl.ds(2 * yp, 2)], pot_ref[site, pl.ds(2 * yp, 2)])
            parts.append(rows.reshape(64, N))
        data = split(jnp.concatenate(parts, axis=0))
        for pair in range(PY // 2):
            wide = dot3(dot, data, (xh_ref[:, 256 * pair:256 * pair + 256], xl_ref[:, 256 * pair:256 * pair + 256]))
            rows = jnp.where(lane_site == 0, wide[0:64], jnp.where(lane_site == 1, wide[64:128], wide[128:192]))
            rows = encode(jnp.where(lane_site == 3, 0.0, rows))
            s1[2 * pair, pl.ds(2 * yp, 2)] = rows[:, 0:128].reshape(2, 32, 128)
            s1[2 * pair + 1, pl.ds(2 * yp, 2)] = rows[:, 128:256].reshape(2, 32, 128)

        @pl.when(yp == 0)
        def _():
            pl.semaphore_wait(barrier, PX + PY - 2)

        pltpu.make_async_copy(
            s1.at[py, pl.ds(2 * yp, 2)], b1.at[pl.ds(2 * yp, 2), pl.ds(32 * py, 32)], recv1.at[yp]
        ).start()

        def send(step, inner):
            other = lax.rem(py + step, PY)
            pltpu.make_async_remote_copy(
                src_ref=s1.at[other, pl.ds(2 * yp, 2)],
                dst_ref=b1.at[pl.ds(2 * yp, 2), pl.ds(32 * py, 32)],
                send_sem=send1.at[yp], recv_sem=recv1.at[yp],
                device_id=(px, other), device_id_type=MESH,
            ).start()
            return inner

        return lax.fori_loop(1, PY, send, carry)

    lax.fori_loop(0, 4, x_forward, 0)

    cos = (ch_ref[...], cl_ref[...])
    sin = (sh_ref[...], sl_ref[...])
    wave = lax.broadcasted_iota(jnp.int32, (N, 1), 0)
    wave_edge = (wave == 0) | (wave == N // 2)
    wave_low = wave < N // 2
    wave_high = wave > N // 2

    def z_forward(yp, carry):
        chunk = b1.at[pl.ds(2 * yp, 2)]
        pltpu.make_async_copy(chunk, chunk, recv1.at[yp]).wait()
        data = split(jnp.concatenate([decode(b1[2 * yp]), decode(b1[2 * yp + 1])], axis=1))
        cos_data = dot3(dot, cos, data)
        sin_data = dot3(dot, sin, data)
        halves = []
        for u in range(2):
            cd = cos_data[:, 128 * u:128 * u + 128]
            sd = sin_data[:, 128 * u:128 * u + 128]
            cd_turn = pltpu.roll(cd, 64, 1)
            sd_turn = pltpu.roll(sd, 64, 1)
            usual = jnp.where(lane_re, cd + sd_turn, cd - sd_turn)
            packed_re = jnp.where(wave_high, cd_turn, cd)
            packed_im = jnp.where(wave_edge, cd, jnp.where(wave_low, -sd_turn, -sd))
            packed = jnp.where(lane_re, packed_re, packed_im)
            halves.append(jnp.where(lane_spec, packed, usual).reshape(PX, 8, 128))
        s2[:, yp] = encode(jnp.concatenate(halves, axis=1))
        pltpu.make_async_copy(s2.at[px, yp], b2.at[px, yp], recv2.at[yp]).start()

        def send(step, inner):
            other = lax.rem(px + step, PX)
            pltpu.make_async_remote_copy(
                src_ref=s2.at[other, yp], dst_ref=b2.at[px, yp],
                send_sem=send2.at[yp], recv_sem=recv2.at[yp],
                device_id=(other, py), device_id_type=MESH,
            ).start()
            return inner

        return lax.fori_loop(1, PX, send, carry)

    lax.fori_loop(0, 4, z_forward, 0)

    def collect(buffer, sem):
        def body(part, carry):
            chunk = buffer.at[:, part]
            pltpu.make_async_copy(chunk, chunk, sem.at[part]).wait()

            def place(source, inner):
                start = pl.multiple_of(source * 64 + part * 16, 16)
                ys[pl.ds(start, 16), :] = decode(buffer[source, part])
                return inner

            return lax.fori_loop(0, PX, place, carry)

        lax.fori_loop(0, 4, body, 0)

    collect(b2, recv2)
    chi_copy0.wait()
    chi_copy1.wait()

    row = lax.broadcasted_iota(jnp.int32, (R, 1), 0)
    first = (row == 0) & (py == 0)
    wave_y = lax.broadcasted_iota(jnp.int32, (1, N), 1)
    unit = 2.0 * np.pi / N

    def signed_square(index):
        shifted = (lax.rem(index + N // 2, N) - N // 2).astype(F32) * unit
        return shifted * shifted

    square_y = signed_square(wave_y)
    scale = jnp.where(first, 2.0 ** -24, 2.0 ** -23)

    def mix(chi_of, x_re, x_im, screened):
        out_re, out_im = [], []
        pot_re = pot_im = 0.0
        for a in range(SITES):
            t_re = t_im = 0.0
            for b in range(SITES):
                factor = chi_of(a, b)
                t_re = t_re + factor * x_re[b]
                t_im = t_im + factor * x_im[b]
            out_re.append((t_re - x_re[a]) * scale)
            out_im.append((t_im - x_im[a]) * scale)
            pot_re = pot_re + charge_ref[a] * t_re
            pot_im = pot_im + charge_ref[a] * t_im
        out_re.append(pot_re * (screened * scale))
        out_im.append(pot_im * (screened * scale))
        return out_re, out_im

    def y_both(kp, carry):
        plain, turned = [], []
        rows = jnp.concatenate(
            [ys[pl.ds(2 * kp + u, N, stride=8), :].T for u in range(2)], axis=0
        )
        data = split(rows)
        cos_data = dot3(dot, data, cos)
        sin_data = dot3(dot, data, sin)
        for u in range(2):
            kz = 2 * kp + u
            kz_all = px * 8 + kz
            base = 128 * u
            pick = lambda array, c, s: array[base + 64 * c + 16 * s:base + 64 * c + 16 * s + 16]
            c_re = [pick(cos_data, 0, s) for s in range(SITES)]
            c_im = [pick(cos_data, 1, s) for s in range(SITES)]
            s_re = [pick(sin_data, 0, s) for s in range(SITES)]
            s_im = [pick(sin_data, 1, s) for s in range(SITES)]
            x_re = [c_re[s] + s_im[s] for s in range(SITES)]
            x_im = [c_im[s] - s_re[s] for s in range(SITES)]
            upper = first & (kz_all > N // 2)
            kx = jnp.where(upper, N // 2, py * R + row)
            square_z = signed_square(jnp.full((1, 1), kz_all, jnp.int32))
            rest = square_z + square_y + 1.0
            screened = (4.0 * np.pi) / (signed_square(kx) + rest)
            chi_of = lambda a, b: jnp.where(upper, chi1[a, b, pl.ds(kz, 1), :], chi0[a, b, :, kz, :])
            if u == 0:
                edge = first & ((kz_all == 0) | (kz_all == N // 2))
                b_re = [c_im[s] for s in range(SITES)]
                b_im = [-s_im[s] for s in range(SITES)]
                x_re = [jnp.where(edge, c_re[s], x_re[s]) for s in range(SITES)]
                x_im = [jnp.where(edge, -s_re[s], x_im[s]) for s in range(SITES)]
                f_re, f_im = mix(chi_of, x_re, x_im, screened)
                screened = (4.0 * np.pi) / (np.pi ** 2 + rest)
                g_re, g_im = mix(lambda a, b: chi1[a, b, pl.ds(kz, 1), :], b_re, b_im, screened)
                plain += f_re + [jnp.where(edge, g_re[f], f_im[f]) for f in range(FIELDS)]
                turned += [-value for value in f_im]
                turned += [jnp.where(edge, -g_im[f], f_re[f]) for f in range(FIELDS)]
            else:
                f_re, f_im = mix(chi_of, x_re, x_im, screened)
                plain += f_re + f_im
                turned += [-value for value in f_im] + f_re
        plain = split(jnp.concatenate(plain, axis=0))
        turned = split(jnp.concatenate(turned, axis=0))
        back = dot3(dot_nt, cos, plain) + dot3(dot_nt, sin, turned)
        s3[:, kp] = encode(
            jnp.concatenate([back[:, 128 * u:128 * u + 128].reshape(PX, 8, 128) for u in range(2)], axis=1)
        )
        pltpu.make_async_copy(s3.at[px, kp], b3.at[px, kp], recv3.at[kp]).start()

        def send(step, inner):
            other = lax.rem(px + step, PX)
            pltpu.make_async_remote_copy(
                src_ref=s3.at[other, kp], dst_ref=b3.at[px, kp],
                send_sem=send3.at[kp], recv_sem=recv3.at[kp],
                device_id=(other, py), device_id_type=MESH,
            ).start()
            return inner

        return lax.fori_loop(1, PX, send, carry)

    lax.fori_loop(0, 4, y_both, 0)

    collect(b3, recv3)

    def z_backward(yp, carry):
        plain, turned = [], []
        for u in range(2):
            data = ys[pl.ds(2 * yp + u, N, stride=8), :]
            turn = pltpu.roll(data, 64, 1)
            packed_re = jnp.where(wave_edge, data, jnp.where(wave_low, data + data, 0.0))
            packed_im = jnp.where(wave_edge, data, jnp.where(wave_low, 0.0, turn + turn))
            other_re = jnp.where(wave_low & ~wave_edge, -2.0 * turn, 0.0)
            other_im = jnp.where(wave_high, -2.0 * data, 0.0)
            plain.append(jnp.where(lane_spec, jnp.where(lane_re, packed_re, packed_im), data))
            turned.append(jnp.where(
                lane_spec, jnp.where(lane_re, other_re, other_im), jnp.where(lane_re, -turn, turn)
            ))
        plain = split(jnp.concatenate(plain, axis=1))
        turned = split(jnp.concatenate(turned, axis=1))
        back = encode(dot3(dot, cos, plain) + dot3(dot, sin, turned))
        s4[2 * yp] = back[:, 0:128]
        s4[2 * yp + 1] = back[:, 128:256]
        pltpu.make_async_copy(
            s4.at[pl.ds(2 * yp, 2), pl.ds(32 * py, 32)], b4.at[py, pl.ds(2 * yp, 2)], recv4.at[yp]
        ).start()

        def send(step, inner):
            other = lax.rem(py + step, PY)
            pltpu.make_async_remote_copy(
                src_ref=s4.at[pl.ds(2 * yp, 2), pl.ds(32 * other, 32)],
                dst_ref=b4.at[py, pl.ds(2 * yp, 2)],
                send_sem=send4.at[yp], recv_sem=recv4.at[yp],
                device_id=(px, other), device_id_type=MESH,
            ).start()
            return inner

        return lax.fori_loop(1, PY, send, carry)

    lax.fori_loop(0, 4, z_backward, 0)

    def x_backward(yp, carry):
        chunk = b4.at[:, pl.ds(2 * yp, 2)]
        pltpu.make_async_copy(chunk, chunk, recv4.at[yp]).wait()
        rows = jnp.concatenate(
            [decode(b4[j, pl.ds(2 * yp, 2)]).reshape(64, 128) for j in range(PY)], axis=1
        )
        field = jnp.concatenate([lane_field] * PY, axis=1)
        data = split(jnp.concatenate([jnp.where(field == f, rows, 0.0) for f in range(FIELDS)], axis=0))
        back = dot3(dot_nt, data, (xh_ref[...], xl_ref[...]))
        for f in range(SITES):
            corr_out[f, pl.ds(2 * yp, 2)] = back[64 * f:64 * f + 64].reshape(2, 32, N)
        potential_out[pl.ds(2 * yp, 2)] = back[192:256].reshape(2, 32, N)
        return carry

    lax.fori_loop(0, 4, x_backward, 0)

    for part in range(4):
        sent = s1.at[pl.ds(0, PY - 1), pl.ds(0, 2)]
        pltpu.make_async_copy(sent, sent, send1.at[part]).wait()
        sent = s2.at[pl.ds(0, PX - 1), 0]
        pltpu.make_async_copy(sent, sent, send2.at[part]).wait()
        pltpu.make_async_copy(sent, sent, send3.at[part]).wait()
        sent = s4.at[pl.ds(0, 2), pl.ds(0, 32 * (PY - 1))]
        pltpu.make_async_copy(sent, sent, send4.at[part]).wait()


def fields(corr, solute_pot, chi, site_charge):
    vmem = pl.BlockSpec(memory_space=pltpu.VMEM)
    dma = pltpu.SemaphoreType.DMA((4,))
    return pl.pallas_call(
        field_kernel,
        name="fields",
        out_shape=(
            jax.ShapeDtypeStruct((SITES, 8, 32, N), F32),
            jax.ShapeDtypeStruct((8, 32, N), F32),
        ),
        in_specs=[vmem, vmem, pl.BlockSpec(memory_space=pl.ANY), pl.BlockSpec(memory_space=pltpu.SMEM)] + [vmem] * 6,
        out_specs=(vmem, vmem),
        scratch_shapes=[
            pltpu.VMEM((SITES, SITES, R, 8, N), F32),
            pltpu.VMEM((SITES, SITES, 8, N), F32),
            pltpu.VMEM((PY, 8, 32, 128), WIRE),
            pltpu.VMEM((8, N, 128), WIRE),
            pltpu.VMEM((PX, 4, 16, 128), WIRE),
            pltpu.VMEM((PX, 4, 16, 128), WIRE),
            pltpu.VMEM((PX * 64, 128), F32),
            pltpu.VMEM((PX, 4, 16, 128), WIRE),
            pltpu.VMEM((PX, 4, 16, 128), WIRE),
            pltpu.VMEM((8, N, 128), WIRE),
            pltpu.VMEM((PY, 8, 32, 128), WIRE),
            pltpu.SemaphoreType.DMA((2,)),
        ] + [dma] * 8,
        compiler_params=pltpu.CompilerParams(
            collective_id=0, has_side_effects=True, vmem_limit_bytes=40 * 2**20
        ),
    )(corr, solute_pot, chi, site_charge, *[jnp.asarray(table) for table in tables()])


def shards(
    corr, solute_pot, chi, site_charge, home_slab, brick_index, block_slot, basis_values, fock_in
):
    home = home_slab[:, 0]
    frags = home.shape[0]
    same = home[:, None] == home[None, :]
    earlier = jnp.arange(frags)[None, :] < jnp.arange(frags)[:, None]
    place = jnp.sum((same & earlier).astype(jnp.int32), axis=1)
    wanted = home * MOST + place
    asked = jnp.zeros((PX * MOST,), jnp.int32).at[wanted].set(brick_index)
    asked = lax.all_to_all(asked, "px", split_axis=0, concat_axis=0, tiled=True)

    corr_next, potential = fields(corr, solute_pot, chi, site_charge)

    bricks = potential.astype(BF16).reshape(1, BRICK, 4, BRICK, 32, BRICK)
    bricks = bricks.transpose(0, 2, 4, 1, 3, 5).reshape(128, 512)
    answer = jnp.take(bricks, asked, axis=0, mode="clip")
    answer = lax.all_to_all(answer, "px", split_axis=0, concat_axis=0, tiled=True)
    sampled = jnp.take(answer, wanted, axis=0, mode="clip")
    weighted = (basis_values.astype(F32) * sampled.astype(F32)[:, :, None]).astype(BF16)
    embed = jnp.einsum("fcb,fcd->fbd", basis_values, weighted, preferred_element_type=F32)
    fock_out = fock_in.at[block_slot[0]].add(embed)
    return (corr_next, potential, fock_out)


def solution(mesh):
    return jax.shard_map(
        shards,
        mesh=mesh,
        in_specs=(
            P(None, "px", "py", None),
            P(None, "px", "py", None),
            P(None, None, None, "py", "px", None),
            P(),
            P(("px", "py"), None),
            P(("px", "py")),
            P(("px", "py"), None),
            P(("px", "py"), None, None),
            P(("px", "py"), None, None),
        ),
        out_specs=(P(None, "px", "py", None), P("px", "py", None), P(("px", "py"), None, None)),
        check_vma=False,
    )
```

```python
import functools
import jax
import jax.numpy as jnp
import numpy as np
from jax import lax
from jax.experimental import pallas as pl
from jax.experimental.pallas import tpu as pltpu
from jax.sharding import PartitionSpec as P

BRICK = 8
MOST = 4
N = 256
PX = 32
PY = 8
SITES = 3
FIELDS = 4
R = 16
MESH = pl.DeviceIdType.MESH
F32 = jnp.float32
BF16 = jnp.bfloat16
WIRE = jnp.bfloat16
FINE, STEEP, SLOPE = 11.0, 8.0, 3.0
CENTRE_X, CENTRE_Z, CENTRE_Y, CENTRE_BACK = 5.0, 9.0, -5.0, -1.0


def split(values):
    high = values.astype(BF16)
    return high, (values - high.astype(F32)).astype(BF16)


def np_split(values):
    high = values.astype(np.float32).astype(BF16)
    low = (values - high.astype(np.float64)).astype(np.float32).astype(BF16)
    return high, low


def tables():
    index = np.arange(N)
    angle = (index[:, None] * index[None, :] % N) * (2.0 * np.pi / N)
    cos, sin = np.cos(angle), np.sin(angle)
    half_re = cos[:, : N // 2].copy()
    half_im = -sin[:, : N // 2]
    half_im[:, 0] = cos[:, N // 2]
    halves = np.stack([half_re.reshape(N, PY, R), half_im.reshape(N, PY, R)], axis=2)
    spread = np.broadcast_to(halves[:, :, :, None, :], (N, PY, 2, FIELDS, R))
    spread = spread.reshape(N, PY * 128)
    return np_split(spread) + np_split(cos) + np_split(sin)


def encode(values, centre):
    power = jnp.log2(jnp.abs(values)) - centre
    power = SLOPE * power + (STEEP - SLOPE) * jnp.clip(power, -FINE, FINE)
    coded = jnp.exp2(power)
    return jnp.where(values < 0, -coded, coded).astype(WIRE)


def decode(coded, centre):
    coded = coded.astype(F32)
    power = jnp.log2(jnp.abs(coded))
    fine = jnp.clip(power, -FINE * STEEP, FINE * STEEP)
    values = jnp.exp2(power * (1.0 / SLOPE) + fine * (1.0 / STEEP - 1.0 / SLOPE) + centre)
    return jnp.where(coded < 0, -values, values)


def dot(left, right):
    return jnp.dot(left, right, preferred_element_type=F32)


def dot_nt(left, right):
    return lax.dot_general(left, right, (((1,), (1,)), ((), ())), preferred_element_type=F32)


def dot3(product, left, right):
    return product(left[0], right[0]) + product(left[0], right[1]) + product(left[1], right[0])


def closure(corr, solute_pot):
    excess = corr - solute_pot.astype(F32)
    low = jnp.minimum(excess, 0.0)
    series = jnp.full_like(low, 1.0 / 362880.0)
    for denominator in (40320.0, 5040.0, 720.0, 120.0, 24.0, 6.0, 2.0, 1.0):
        series = series * low + 1.0 / denominator
    grown = jnp.where(low > -0.5, series * low, jnp.exp(low) - 1.0)
    return jnp.where(excess > 0, excess, grown) - corr


def field_kernel(
    corr_ref, pot_ref, chi_ref, charge_ref, xh_ref, xl_ref, ch_ref, cl_ref, sh_ref, sl_ref,
    corr_out, potential_out,
    chi0, chi1, s1, b1, s2, b2, ys, s3, b3, s4, b4,
    chi_sem, send1, recv1, send2, recv2, send3, recv3, send4, recv4,
):
    px = lax.axis_index("px")
    py = lax.axis_index("py")
    barrier = pltpu.get_barrier_semaphore()

    def greet_px(step, carry):
        pl.semaphore_signal(barrier, inc=1, device_id=(lax.rem(px + step, PX), py), device_id_type=MESH)
        return carry

    def greet_py(step, carry):
        pl.semaphore_signal(barrier, inc=1, device_id=(px, lax.rem(py + step, PY)), device_id_type=MESH)
        return carry

    lax.fori_loop(1, PX, greet_px, 0)
    lax.fori_loop(1, PY, greet_py, 0)
    chi_copy0 = pltpu.make_async_copy(chi_ref.at[:, :, 0], chi0, chi_sem.at[0])
    chi_copy1 = pltpu.make_async_copy(chi_ref.at[:, :, 1, 0], chi1, chi_sem.at[1])
    chi_copy0.start()
    chi_copy1.start()

    lane = lax.broadcasted_iota(jnp.int32, (1, 128), 1)
    lane_re = lane < 64
    lane_field = lax.rem(lane // R, FIELDS)
    lane_spec = (lax.rem(lane, R) == 0) & (py == 0)

    lane_site = jnp.concatenate([lane_field, lane_field], axis=1)

    def x_forward(yp, carry):
        parts = []
        for site in range(SITES):
            rows = closure(corr_ref[site, pl.ds(2 * yp, 2)], pot_ref[site, pl.ds(2 * yp, 2)])
            parts.append(rows.reshape(64, N))
        data = split(jnp.concatenate(parts, axis=0))
        for pair in range(PY // 2):
            wide = dot3(dot, data, (xh_ref[:, 256 * pair:256 * pair + 256], xl_ref[:, 256 * pair:256 * pair + 256]))
            rows = jnp.where(lane_site == 0, wide[0:64], jnp.where(lane_site == 1, wide[64:128], wide[128:192]))
            rows = encode(jnp.where(lane_site == 3, 0.0, rows), CENTRE_X)
            s1[2 * pair, pl.ds(2 * yp, 2)] = rows[:, 0:128].reshape(2, 32, 128)
            s1[2 * pair + 1, pl.ds(2 * yp, 2)] = rows[:, 128:256].reshape(2, 32, 128)

        @pl.when(yp == 0)
        def _():
            pl.semaphore_wait(barrier, PX + PY - 2)

        pltpu.make_async_copy(
            s1.at[py, pl.ds(2 * yp, 2)], b1.at[pl.ds(2 * yp, 2), pl.ds(32 * py, 32)], recv1.at[yp]
        ).start()

        def send(step, inner):
            other = lax.rem(py + step, PY)
            pltpu.make_async_remote_copy(
                src_ref=s1.at[other, pl.ds(2 * yp, 2)],
                dst_ref=b1.at[pl.ds(2 * yp, 2), pl.ds(32 * py, 32)],
                send_sem=send1.at[yp], recv_sem=recv1.at[yp],
                device_id=(px, other), device_id_type=MESH,
            ).start()
            return inner

        return lax.fori_loop(1, PY, send, carry)

    lax.fori_loop(0, 4, x_forward, 0)

    cos = (ch_ref[...], cl_ref[...])
    sin = (sh_ref[...], sl_ref[...])
    wave = lax.broadcasted_iota(jnp.int32, (N, 1), 0)
    wave_edge = (wave == 0) | (wave == N // 2)
    wave_low = wave < N // 2
    wave_high = wave > N // 2

    def z_forward(yp, carry):
        chunk = b1.at[pl.ds(2 * yp, 2)]
        pltpu.make_async_copy(chunk, chunk, recv1.at[yp]).wait()
        data = split(jnp.concatenate([decode(b1[2 * yp + u], CENTRE_X) for u in range(2)], axis=1))
        cos_data = dot3(dot, cos, data)
        sin_data = dot3(dot, sin, data)
        halves = []
        for u in range(2):
            cd = cos_data[:, 128 * u:128 * u + 128]
            sd = sin_data[:, 128 * u:128 * u + 128]
            cd_turn = pltpu.roll(cd, 64, 1)
            sd_turn = pltpu.roll(sd, 64, 1)
            usual = jnp.where(lane_re, cd + sd_turn, cd - sd_turn)
            packed_re = jnp.where(wave_high, cd_turn, cd)
            packed_im = jnp.where(wave_edge, cd, jnp.where(wave_low, -sd_turn, -sd))
            packed = jnp.where(lane_re, packed_re, packed_im)
            halves.append(jnp.where(lane_spec, packed, usual).reshape(PX, 8, 128))
        s2[:, yp] = encode(jnp.concatenate(halves, axis=1), CENTRE_Z)
        pltpu.make_async_copy(s2.at[px, yp], b2.at[px, yp], recv2.at[yp]).start()

        def send(step, inner):
            other = lax.rem(px + step, PX)
            pltpu.make_async_remote_copy(
                src_ref=s2.at[other, yp], dst_ref=b2.at[px, yp],
                send_sem=send2.at[yp], recv_sem=recv2.at[yp],
                device_id=(other, py), device_id_type=MESH,
            ).start()
            return inner

        return lax.fori_loop(1, PX, send, carry)

    lax.fori_loop(0, 4, z_forward, 0)

    def collect(buffer, sem, centre):
        def body(part, carry):
            chunk = buffer.at[:, part]
            pltpu.make_async_copy(chunk, chunk, sem.at[part]).wait()

            def place(source, inner):
                start = pl.multiple_of(source * 64 + part * 16, 16)
                ys[pl.ds(start, 16), :] = decode(buffer[source, part], centre)
                return inner

            return lax.fori_loop(0, PX, place, carry)

        lax.fori_loop(0, 4, body, 0)

    collect(b2, recv2, CENTRE_Z)
    chi_copy0.wait()
    chi_copy1.wait()

    row = lax.broadcasted_iota(jnp.int32, (R, 1), 0)
    first = (row == 0) & (py == 0)
    wave_y = lax.broadcasted_iota(jnp.int32, (1, N), 1)
    unit = 2.0 * np.pi / N

    def signed_square(index):
        shifted = (lax.rem(index + N // 2, N) - N // 2).astype(F32) * unit
        return shifted * shifted

    square_y = signed_square(wave_y)
    scale = jnp.where(first, 2.0 ** -24, 2.0 ** -23)

    def mix(chi_of, x_re, x_im, screened):
        out_re, out_im = [], []
        pot_re = pot_im = 0.0
        for a in range(SITES):
            t_re = t_im = 0.0
            for b in range(SITES):
                factor = chi_of(a, b)
                t_re = t_re + factor * x_re[b]
                t_im = t_im + factor * x_im[b]
            out_re.append((t_re - x_re[a]) * scale)
            out_im.append((t_im - x_im[a]) * scale)
            pot_re = pot_re + charge_ref[a] * t_re
            pot_im = pot_im + charge_ref[a] * t_im
        out_re.append(pot_re * (screened * scale))
        out_im.append(pot_im * (screened * scale))
        return out_re, out_im

    def y_both(kp, carry):
        plain, turned = [], []
        rows = jnp.concatenate(
            [ys[pl.ds(2 * kp + u, N, stride=8), :].T for u in range(2)], axis=0
        )
        data = split(rows)
        cos_data = dot3(dot, data, cos)
        sin_data = dot3(dot, data, sin)
        for u in range(2):
            kz = 2 * kp + u
            kz_all = px * 8 + kz
            base = 128 * u
            pick = lambda array, c, s: array[base + 64 * c + 16 * s:base + 64 * c + 16 * s + 16]
            c_re = [pick(cos_data, 0, s) for s in range(SITES)]
            c_im = [pick(cos_data, 1, s) for s in range(SITES)]
            s_re = [pick(sin_data, 0, s) for s in range(SITES)]
            s_im = [pick(sin_data, 1, s) for s in range(SITES)]
            x_re = [c_re[s] + s_im[s] for s in range(SITES)]
            x_im = [c_im[s] - s_re[s] for s in range(SITES)]
            upper = first & (kz_all > N // 2)
            kx = jnp.where(upper, N // 2, py * R + row)
            square_z = signed_square(jnp.full((1, 1), kz_all, jnp.int32))
            rest = square_z + square_y + 1.0
            screened = (4.0 * np.pi) / (signed_square(kx) + rest)
            chi_of = lambda a, b: jnp.where(upper, chi1[a, b, pl.ds(kz, 1), :], chi0[a, b, :, kz, :])
            if u == 0:
                edge = first & ((kz_all == 0) | (kz_all == N // 2))
                b_re = [c_im[s] for s in range(SITES)]
                b_im = [-s_im[s] for s in range(SITES)]
                x_re = [jnp.where(edge, c_re[s], x_re[s]) for s in range(SITES)]
                x_im = [jnp.where(edge, -s_re[s], x_im[s]) for s in range(SITES)]
                f_re, f_im = mix(chi_of, x_re, x_im, screened)
                screened = (4.0 * np.pi) / (np.pi ** 2 + rest)
                g_re, g_im = mix(lambda a, b: chi1[a, b, pl.ds(kz, 1), :], b_re, b_im, screened)
                plain += f_re + [jnp.where(edge, g_re[f], f_im[f]) for f in range(FIELDS)]
                turned += [-value for value in f_im]
                turned += [jnp.where(edge, -g_im[f], f_re[f]) for f in range(FIELDS)]
            else:
                f_re, f_im = mix(chi_of, x_re, x_im, screened)
                plain += f_re + f_im
                turned += [-value for value in f_im] + f_re
        plain = split(jnp.concatenate(plain, axis=0))
        turned = split(jnp.concatenate(turned, axis=0))
        back = dot3(dot_nt, cos, plain) + dot3(dot_nt, sin, turned)
        s3[:, kp] = encode(
            jnp.concatenate([back[:, 128 * u:128 * u + 128].reshape(PX, 8, 128) for u in range(2)], axis=1),
            CENTRE_Y,
        )
        pltpu.make_async_copy(s3.at[px, kp], b3.at[px, kp], recv3.at[kp]).start()

        def send(step, inner):
            other = lax.rem(px + step, PX)
            pltpu.make_async_remote_copy(
                src_ref=s3.at[other, kp], dst_ref=b3.at[px, kp],
                send_sem=send3.at[kp], recv_sem=recv3.at[kp],
                device_id=(other, py), device_id_type=MESH,
            ).start()
            return inner

        return lax.fori_loop(1, PX, send, carry)

    lax.fori_loop(0, 4, y_both, 0)

    collect(b3, recv3, CENTRE_Y)

    def z_backward(yp, carry):
        plain, turned = [], []
        for u in range(2):
            data = ys[pl.ds(2 * yp + u, N, stride=8), :]
            turn = pltpu.roll(data, 64, 1)
            packed_re = jnp.where(wave_edge, data, jnp.where(wave_low, data + data, 0.0))
            packed_im = jnp.where(wave_edge, data, jnp.where(wave_low, 0.0, turn + turn))
            other_re = jnp.where(wave_low & ~wave_edge, -2.0 * turn, 0.0)
            other_im = jnp.where(wave_high, -2.0 * data, 0.0)
            plain.append(jnp.where(lane_spec, jnp.where(lane_re, packed_re, packed_im), data))
            turned.append(jnp.where(
                lane_spec, jnp.where(lane_re, other_re, other_im), jnp.where(lane_re, -turn, turn)
            ))
        plain = split(jnp.concatenate(plain, axis=1))
        turned = split(jnp.concatenate(turned, axis=1))
        back = encode(dot3(dot, cos, plain) + dot3(dot, sin, turned), CENTRE_BACK)
        s4[2 * yp] = back[:, 0:128]
        s4[2 * yp + 1] = back[:, 128:256]
        pltpu.make_async_copy(
            s4.at[pl.ds(2 * yp, 2), pl.ds(32 * py, 32)], b4.at[py, pl.ds(2 * yp, 2)], recv4.at[yp]
        ).start()

        def send(step, inner):
            other = lax.rem(py + step, PY)
            pltpu.make_async_remote_copy(
                src_ref=s4.at[pl.ds(2 * yp, 2), pl.ds(32 * other, 32)],
                dst_ref=b4.at[py, pl.ds(2 * yp, 2)],
                send_sem=send4.at[yp], recv_sem=recv4.at[yp],
                device_id=(px, other), device_id_type=MESH,
            ).start()
            return inner

        return lax.fori_loop(1, PY, send, carry)

    lax.fori_loop(0, 4, z_backward, 0)

    def x_backward(yp, carry):
        chunk = b4.at[:, pl.ds(2 * yp, 2)]
        pltpu.make_async_copy(chunk, chunk, recv4.at[yp]).wait()
        rows = jnp.concatenate(
            [decode(b4[j, pl.ds(2 * yp, 2)], CENTRE_BACK).reshape(64, 128) for j in range(PY)], axis=1
        )
        field = jnp.concatenate([lane_field] * PY, axis=1)
        data = split(jnp.concatenate([jnp.where(field == f, rows, 0.0) for f in range(FIELDS)], axis=0))
        back = dot3(dot_nt, data, (xh_ref[...], xl_ref[...]))
        for f in range(SITES):
            corr_out[f, pl.ds(2 * yp, 2)] = back[64 * f:64 * f + 64].reshape(2, 32, N)
        potential_out[pl.ds(2 * yp, 2)] = back[192:256].reshape(2, 32, N)
        return carry

    lax.fori_loop(0, 4, x_backward, 0)

    for part in range(4):
        sent = s1.at[pl.ds(0, PY - 1), pl.ds(0, 2)]
        pltpu.make_async_copy(sent, sent, send1.at[part]).wait()
        sent = s2.at[pl.ds(0, PX - 1), 0]
        pltpu.make_async_copy(sent, sent, send2.at[part]).wait()
        pltpu.make_async_copy(sent, sent, send3.at[part]).wait()
        sent = s4.at[pl.ds(0, 2), pl.ds(0, 32 * (PY - 1))]
        pltpu.make_async_copy(sent, sent, send4.at[part]).wait()


def fields(corr, solute_pot, chi, site_charge):
    vmem = pl.BlockSpec(memory_space=pltpu.VMEM)
    dma = pltpu.SemaphoreType.DMA((4,))
    return pl.pallas_call(
        field_kernel,
        name="fields",
        out_shape=(
            jax.ShapeDtypeStruct((SITES, 8, 32, N), F32),
            jax.ShapeDtypeStruct((8, 32, N), F32),
        ),
        in_specs=[vmem, vmem, pl.BlockSpec(memory_space=pl.ANY), pl.BlockSpec(memory_space=pltpu.SMEM)] + [vmem] * 6,
        out_specs=(vmem, vmem),
        scratch_shapes=[
            pltpu.VMEM((SITES, SITES, R, 8, N), F32),
            pltpu.VMEM((SITES, SITES, 8, N), F32),
            pltpu.VMEM((PY, 8, 32, 128), WIRE),
            pltpu.VMEM((8, N, 128), WIRE),
            pltpu.VMEM((PX, 4, 16, 128), WIRE),
            pltpu.VMEM((PX, 4, 16, 128), WIRE),
            pltpu.VMEM((PX * 64, 128), F32),
            pltpu.VMEM((PX, 4, 16, 128), WIRE),
            pltpu.VMEM((PX, 4, 16, 128), WIRE),
            pltpu.VMEM((8, N, 128), WIRE),
            pltpu.VMEM((PY, 8, 32, 128), WIRE),
            pltpu.SemaphoreType.DMA((2,)),
        ] + [dma] * 8,
        compiler_params=pltpu.CompilerParams(
            collective_id=0, has_side_effects=True, vmem_limit_bytes=40 * 2**20
        ),
    )(corr, solute_pot, chi, site_charge, *[jnp.asarray(table) for table in tables()])


def shards(
    corr, solute_pot, chi, site_charge, home_slab, brick_index, block_slot, basis_values, fock_in
):
    home = home_slab[:, 0]
    frags = home.shape[0]
    same = home[:, None] == home[None, :]
    earlier = jnp.arange(frags)[None, :] < jnp.arange(frags)[:, None]
    place = jnp.sum((same & earlier).astype(jnp.int32), axis=1)
    wanted = home * MOST + place
    asked = jnp.zeros((PX * MOST,), jnp.int32).at[wanted].set(brick_index)
    asked = lax.all_to_all(asked, "px", split_axis=0, concat_axis=0, tiled=True)

    corr_next, potential = fields(corr, solute_pot, chi, site_charge)

    bricks = potential.astype(BF16).reshape(1, BRICK, 4, BRICK, 32, BRICK)
    bricks = bricks.transpose(0, 2, 4, 1, 3, 5).reshape(128, 512)
    answer = jnp.take(bricks, asked, axis=0, mode="clip")
    answer = lax.all_to_all(answer, "px", split_axis=0, concat_axis=0, tiled=True)
    sampled = jnp.take(answer, wanted, axis=0, mode="clip")
    weighted = (basis_values.astype(F32) * sampled.astype(F32)[:, :, None]).astype(BF16)
    embed = jnp.einsum("fcb,fcd->fbd", basis_values, weighted, preferred_element_type=F32)
    fock_out = fock_in.at[block_slot[0]].add(embed)
    return (corr_next, potential, fock_out)


def solution(mesh):
    return jax.shard_map(
        shards,
        mesh=mesh,
        in_specs=(
            P(None, "px", "py", None),
            P(None, "px", "py", None),
            P(None, None, None, "py", "px", None),
            P(),
            P(("px", "py"), None),
            P(("px", "py")),
            P(("px", "py"), None),
            P(("px", "py"), None, None),
            P(("px", "py"), None, None),
        ),
        out_specs=(P(None, "px", "py", None), P("px", "py", None), P(("px", "py"), None, None)),
        check_vma=False,
    )
```

```python
import functools
import jax
import jax.numpy as jnp
import numpy as np
from jax import lax
from jax.experimental import pallas as pl
from jax.experimental.pallas import tpu as pltpu
from jax.sharding import PartitionSpec as P

BRICK = 8
MOST = 4
N = 256
PX = 32
PY = 8
SITES = 3
FIELDS = 4
R = 16
MESH = pl.DeviceIdType.MESH
F32 = jnp.float32
BF16 = jnp.bfloat16
WIRE = jnp.bfloat16
FINE, STEEP, SLOPE = 11.0, 8.0, 3.0
CENTRE_X, CENTRE_Z, CENTRE_Y, CENTRE_BACK = 5.0, 9.0, -5.0, -1.0


def split(values):
    high = values.astype(BF16)
    return high, (values - high.astype(F32)).astype(BF16)


def np_split(values):
    high = values.astype(np.float32).astype(BF16)
    low = (values - high.astype(np.float64)).astype(np.float32).astype(BF16)
    return high, low


def tables():
    index = np.arange(N)
    angle = (index[:, None] * index[None, :] % N) * (2.0 * np.pi / N)
    cos, sin = np.cos(angle), np.sin(angle)
    half_re = cos[:, : N // 2].copy()
    half_im = -sin[:, : N // 2]
    half_im[:, 0] = cos[:, N // 2]
    halves = np.stack([half_re.reshape(N, PY, R), half_im.reshape(N, PY, R)], axis=2)
    spread = np.broadcast_to(halves[:, :, :, None, :], (N, PY, 2, FIELDS, R))
    spread = spread.reshape(N, PY * 128)
    return np_split(spread) + np_split(cos) + np_split(sin)


def encode(values, centre):
    power = jnp.log2(jnp.abs(values)) - centre
    power = SLOPE * power + (STEEP - SLOPE) * jnp.clip(power, -FINE, FINE)
    coded = jnp.exp2(power)
    return jnp.where(values < 0, -coded, coded).astype(WIRE)


def decode(coded, centre):
    coded = coded.astype(F32)
    power = jnp.log2(jnp.abs(coded))
    fine = jnp.clip(power, -FINE * STEEP, FINE * STEEP)
    values = jnp.exp2(power * (1.0 / SLOPE) + fine * (1.0 / STEEP - 1.0 / SLOPE) + centre)
    return jnp.where(coded < 0, -values, values)


def dot(left, right):
    return jnp.dot(left, right, preferred_element_type=F32)


def dot_nt(left, right):
    return lax.dot_general(left, right, (((1,), (1,)), ((), ())), preferred_element_type=F32)


def dot3(product, left, right):
    return product(left[0], right[0]) + product(left[0], right[1]) + product(left[1], right[0])


def closure(corr, solute_pot):
    excess = corr - solute_pot.astype(F32)
    low = jnp.minimum(excess, 0.0)
    series = jnp.full_like(low, 1.0 / 362880.0)
    for denominator in (40320.0, 5040.0, 720.0, 120.0, 24.0, 6.0, 2.0, 1.0):
        series = series * low + 1.0 / denominator
    grown = jnp.where(low > -0.5, series * low, jnp.exp(low) - 1.0)
    return jnp.where(excess > 0, excess, grown) - corr


def field_kernel(
    charge_ref, corr_hbm, solute_hbm, chi_hbm, home_hbm, brick_hbm, slot_hbm, basis_hbm, fock_hbm,
    xh_hbm, xl_hbm, ch_hbm, cl_hbm, sh_hbm, sl_hbm,
    corr_out, potential_out, fock_out,
    corr_ref, solute_ref, chi0, chi1, home_ref, brick_ref, slot_ref, basis_ref, fock_ref,
    xh_ref, xl_ref, ch_ref, cl_ref, sh_ref, sl_ref,
    s1, b1, s2, b2, ys, s3, b3, s4, b4,
    ask_out, ask_in, ask_smem, info, info_smem, pot_ref, shuffled, brick_out, brick_in, turned_basis, tiles, samples,
    in_sem, send1, recv1, send2, recv2, send3, recv3, send4, recv4, brick_sem,
):
    px = lax.axis_index("px")
    py = lax.axis_index("py")
    barrier = pltpu.get_barrier_semaphore()

    def greet_px(step, carry):
        pl.semaphore_signal(barrier, inc=1, device_id=(lax.rem(px + step, PX), py), device_id_type=MESH)
        return carry

    def greet_py(step, carry):
        pl.semaphore_signal(barrier, inc=1, device_id=(px, lax.rem(py + step, PY)), device_id_type=MESH)
        return carry

    pairs = (
        (corr_hbm, corr_ref), (solute_hbm, solute_ref), (xh_hbm, xh_ref), (xl_hbm, xl_ref),
        (ch_hbm, ch_ref), (cl_hbm, cl_ref), (sh_hbm, sh_ref), (sl_hbm, sl_ref),
        (home_hbm, home_ref), (brick_hbm, brick_ref), (slot_hbm, slot_ref),
        (chi_hbm.at[:, :, 0], chi0), (chi_hbm.at[:, :, 1, 0], chi1),
        (basis_hbm, basis_ref), (fock_hbm, fock_ref),
    )
    loads = [pltpu.make_async_copy(source, to, in_sem.at[i]) for i, (source, to) in enumerate(pairs)]
    for load in loads[:11]:
        load.start()
    lax.fori_loop(1, PX, greet_px, 0)
    lax.fori_loop(1, PY, greet_py, 0)
    for load in loads[11:]:
        load.start()
    for load in loads[:4]:
        load.wait()

    lane = lax.broadcasted_iota(jnp.int32, (1, 128), 1)
    lane_re = lane < 64
    lane_field = lax.rem(lane // R, FIELDS)
    lane_spec = (lax.rem(lane, R) == 0) & (py == 0)

    lane_site = jnp.concatenate([lane_field, lane_field], axis=1)

    def x_forward(yp, carry):
        parts = []
        for site in range(SITES):
            rows = closure(corr_ref[site, pl.ds(2 * yp, 2)], solute_ref[site, pl.ds(2 * yp, 2)])
            parts.append(rows.reshape(64, N))
        data = split(jnp.concatenate(parts, axis=0))
        for pair in range(PY // 2):
            wide = dot3(dot, data, (xh_ref[:, 256 * pair:256 * pair + 256], xl_ref[:, 256 * pair:256 * pair + 256]))
            rows = jnp.where(lane_site == 0, wide[0:64], jnp.where(lane_site == 1, wide[64:128], wide[128:192]))
            rows = encode(jnp.where(lane_site == 3, 0.0, rows), CENTRE_X)
            s1[2 * pair, pl.ds(2 * yp, 2)] = rows[:, 0:128].reshape(2, 32, 128)
            s1[2 * pair + 1, pl.ds(2 * yp, 2)] = rows[:, 128:256].reshape(2, 32, 128)

        @pl.when(yp == 0)
        def _():
            pl.semaphore_wait(barrier, PX + PY - 2)

        pltpu.make_async_copy(
            s1.at[py, pl.ds(2 * yp, 2)], b1.at[pl.ds(2 * yp, 2), pl.ds(32 * py, 32)], recv1.at[yp]
        ).start()

        def send(step, inner):
            other = lax.rem(py + step, PY)
            pltpu.make_async_remote_copy(
                src_ref=s1.at[other, pl.ds(2 * yp, 2)],
                dst_ref=b1.at[pl.ds(2 * yp, 2), pl.ds(32 * py, 32)],
                send_sem=send1.at[yp], recv_sem=recv1.at[yp],
                device_id=(px, other), device_id_type=MESH,
            ).start()
            return inner

        return lax.fori_loop(1, PY, send, carry)

    lax.fori_loop(0, 4, x_forward, 0)

    for load in loads[8:11]:
        load.wait()
    home = home_ref[...]
    brick = brick_ref[...]
    down = lax.broadcasted_iota(jnp.int32, (32, 32), 0)
    across = lax.broadcasted_iota(jnp.int32, (32, 32), 1)
    home_down = jnp.sum(jnp.where(down == across, home, 0), axis=1, keepdims=True)
    place = jnp.sum(jnp.where((home_down == home) & (down < across), 1, 0), axis=0, keepdims=True)
    wide_lane = lax.broadcasted_iota(jnp.int32, (32, 128), 1)
    asked = jnp.zeros((32, 128), jnp.int32)
    for k in range(MOST):
        found = jnp.sum(jnp.where((home == down) & (place == k), brick, 0), axis=1, keepdims=True)
        asked = jnp.where(wide_lane == k, jnp.clip(found, 0, 127), asked)
    for other in range(PX):
        ask_out[other] = asked[other:other + 1]
    table = jnp.zeros((32, 128), jnp.int32)
    for k, (value, most) in enumerate(((across, 31), (home, PX - 1), (place, MOST - 1))):
        found = jnp.sum(jnp.where(slot_ref[...] == down, value, 0), axis=1, keepdims=True)
        table = jnp.where(wide_lane == k, jnp.clip(found, 0, most), table)
    info[...] = table
    info_copy = pltpu.make_async_copy(info, info_smem, brick_sem.at[0])
    info_copy.start()
    pltpu.make_async_copy(ask_out.at[px], ask_in.at[px], brick_sem.at[2]).start()

    def ask(step, carry):
        other = lax.rem(px + step, PX)
        pltpu.make_async_remote_copy(
            src_ref=ask_out.at[other], dst_ref=ask_in.at[px],
            send_sem=brick_sem.at[1], recv_sem=brick_sem.at[2],
            device_id=(other, py), device_id_type=MESH,
        ).start()
        return carry

    lax.fori_loop(1, PX, ask, 0)
    for load in loads[4:8]:
        load.wait()
    loads[13].wait()

    cos = (ch_ref[...], cl_ref[...])
    sin = (sh_ref[...], sl_ref[...])
    wave = lax.broadcasted_iota(jnp.int32, (N, 1), 0)
    wave_edge = (wave == 0) | (wave == N // 2)
    wave_low = wave < N // 2
    wave_high = wave > N // 2

    def z_forward(yp, carry):
        def turn_basis(item, inner):
            turned_basis[8 * yp + item] = basis_ref[8 * yp + item].T
            return inner

        lax.fori_loop(0, 8, turn_basis, 0)
        chunk = b1.at[pl.ds(2 * yp, 2)]
        pltpu.make_async_copy(chunk, chunk, recv1.at[yp]).wait()
        data = split(jnp.concatenate([decode(b1[2 * yp + u], CENTRE_X) for u in range(2)], axis=1))
        cos_data = dot3(dot, cos, data)
        sin_data = dot3(dot, sin, data)
        halves = []
        for u in range(2):
            cd = cos_data[:, 128 * u:128 * u + 128]
            sd = sin_data[:, 128 * u:128 * u + 128]
            cd_turn = pltpu.roll(cd, 64, 1)
            sd_turn = pltpu.roll(sd, 64, 1)
            usual = jnp.where(lane_re, cd + sd_turn, cd - sd_turn)
            packed_re = jnp.where(wave_high, cd_turn, cd)
            packed_im = jnp.where(wave_edge, cd, jnp.where(wave_low, -sd_turn, -sd))
            packed = jnp.where(lane_re, packed_re, packed_im)
            halves.append(jnp.where(lane_spec, packed, usual).reshape(PX, 8, 128))
        s2[:, yp] = encode(jnp.concatenate(halves, axis=1), CENTRE_Z)
        pltpu.make_async_copy(s2.at[px, yp], b2.at[px, yp], recv2.at[yp]).start()

        def send(step, inner):
            other = lax.rem(px + step, PX)
            pltpu.make_async_remote_copy(
                src_ref=s2.at[other, yp], dst_ref=b2.at[px, yp],
                send_sem=send2.at[yp], recv_sem=recv2.at[yp],
                device_id=(other, py), device_id_type=MESH,
            ).start()
            return inner

        return lax.fori_loop(1, PX, send, carry)

    lax.fori_loop(0, 4, z_forward, 0)

    def collect(buffer, sem, centre):
        def body(part, carry):
            chunk = buffer.at[:, part]
            pltpu.make_async_copy(chunk, chunk, sem.at[part]).wait()

            def place(source, inner):
                start = pl.multiple_of(source * 64 + part * 16, 16)
                ys[pl.ds(start, 16), :] = decode(buffer[source, part], centre)
                return inner

            return lax.fori_loop(0, PX, place, carry)

        lax.fori_loop(0, 4, body, 0)

    collect(b2, recv2, CENTRE_Z)
    loads[11].wait()
    loads[12].wait()

    row = lax.broadcasted_iota(jnp.int32, (R, 1), 0)
    first = (row == 0) & (py == 0)
    wave_y = lax.broadcasted_iota(jnp.int32, (1, N), 1)
    unit = 2.0 * np.pi / N

    def signed_square(index):
        shifted = (lax.rem(index + N // 2, N) - N // 2).astype(F32) * unit
        return shifted * shifted

    square_y = signed_square(wave_y)
    scale = jnp.where(first, 2.0 ** -24, 2.0 ** -23)

    def mix(chi_of, x_re, x_im, screened):
        out_re, out_im = [], []
        pot_re = pot_im = 0.0
        for a in range(SITES):
            t_re = t_im = 0.0
            for b in range(SITES):
                factor = chi_of(a, b)
                t_re = t_re + factor * x_re[b]
                t_im = t_im + factor * x_im[b]
            out_re.append((t_re - x_re[a]) * scale)
            out_im.append((t_im - x_im[a]) * scale)
            pot_re = pot_re + charge_ref[a] * t_re
            pot_im = pot_im + charge_ref[a] * t_im
        out_re.append(pot_re * (screened * scale))
        out_im.append(pot_im * (screened * scale))
        return out_re, out_im

    def y_both(kp, carry):
        plain, turned = [], []
        rows = jnp.concatenate(
            [ys[pl.ds(2 * kp + u, N, stride=8), :].T for u in range(2)], axis=0
        )
        data = split(rows)
        cos_data = dot3(dot, data, cos)
        sin_data = dot3(dot, data, sin)
        for u in range(2):
            kz = 2 * kp + u
            kz_all = px * 8 + kz
            base = 128 * u
            pick = lambda array, c, s: array[base + 64 * c + 16 * s:base + 64 * c + 16 * s + 16]
            c_re = [pick(cos_data, 0, s) for s in range(SITES)]
            c_im = [pick(cos_data, 1, s) for s in range(SITES)]
            s_re = [pick(sin_data, 0, s) for s in range(SITES)]
            s_im = [pick(sin_data, 1, s) for s in range(SITES)]
            x_re = [c_re[s] + s_im[s] for s in range(SITES)]
            x_im = [c_im[s] - s_re[s] for s in range(SITES)]
            upper = first & (kz_all > N // 2)
            kx = jnp.where(upper, N // 2, py * R + row)
            square_z = signed_square(jnp.full((1, 1), kz_all, jnp.int32))
            rest = square_z + square_y + 1.0
            screened = (4.0 * np.pi) / (signed_square(kx) + rest)
            chi_of = lambda a, b: jnp.where(upper, chi1[a, b, pl.ds(kz, 1), :], chi0[a, b, :, kz, :])
            if u == 0:
                edge = first & ((kz_all == 0) | (kz_all == N // 2))
                b_re = [c_im[s] for s in range(SITES)]
                b_im = [-s_im[s] for s in range(SITES)]
                x_re = [jnp.where(edge, c_re[s], x_re[s]) for s in range(SITES)]
                x_im = [jnp.where(edge, -s_re[s], x_im[s]) for s in range(SITES)]
                f_re, f_im = mix(chi_of, x_re, x_im, screened)
                screened = (4.0 * np.pi) / (np.pi ** 2 + rest)
                g_re, g_im = mix(lambda a, b: chi1[a, b, pl.ds(kz, 1), :], b_re, b_im, screened)
                plain += f_re + [jnp.where(edge, g_re[f], f_im[f]) for f in range(FIELDS)]
                turned += [-value for value in f_im]
                turned += [jnp.where(edge, -g_im[f], f_re[f]) for f in range(FIELDS)]
            else:
                f_re, f_im = mix(chi_of, x_re, x_im, screened)
                plain += f_re + f_im
                turned += [-value for value in f_im] + f_re
        plain = split(jnp.concatenate(plain, axis=0))
        turned = split(jnp.concatenate(turned, axis=0))
        back = dot3(dot_nt, cos, plain) + dot3(dot_nt, sin, turned)
        s3[:, kp] = encode(
            jnp.concatenate([back[:, 128 * u:128 * u + 128].reshape(PX, 8, 128) for u in range(2)], axis=1),
            CENTRE_Y,
        )
        pltpu.make_async_copy(s3.at[px, kp], b3.at[px, kp], recv3.at[kp]).start()

        def send(step, inner):
            other = lax.rem(px + step, PX)
            pltpu.make_async_remote_copy(
                src_ref=s3.at[other, kp], dst_ref=b3.at[px, kp],
                send_sem=send3.at[kp], recv_sem=recv3.at[kp],
                device_id=(other, py), device_id_type=MESH,
            ).start()
            return inner

        return lax.fori_loop(1, PX, send, carry)

    lax.fori_loop(0, 4, y_both, 0)

    collect(b3, recv3, CENTRE_Y)

    def z_backward(yp, carry):
        plain, turned = [], []
        for u in range(2):
            data = ys[pl.ds(2 * yp + u, N, stride=8), :]
            turn = pltpu.roll(data, 64, 1)
            packed_re = jnp.where(wave_edge, data, jnp.where(wave_low, data + data, 0.0))
            packed_im = jnp.where(wave_edge, data, jnp.where(wave_low, 0.0, turn + turn))
            other_re = jnp.where(wave_low & ~wave_edge, -2.0 * turn, 0.0)
            other_im = jnp.where(wave_high, -2.0 * data, 0.0)
            plain.append(jnp.where(lane_spec, jnp.where(lane_re, packed_re, packed_im), data))
            turned.append(jnp.where(
                lane_spec, jnp.where(lane_re, other_re, other_im), jnp.where(lane_re, -turn, turn)
            ))
        plain = split(jnp.concatenate(plain, axis=1))
        turned = split(jnp.concatenate(turned, axis=1))
        back = encode(dot3(dot, cos, plain) + dot3(dot, sin, turned), CENTRE_BACK)
        s4[2 * yp] = back[:, 0:128]
        s4[2 * yp + 1] = back[:, 128:256]
        pltpu.make_async_copy(
            s4.at[pl.ds(2 * yp, 2), pl.ds(32 * py, 32)], b4.at[py, pl.ds(2 * yp, 2)], recv4.at[yp]
        ).start()

        def send(step, inner):
            other = lax.rem(py + step, PY)
            pltpu.make_async_remote_copy(
                src_ref=s4.at[pl.ds(2 * yp, 2), pl.ds(32 * other, 32)],
                dst_ref=b4.at[py, pl.ds(2 * yp, 2)],
                send_sem=send4.at[yp], recv_sem=recv4.at[yp],
                device_id=(px, other), device_id_type=MESH,
            ).start()
            return inner

        return lax.fori_loop(1, PY, send, carry)

    lax.fori_loop(0, 4, z_backward, 0)

    def x_backward(yp, carry):
        chunk = b4.at[:, pl.ds(2 * yp, 2)]
        pltpu.make_async_copy(chunk, chunk, recv4.at[yp]).wait()
        rows = jnp.concatenate(
            [decode(b4[j, pl.ds(2 * yp, 2)], CENTRE_BACK).reshape(64, 128) for j in range(PY)], axis=1
        )
        field = jnp.concatenate([lane_field] * PY, axis=1)
        data = split(jnp.concatenate([jnp.where(field == f, rows, 0.0) for f in range(FIELDS)], axis=0))
        back = dot3(dot_nt, data, (xh_ref[...], xl_ref[...]))
        for f in range(SITES):
            corr_out[f, pl.ds(2 * yp, 2)] = back[64 * f:64 * f + 64].reshape(2, 32, N)
        potential = back[192:256].reshape(2, 32, N)
        potential_out[pl.ds(2 * yp, 2)] = potential
        pot_ref[0, pl.ds(2 * yp, 2)] = potential[:, :, 0:128]
        pot_ref[1, pl.ds(2 * yp, 2)] = potential[:, :, 128:256]
        return carry

    lax.fori_loop(0, 4, x_backward, 0)

    pltpu.make_async_copy(ask_in, ask_in, brick_sem.at[2]).wait()
    ask_copy = pltpu.make_async_copy(ask_in, ask_smem, brick_sem.at[3])
    ask_copy.start()
    lane_row = lane // 32

    def shuffle(bz, carry):
        for half in range(2):
            slabs = [pot_ref[half, y, pl.ds(8 * bz, 8), :] for y in range(8)]
            for quad in range(4):
                rows = []
                for u in range(2):
                    row = slabs[u]
                    if quad:
                        row = pltpu.roll(row, 128 - 32 * quad, 1)
                    for yg in range(1, 4):
                        move = 32 * ((yg - quad) % 4)
                        other = slabs[2 * yg + u]
                        other = pltpu.roll(other, move, 1) if move else other
                        row = jnp.where(lane_row == yg, other, row)
                    rows.append(row)
                shuffled[8 * bz + 4 * half + quad] = jnp.concatenate(rows, axis=0)
        return carry

    lax.fori_loop(0, 4, shuffle, 0)
    ask_copy.wait()
    lane_place = lax.rem(lane // BRICK, MOST)

    def answer(step, carry):
        other = lax.rem(px + step, PX)
        tile = jnp.zeros((16, 128), F32)
        for k in range(MOST):
            index = ask_smem[other, 0, k]
            moved = pltpu.roll(shuffled[index // 4], lax.rem(BRICK * (k - lax.rem(index, 4)) + 128, 128), 1)
            tile = jnp.where(lane_place == k, moved, tile)
        brick_out[other] = tile.astype(BF16)

        @pl.when(step > 0)
        def _():
            pltpu.make_async_remote_copy(
                src_ref=brick_out.at[other], dst_ref=brick_in.at[px],
                send_sem=brick_sem.at[4], recv_sem=brick_sem.at[5],
                device_id=(other, py), device_id_type=MESH,
            ).start()

        return carry

    lax.fori_loop(0, PX, answer, 0)
    pltpu.make_async_copy(brick_out.at[px], brick_in.at[px], brick_sem.at[5]).start()
    info_copy.wait()
    loads[14].wait()
    pltpu.make_async_copy(brick_in, brick_in, brick_sem.at[5]).wait()

    def take(slot, carry):
        tile = brick_in[info_smem[slot, 1]].astype(F32)
        tile = pltpu.roll(tile, lax.rem(128 - BRICK * info_smem[slot, 2], 128), 1)
        tiles[pl.ds(pl.multiple_of(16 * slot, 16), 16), :] = tile.astype(BF16)
        return carry

    lax.fori_loop(0, 32, take, 0)
    cell = lax.broadcasted_iota(jnp.int32, (128, 512), 1)
    origin = lax.broadcasted_iota(jnp.int32, (128, 512), 0)
    spread = (origin == 32 * (cell // 128) + lax.rem(cell, BRICK)).astype(F32).astype(BF16)
    wide = dot(tiles[...], spread)
    tile_row = lax.broadcasted_iota(jnp.int32, (512, 512), 0)
    tile_cell = lax.broadcasted_iota(jnp.int32, (512, 512), 1)
    wide = jnp.where(lax.rem(tile_row, 16) == lax.rem(tile_cell, 128) // BRICK, wide, 0.0).astype(BF16)
    slot_down = lax.broadcasted_iota(jnp.int32, (32, 512), 0)
    slot_cell = lax.broadcasted_iota(jnp.int32, (32, 512), 1)
    samples[...] = dot((slot_down == slot_cell // 16).astype(F32).astype(BF16), wide)

    def embed(slot, carry):
        basis = turned_basis[info_smem[slot, 0]]
        weighted = basis * samples[pl.ds(slot, 1), :].astype(BF16)
        fock_out[slot] = fock_ref[slot] + dot_nt(basis, weighted)
        return carry

    lax.fori_loop(0, 32, embed, 0)

    for part in range(4):
        sent = s1.at[pl.ds(0, PY - 1), pl.ds(0, 2)]
        pltpu.make_async_copy(sent, sent, send1.at[part]).wait()
        sent = s2.at[pl.ds(0, PX - 1), 0]
        pltpu.make_async_copy(sent, sent, send2.at[part]).wait()
        pltpu.make_async_copy(sent, sent, send3.at[part]).wait()
        sent = s4.at[pl.ds(0, 2), pl.ds(0, 32 * (PY - 1))]
        pltpu.make_async_copy(sent, sent, send4.at[part]).wait()
    sent = ask_out.at[pl.ds(0, PX - 1)]
    pltpu.make_async_copy(sent, sent, brick_sem.at[1]).wait()
    sent = brick_out.at[pl.ds(0, PX - 1)]
    pltpu.make_async_copy(sent, sent, brick_sem.at[4]).wait()


def shards(
    corr, solute_pot, chi, site_charge, home_slab, brick_index, block_slot, basis_values, fock_in
):
    vmem = pl.BlockSpec(memory_space=pltpu.VMEM)
    hbm = pl.BlockSpec(memory_space=pltpu.HBM)
    dma = pltpu.SemaphoreType.DMA((4,))
    frags = home_slab.shape[0]
    return pl.pallas_call(
        field_kernel,
        name="fields",
        out_shape=(
            jax.ShapeDtypeStruct((SITES, 8, 32, N), F32),
            jax.ShapeDtypeStruct((8, 32, N), F32),
            jax.ShapeDtypeStruct(fock_in.shape, F32),
        ),
        in_specs=[pl.BlockSpec(memory_space=pltpu.SMEM)] + [hbm] * 14,
        out_specs=(vmem,) * 3,
        scratch_shapes=[
            pltpu.VMEM(corr.shape, F32),
            pltpu.VMEM(solute_pot.shape, BF16),
            pltpu.VMEM((SITES, SITES, R, 8, N), F32),
            pltpu.VMEM((SITES, SITES, 8, N), F32),
            pltpu.VMEM((1, frags), jnp.int32),
            pltpu.VMEM((1, frags), jnp.int32),
            pltpu.VMEM((1, frags), jnp.int32),
            pltpu.VMEM(basis_values.shape, BF16),
            pltpu.VMEM(fock_in.shape, F32),
            pltpu.VMEM((N, PY * 128), BF16),
            pltpu.VMEM((N, PY * 128), BF16),
            pltpu.VMEM((N, N), BF16),
            pltpu.VMEM((N, N), BF16),
            pltpu.VMEM((N, N), BF16),
            pltpu.VMEM((N, N), BF16),
            pltpu.VMEM((PY, 8, 32, 128), WIRE),
            pltpu.VMEM((8, N, 128), WIRE),
            pltpu.VMEM((PX, 4, 16, 128), WIRE),
            pltpu.VMEM((PX, 4, 16, 128), WIRE),
            pltpu.VMEM((PX * 64, 128), F32),
            pltpu.VMEM((PX, 4, 16, 128), WIRE),
            pltpu.VMEM((PX, 4, 16, 128), WIRE),
            pltpu.VMEM((8, N, 128), WIRE),
            pltpu.VMEM((PY, 8, 32, 128), WIRE),
            pltpu.VMEM((PX, 1, 128), jnp.int32),
            pltpu.VMEM((PX, 1, 128), jnp.int32),
            pltpu.SMEM((PX, 1, 128), jnp.int32),
            pltpu.VMEM((frags, 128), jnp.int32),
            pltpu.SMEM((frags, 128), jnp.int32),
            pltpu.VMEM((2, 8, 32, 128), F32),
            pltpu.VMEM((32, 16, 128), F32),
            pltpu.VMEM((PX, 16, 128), BF16),
            pltpu.VMEM((PX, 16, 128), BF16),
            pltpu.VMEM((frags, 128, 512), BF16),
            pltpu.VMEM((frags * 16, 128), BF16),
            pltpu.VMEM((frags, 512), F32),
            pltpu.SemaphoreType.DMA((15,)),
        ] + [dma] * 8 + [pltpu.SemaphoreType.DMA((6,))],
        compiler_params=pltpu.CompilerParams(
            collective_id=0, has_side_effects=True, vmem_limit_bytes=48 * 2**20
        ),
    )(
        site_charge, corr, solute_pot, chi, home_slab.reshape(1, frags), brick_index.reshape(1, frags),
        block_slot, basis_values, fock_in, *[jnp.asarray(table) for table in tables()],
    )


def solution(mesh):
    return jax.shard_map(
        shards,
        mesh=mesh,
        in_specs=(
            P(None, "px", "py", None),
            P(None, "px", "py", None),
            P(None, None, None, "py", "px", None),
            P(),
            P(("px", "py"), None),
            P(("px", "py")),
            P(("px", "py"), None),
            P(("px", "py"), None, None),
            P(("px", "py"), None, None),
        ),
        out_specs=(P(None, "px", "py", None), P("px", "py", None), P(("px", "py"), None, None)),
        check_vma=False,
    )
```

```python
import functools
import jax
import jax.numpy as jnp
import numpy as np
from jax import lax
from jax.experimental import pallas as pl
from jax.experimental.pallas import tpu as pltpu
from jax.sharding import PartitionSpec as P

BRICK = 8
MOST = 4
N = 256
PX = 32
PY = 8
SITES = 3
FIELDS = 4
R = 16
MESH = pl.DeviceIdType.MESH
F32 = jnp.float32
BF16 = jnp.bfloat16
WIRE = jnp.bfloat16
FINE, STEEP, SLOPE = 11.0, 8.0, 3.0
CENTRE_X, CENTRE_Z, CENTRE_Y, CENTRE_BACK = 5.0, 9.0, -5.0, -1.0


def split(values):
    high = values.astype(BF16)
    return high, (values - high.astype(F32)).astype(BF16)


def np_split(values):
    high = values.astype(np.float32).astype(BF16)
    low = (values - high.astype(np.float64)).astype(np.float32).astype(BF16)
    return high, low


def tables():
    index = np.arange(N)
    angle = (index[:, None] * index[None, :] % N) * (2.0 * np.pi / N)
    cos, sin = np.cos(angle), np.sin(angle)
    half_re = cos[:, : N // 2].copy()
    half_im = -sin[:, : N // 2]
    half_im[:, 0] = cos[:, N // 2]
    halves = np.stack([half_re.reshape(N, PY, R), half_im.reshape(N, PY, R)], axis=2)
    spread = np.broadcast_to(halves[:, :, :, None, :], (N, PY, 2, FIELDS, R))
    spread = spread.reshape(N, PY * 128)
    return np_split(spread) + np_split(cos) + np_split(sin)


def encode(values, centre):
    power = jnp.log2(jnp.abs(values)) - centre
    power = SLOPE * power + (STEEP - SLOPE) * jnp.clip(power, -FINE, FINE)
    coded = jnp.exp2(power)
    return jnp.where(values < 0, -coded, coded).astype(WIRE)


def decode(coded, centre):
    coded = coded.astype(F32)
    power = jnp.log2(jnp.abs(coded))
    fine = jnp.clip(power, -FINE * STEEP, FINE * STEEP)
    values = jnp.exp2(power * (1.0 / SLOPE) + fine * (1.0 / STEEP - 1.0 / SLOPE) + centre)
    return jnp.where(coded < 0, -values, values)


def dot(left, right):
    return jnp.dot(left, right, preferred_element_type=F32)


def dot_nt(left, right):
    return lax.dot_general(left, right, (((1,), (1,)), ((), ())), preferred_element_type=F32)


def dot3(product, left, right):
    return product(left[0], right[0]) + product(left[0], right[1]) + product(left[1], right[0])


def closure(corr, solute_pot):
    excess = corr - solute_pot.astype(F32)
    low = jnp.minimum(excess, 0.0)
    series = jnp.full_like(low, 1.0 / 362880.0)
    for denominator in (40320.0, 5040.0, 720.0, 120.0, 24.0, 6.0, 2.0, 1.0):
        series = series * low + 1.0 / denominator
    grown = jnp.where(low > -0.5, series * low, jnp.exp(low) - 1.0)
    return jnp.where(excess > 0, excess, grown) - corr


def field_kernel(
    charge_ref, corr_hbm, solute_hbm, chi_hbm, home_hbm, brick_hbm, slot_hbm, basis_hbm, fock_hbm,
    xh_hbm, xl_hbm, ch_hbm, cl_hbm, sh_hbm, sl_hbm,
    corr_hbm_out, potential_hbm_out, fock_hbm_out,
    corr_out, potential_out, fock_out,
    corr_ref, solute_ref, chi0, chi1, home_ref, brick_ref, slot_ref, basis_ref, fock_ref,
    xh_ref, xl_ref, ch_ref, cl_ref, sh_ref, sl_ref,
    s1, b1, s2, b2, ys, s3, b3, s4, b4,
    ask_out, ask_in, ask_smem, info, info_smem, pot_ref, shuffled, brick_out, brick_in, turned_basis, tiles, samples,
    in_sem, send1, recv1, send2, recv2, send3, recv3, send4, recv4, brick_sem, corr_sem, potential_sem, fock_sem,
):
    px = lax.axis_index("px")
    py = lax.axis_index("py")
    barrier = pltpu.get_barrier_semaphore()

    def greet_px(step, carry):
        pl.semaphore_signal(barrier, inc=1, device_id=(lax.rem(px + step, PX), py), device_id_type=MESH)
        return carry

    def greet_py(step, carry):
        pl.semaphore_signal(barrier, inc=1, device_id=(px, lax.rem(py + step, PY)), device_id_type=MESH)
        return carry

    pairs = (
        (corr_hbm, corr_ref), (solute_hbm, solute_ref), (xh_hbm, xh_ref), (xl_hbm, xl_ref),
        (ch_hbm, ch_ref), (cl_hbm, cl_ref), (sh_hbm, sh_ref), (sl_hbm, sl_ref),
        (home_hbm, home_ref), (brick_hbm, brick_ref), (slot_hbm, slot_ref),
        (chi_hbm.at[:, :, 0], chi0), (chi_hbm.at[:, :, 1, 0], chi1),
        (basis_hbm, basis_ref), (fock_hbm, fock_ref),
    )
    loads = [pltpu.make_async_copy(source, to, in_sem.at[i]) for i, (source, to) in enumerate(pairs)]
    for load in loads[:11]:
        load.start()
    lax.fori_loop(1, PX, greet_px, 0)
    lax.fori_loop(1, PY, greet_py, 0)
    for load in loads[11:]:
        load.start()
    for load in loads[:4]:
        load.wait()

    lane = lax.broadcasted_iota(jnp.int32, (1, 128), 1)
    lane_re = lane < 64
    lane_field = lax.rem(lane // R, FIELDS)
    lane_spec = (lax.rem(lane, R) == 0) & (py == 0)

    lane_site = jnp.concatenate([lane_field, lane_field], axis=1)

    def x_forward(yp, carry):
        parts = []
        for site in range(SITES):
            rows = closure(corr_ref[site, pl.ds(2 * yp, 2)], solute_ref[site, pl.ds(2 * yp, 2)])
            parts.append(rows.reshape(64, N))
        data = split(jnp.concatenate(parts, axis=0))
        for pair in range(PY // 2):
            wide = dot3(dot, data, (xh_ref[:, 256 * pair:256 * pair + 256], xl_ref[:, 256 * pair:256 * pair + 256]))
            rows = jnp.where(lane_site == 0, wide[0:64], jnp.where(lane_site == 1, wide[64:128], wide[128:192]))
            rows = encode(jnp.where(lane_site == 3, 0.0, rows), CENTRE_X)
            s1[2 * pair, pl.ds(2 * yp, 2)] = rows[:, 0:128].reshape(2, 32, 128)
            s1[2 * pair + 1, pl.ds(2 * yp, 2)] = rows[:, 128:256].reshape(2, 32, 128)

        @pl.when(yp == 0)
        def _():
            pl.semaphore_wait(barrier, PX + PY - 2)

        pltpu.make_async_copy(
            s1.at[py, pl.ds(2 * yp, 2)], b1.at[pl.ds(2 * yp, 2), pl.ds(32 * py, 32)], recv1.at[yp]
        ).start()

        def send(step, inner):
            other = lax.rem(py + step, PY)
            pltpu.make_async_remote_copy(
                src_ref=s1.at[other, pl.ds(2 * yp, 2)],
                dst_ref=b1.at[pl.ds(2 * yp, 2), pl.ds(32 * py, 32)],
                send_sem=send1.at[yp], recv_sem=recv1.at[yp],
                device_id=(px, other), device_id_type=MESH,
            ).start()
            return inner

        return lax.fori_loop(1, PY, send, carry)

    lax.fori_loop(0, 4, x_forward, 0)

    for load in loads[8:11]:
        load.wait()
    home = home_ref[...]
    brick = brick_ref[...]
    down = lax.broadcasted_iota(jnp.int32, (32, 32), 0)
    across = lax.broadcasted_iota(jnp.int32, (32, 32), 1)
    home_down = jnp.sum(jnp.where(down == across, home, 0), axis=1, keepdims=True)
    place = jnp.sum(jnp.where((home_down == home) & (down < across), 1, 0), axis=0, keepdims=True)
    wide_lane = lax.broadcasted_iota(jnp.int32, (32, 128), 1)
    asked = jnp.zeros((32, 128), jnp.int32)
    for k in range(MOST):
        found = jnp.sum(jnp.where((home == down) & (place == k), brick, 0), axis=1, keepdims=True)
        asked = jnp.where(wide_lane == k, jnp.clip(found, 0, 127), asked)
    for other in range(PX):
        ask_out[other] = asked[other:other + 1]
    table = jnp.zeros((32, 128), jnp.int32)
    for k, (value, most) in enumerate(((across, 31), (home, PX - 1), (place, MOST - 1))):
        found = jnp.sum(jnp.where(slot_ref[...] == down, value, 0), axis=1, keepdims=True)
        table = jnp.where(wide_lane == k, jnp.clip(found, 0, most), table)
    info[...] = table
    info_copy = pltpu.make_async_copy(info, info_smem, brick_sem.at[0])
    info_copy.start()
    pltpu.make_async_copy(ask_out.at[px], ask_in.at[px], brick_sem.at[2]).start()

    def ask(step, carry):
        other = lax.rem(px + step, PX)
        pltpu.make_async_remote_copy(
            src_ref=ask_out.at[other], dst_ref=ask_in.at[px],
            send_sem=brick_sem.at[1], recv_sem=brick_sem.at[2],
            device_id=(other, py), device_id_type=MESH,
        ).start()
        return carry

    lax.fori_loop(1, PX, ask, 0)
    for load in loads[4:8]:
        load.wait()

    cos = (ch_ref[...], cl_ref[...])
    sin = (sh_ref[...], sl_ref[...])
    wave = lax.broadcasted_iota(jnp.int32, (N, 1), 0)
    wave_edge = (wave == 0) | (wave == N // 2)
    wave_low = wave < N // 2
    wave_high = wave > N // 2

    def z_forward(yp, carry):
        chunk = b1.at[pl.ds(2 * yp, 2)]
        pltpu.make_async_copy(chunk, chunk, recv1.at[yp]).wait()
        data = split(jnp.concatenate([decode(b1[2 * yp + u], CENTRE_X) for u in range(2)], axis=1))
        cos_data = dot3(dot, cos, data)
        sin_data = dot3(dot, sin, data)
        halves = []
        for u in range(2):
            cd = cos_data[:, 128 * u:128 * u + 128]
            sd = sin_data[:, 128 * u:128 * u + 128]
            cd_turn = pltpu.roll(cd, 64, 1)
            sd_turn = pltpu.roll(sd, 64, 1)
            usual = jnp.where(lane_re, cd + sd_turn, cd - sd_turn)
            packed_re = jnp.where(wave_high, cd_turn, cd)
            packed_im = jnp.where(wave_edge, cd, jnp.where(wave_low, -sd_turn, -sd))
            packed = jnp.where(lane_re, packed_re, packed_im)
            halves.append(jnp.where(lane_spec, packed, usual).reshape(PX, 8, 128))
        s2[:, yp] = encode(jnp.concatenate(halves, axis=1), CENTRE_Z)
        pltpu.make_async_copy(s2.at[px, yp], b2.at[px, yp], recv2.at[yp]).start()

        def send(step, inner):
            other = lax.rem(px + step, PX)
            pltpu.make_async_remote_copy(
                src_ref=s2.at[other, yp], dst_ref=b2.at[px, yp],
                send_sem=send2.at[yp], recv_sem=recv2.at[yp],
                device_id=(other, py), device_id_type=MESH,
            ).start()
            return inner

        return lax.fori_loop(1, PX, send, carry)

    lax.fori_loop(0, 4, z_forward, 0)

    def collect(buffer, sem, centre):
        def body(part, carry):
            chunk = buffer.at[:, part]
            pltpu.make_async_copy(chunk, chunk, sem.at[part]).wait()

            def place(group, inner):
                sources = pl.ds(8 * group, 8)
                ys[sources, pl.ds(pl.multiple_of(16 * part, 16), 16), :] = decode(buffer[sources, part], centre)
                return inner

            return lax.fori_loop(0, PX // 8, place, carry)

        lax.fori_loop(0, 4, body, 0)

    pencils = ys.reshape(PX * 64, 128)

    def turn_basis(item, carry):
        turned_basis[item] = basis_ref[item].T
        return carry

    loads[13].wait()
    lax.fori_loop(0, 32, turn_basis, 0)
    collect(b2, recv2, CENTRE_Z)
    loads[11].wait()
    loads[12].wait()

    row = lax.broadcasted_iota(jnp.int32, (R, 1), 0)
    first = (row == 0) & (py == 0)
    wave_y = lax.broadcasted_iota(jnp.int32, (1, N), 1)
    unit = 2.0 * np.pi / N

    def signed_square(index):
        shifted = (lax.rem(index + N // 2, N) - N // 2).astype(F32) * unit
        return shifted * shifted

    square_y = signed_square(wave_y)
    scale = jnp.where(first, 2.0 ** -24, 2.0 ** -23)

    def mix(chi_of, x_re, x_im, screened):
        out_re, out_im = [], []
        pot_re = pot_im = 0.0
        for a in range(SITES):
            t_re = t_im = 0.0
            for b in range(SITES):
                factor = chi_of(a, b)
                t_re = t_re + factor * x_re[b]
                t_im = t_im + factor * x_im[b]
            out_re.append((t_re - x_re[a]) * scale)
            out_im.append((t_im - x_im[a]) * scale)
            pot_re = pot_re + charge_ref[a] * t_re
            pot_im = pot_im + charge_ref[a] * t_im
        out_re.append(pot_re * (screened * scale))
        out_im.append(pot_im * (screened * scale))
        return out_re, out_im

    def y_both(kp, carry):
        plain, turned = [], []
        rows = jnp.concatenate(
            [pencils[pl.ds(2 * kp + u, N, stride=8), :].T for u in range(2)], axis=0
        )
        data = split(rows)
        cos_data = dot3(dot, data, cos)
        sin_data = dot3(dot, data, sin)
        for u in range(2):
            kz = 2 * kp + u
            kz_all = px * 8 + kz
            base = 128 * u
            pick = lambda array, c, s: array[base + 64 * c + 16 * s:base + 64 * c + 16 * s + 16]
            c_re = [pick(cos_data, 0, s) for s in range(SITES)]
            c_im = [pick(cos_data, 1, s) for s in range(SITES)]
            s_re = [pick(sin_data, 0, s) for s in range(SITES)]
            s_im = [pick(sin_data, 1, s) for s in range(SITES)]
            x_re = [c_re[s] + s_im[s] for s in range(SITES)]
            x_im = [c_im[s] - s_re[s] for s in range(SITES)]
            upper = first & (kz_all > N // 2)
            kx = jnp.where(upper, N // 2, py * R + row)
            square_z = signed_square(jnp.full((1, 1), kz_all, jnp.int32))
            rest = square_z + square_y + 1.0
            screened = (4.0 * np.pi) / (signed_square(kx) + rest)
            chi_of = lambda a, b: jnp.where(upper, chi1[a, b, pl.ds(kz, 1), :], chi0[a, b, :, kz, :])
            if u == 0:
                edge = first & ((kz_all == 0) | (kz_all == N // 2))
                b_re = [c_im[s] for s in range(SITES)]
                b_im = [-s_im[s] for s in range(SITES)]
                x_re = [jnp.where(edge, c_re[s], x_re[s]) for s in range(SITES)]
                x_im = [jnp.where(edge, -s_re[s], x_im[s]) for s in range(SITES)]
                f_re, f_im = mix(chi_of, x_re, x_im, screened)
                screened = (4.0 * np.pi) / (np.pi ** 2 + rest)
                g_re, g_im = mix(lambda a, b: chi1[a, b, pl.ds(kz, 1), :], b_re, b_im, screened)
                plain += f_re + [jnp.where(edge, g_re[f], f_im[f]) for f in range(FIELDS)]
                turned += [-value for value in f_im]
                turned += [jnp.where(edge, -g_im[f], f_re[f]) for f in range(FIELDS)]
            else:
                f_re, f_im = mix(chi_of, x_re, x_im, screened)
                plain += f_re + f_im
                turned += [-value for value in f_im] + f_re
        plain = split(jnp.concatenate(plain, axis=0))
        turned = split(jnp.concatenate(turned, axis=0))
        back = dot3(dot_nt, cos, plain) + dot3(dot_nt, sin, turned)
        s3[:, kp] = encode(
            jnp.concatenate([back[:, 128 * u:128 * u + 128].reshape(PX, 8, 128) for u in range(2)], axis=1),
            CENTRE_Y,
        )
        pltpu.make_async_copy(s3.at[px, kp], b3.at[px, kp], recv3.at[kp]).start()

        def send(step, inner):
            other = lax.rem(px + step, PX)
            pltpu.make_async_remote_copy(
                src_ref=s3.at[other, kp], dst_ref=b3.at[px, kp],
                send_sem=send3.at[kp], recv_sem=recv3.at[kp],
                device_id=(other, py), device_id_type=MESH,
            ).start()
            return inner

        return lax.fori_loop(1, PX, send, carry)

    lax.fori_loop(0, 4, y_both, 0)

    collect(b3, recv3, CENTRE_Y)

    def z_backward(yp, carry):
        plain, turned = [], []
        for u in range(2):
            data = pencils[pl.ds(2 * yp + u, N, stride=8), :]
            turn = pltpu.roll(data, 64, 1)
            packed_re = jnp.where(wave_edge, data, jnp.where(wave_low, data + data, 0.0))
            packed_im = jnp.where(wave_edge, data, jnp.where(wave_low, 0.0, turn + turn))
            other_re = jnp.where(wave_low & ~wave_edge, -2.0 * turn, 0.0)
            other_im = jnp.where(wave_high, -2.0 * data, 0.0)
            plain.append(jnp.where(lane_spec, jnp.where(lane_re, packed_re, packed_im), data))
            turned.append(jnp.where(
                lane_spec, jnp.where(lane_re, other_re, other_im), jnp.where(lane_re, -turn, turn)
            ))
        plain = split(jnp.concatenate(plain, axis=1))
        turned = split(jnp.concatenate(turned, axis=1))
        back = encode(dot3(dot, cos, plain) + dot3(dot, sin, turned), CENTRE_BACK)
        s4[2 * yp] = back[:, 0:128]
        s4[2 * yp + 1] = back[:, 128:256]
        pltpu.make_async_copy(
            s4.at[pl.ds(2 * yp, 2), pl.ds(32 * py, 32)], b4.at[py, pl.ds(2 * yp, 2)], recv4.at[yp]
        ).start()

        def send(step, inner):
            other = lax.rem(py + step, PY)
            pltpu.make_async_remote_copy(
                src_ref=s4.at[pl.ds(2 * yp, 2), pl.ds(32 * other, 32)],
                dst_ref=b4.at[py, pl.ds(2 * yp, 2)],
                send_sem=send4.at[yp], recv_sem=recv4.at[yp],
                device_id=(px, other), device_id_type=MESH,
            ).start()
            return inner

        return lax.fori_loop(1, PY, send, carry)

    lax.fori_loop(0, 4, z_backward, 0)

    def x_backward(yp, carry):
        chunk = b4.at[:, pl.ds(2 * yp, 2)]
        pltpu.make_async_copy(chunk, chunk, recv4.at[yp]).wait()
        rows = jnp.concatenate(
            [decode(b4[j, pl.ds(2 * yp, 2)], CENTRE_BACK).reshape(64, 128) for j in range(PY)], axis=1
        )
        field = jnp.concatenate([lane_field] * PY, axis=1)
        data = split(jnp.concatenate([jnp.where(field == f, rows, 0.0) for f in range(FIELDS)], axis=0))
        back = dot3(dot_nt, data, (xh_ref[...], xl_ref[...]))
        for f in range(SITES):
            corr_out[f, pl.ds(2 * yp, 2)] = back[64 * f:64 * f + 64].reshape(2, 32, N)
        potential = back[192:256].reshape(2, 32, N)
        potential_out[pl.ds(2 * yp, 2)] = potential
        pot_ref[0, pl.ds(2 * yp, 2)] = potential[:, :, 0:128]
        pot_ref[1, pl.ds(2 * yp, 2)] = potential[:, :, 128:256]
        slabs = pl.ds(2 * yp, 2)
        pltpu.make_async_copy(corr_out.at[:, slabs], corr_hbm_out.at[:, slabs], corr_sem.at[yp]).start()
        pltpu.make_async_copy(potential_out.at[slabs], potential_hbm_out.at[slabs], potential_sem.at[yp]).start()
        return carry

    lax.fori_loop(0, 4, x_backward, 0)

    pltpu.make_async_copy(ask_in, ask_in, brick_sem.at[2]).wait()
    ask_copy = pltpu.make_async_copy(ask_in, ask_smem, brick_sem.at[3])
    ask_copy.start()
    lane_row = lane // 32

    def shuffle(bz, carry):
        for half in range(2):
            slabs = [pot_ref[half, y, pl.ds(8 * bz, 8), :] for y in range(8)]
            for quad in range(4):
                rows = []
                for u in range(2):
                    row = slabs[u]
                    if quad:
                        row = pltpu.roll(row, 128 - 32 * quad, 1)
                    for yg in range(1, 4):
                        move = 32 * ((yg - quad) % 4)
                        other = slabs[2 * yg + u]
                        other = pltpu.roll(other, move, 1) if move else other
                        row = jnp.where(lane_row == yg, other, row)
                    rows.append(row)
                shuffled[8 * bz + 4 * half + quad] = jnp.concatenate(rows, axis=0)
        return carry

    lax.fori_loop(0, 4, shuffle, 0)
    ask_copy.wait()
    lane_place = lax.rem(lane // BRICK, MOST)

    def answer(step, carry):
        other = lax.rem(px + step, PX)
        tile = jnp.zeros((16, 128), F32)
        for k in range(MOST):
            index = ask_smem[other, 0, k]
            moved = pltpu.roll(shuffled[index // 4], lax.rem(BRICK * (k - lax.rem(index, 4)) + 128, 128), 1)
            tile = jnp.where(lane_place == k, moved, tile)
        brick_out[other] = tile.astype(BF16)

        @pl.when(step > 0)
        def _():
            pltpu.make_async_remote_copy(
                src_ref=brick_out.at[other], dst_ref=brick_in.at[px],
                send_sem=brick_sem.at[4], recv_sem=brick_sem.at[5],
                device_id=(other, py), device_id_type=MESH,
            ).start()

        return carry

    lax.fori_loop(0, PX, answer, 0, unroll=2)
    pltpu.make_async_copy(brick_out.at[px], brick_in.at[px], brick_sem.at[5]).start()
    info_copy.wait()
    loads[14].wait()
    pltpu.make_async_copy(brick_in, brick_in, brick_sem.at[5]).wait()

    def take(slot, carry):
        tile = brick_in[info_smem[slot, 1]].astype(F32)
        tile = pltpu.roll(tile, lax.rem(128 - BRICK * info_smem[slot, 2], 128), 1)
        tiles[pl.ds(pl.multiple_of(16 * slot, 16), 16), :] = tile.astype(BF16)
        return carry

    lax.fori_loop(0, 32, take, 0, unroll=4)
    cell = lax.broadcasted_iota(jnp.int32, (128, 512), 1)
    origin = lax.broadcasted_iota(jnp.int32, (128, 512), 0)
    spread = (origin == 32 * (cell // 128) + lax.rem(cell, BRICK)).astype(F32).astype(BF16)
    wide = dot(tiles[...], spread)
    tile_row = lax.broadcasted_iota(jnp.int32, (512, 512), 0)
    tile_cell = lax.broadcasted_iota(jnp.int32, (512, 512), 1)
    wide = jnp.where(lax.rem(tile_row, 16) == lax.rem(tile_cell, 128) // BRICK, wide, 0.0).astype(BF16)
    slot_down = lax.broadcasted_iota(jnp.int32, (32, 512), 0)
    slot_cell = lax.broadcasted_iota(jnp.int32, (32, 512), 1)
    samples[...] = dot((slot_down == slot_cell // 16).astype(F32).astype(BF16), wide)

    def embed(group, carry):
        for item in range(4):
            slot = 4 * group + item
            fragment = info_smem[slot, 0]
            weighted = turned_basis[fragment] * samples[pl.ds(slot, 1), :].astype(BF16)
            fock_out[slot] = fock_ref[slot] + dot(weighted, basis_ref[fragment])
        slots = pl.ds(4 * group, 4)
        pltpu.make_async_copy(fock_out.at[slots], fock_hbm_out.at[slots], fock_sem.at[group]).start()
        return carry

    lax.fori_loop(0, 8, embed, 0)
    for part in range(4):
        slabs = pl.ds(2 * part, 2)
        pltpu.make_async_copy(corr_out.at[:, slabs], corr_hbm_out.at[:, slabs], corr_sem.at[part]).wait()
        pltpu.make_async_copy(potential_out.at[slabs], potential_hbm_out.at[slabs], potential_sem.at[part]).wait()
    for part in range(8):
        slots = pl.ds(4 * part, 4)
        pltpu.make_async_copy(fock_out.at[slots], fock_hbm_out.at[slots], fock_sem.at[part]).wait()

    for part in range(4):
        sent = s1.at[pl.ds(0, PY - 1), pl.ds(0, 2)]
        pltpu.make_async_copy(sent, sent, send1.at[part]).wait()
        sent = s2.at[pl.ds(0, PX - 1), 0]
        pltpu.make_async_copy(sent, sent, send2.at[part]).wait()
        pltpu.make_async_copy(sent, sent, send3.at[part]).wait()
        sent = s4.at[pl.ds(0, 2), pl.ds(0, 32 * (PY - 1))]
        pltpu.make_async_copy(sent, sent, send4.at[part]).wait()
    sent = ask_out.at[pl.ds(0, PX - 1)]
    pltpu.make_async_copy(sent, sent, brick_sem.at[1]).wait()
    sent = brick_out.at[pl.ds(0, PX - 1)]
    pltpu.make_async_copy(sent, sent, brick_sem.at[4]).wait()


def shards(
    corr, solute_pot, chi, site_charge, home_slab, brick_index, block_slot, basis_values, fock_in
):
    hbm = pl.BlockSpec(memory_space=pltpu.HBM)
    dma = pltpu.SemaphoreType.DMA((4,))
    frags = home_slab.shape[0]
    return pl.pallas_call(
        field_kernel,
        name="fields",
        out_shape=(
            jax.ShapeDtypeStruct((SITES, 8, 32, N), F32),
            jax.ShapeDtypeStruct((8, 32, N), F32),
            jax.ShapeDtypeStruct(fock_in.shape, F32),
        ),
        in_specs=[pl.BlockSpec(memory_space=pltpu.SMEM)] + [hbm] * 14,
        out_specs=(hbm,) * 3,
        scratch_shapes=[
            pltpu.VMEM(corr.shape, F32),
            pltpu.VMEM(corr.shape[1:], F32),
            pltpu.VMEM(fock_in.shape, F32),
            pltpu.VMEM(corr.shape, F32),
            pltpu.VMEM(solute_pot.shape, BF16),
            pltpu.VMEM((SITES, SITES, R, 8, N), F32),
            pltpu.VMEM((SITES, SITES, 8, N), F32),
            pltpu.VMEM((1, frags), jnp.int32),
            pltpu.VMEM((1, frags), jnp.int32),
            pltpu.VMEM((1, frags), jnp.int32),
            pltpu.VMEM(basis_values.shape, BF16),
            pltpu.VMEM(fock_in.shape, F32),
            pltpu.VMEM((N, PY * 128), BF16),
            pltpu.VMEM((N, PY * 128), BF16),
            pltpu.VMEM((N, N), BF16),
            pltpu.VMEM((N, N), BF16),
            pltpu.VMEM((N, N), BF16),
            pltpu.VMEM((N, N), BF16),
            pltpu.VMEM((PY, 8, 32, 128), WIRE),
            pltpu.VMEM((8, N, 128), WIRE),
            pltpu.VMEM((PX, 4, 16, 128), WIRE),
            pltpu.VMEM((PX, 4, 16, 128), WIRE),
            pltpu.VMEM((PX, 64, 128), F32),
            pltpu.VMEM((PX, 4, 16, 128), WIRE),
            pltpu.VMEM((PX, 4, 16, 128), WIRE),
            pltpu.VMEM((8, N, 128), WIRE),
            pltpu.VMEM((PY, 8, 32, 128), WIRE),
            pltpu.VMEM((PX, 1, 128), jnp.int32),
            pltpu.VMEM((PX, 1, 128), jnp.int32),
            pltpu.SMEM((PX, 1, 128), jnp.int32),
            pltpu.VMEM((frags, 128), jnp.int32),
            pltpu.SMEM((frags, 128), jnp.int32),
            pltpu.VMEM((2, 8, 32, 128), F32),
            pltpu.VMEM((32, 16, 128), F32),
            pltpu.VMEM((PX, 16, 128), BF16),
            pltpu.VMEM((PX, 16, 128), BF16),
            pltpu.VMEM((frags, 128, 512), BF16),
            pltpu.VMEM((frags * 16, 128), BF16),
            pltpu.VMEM((frags, 512), F32),
            pltpu.SemaphoreType.DMA((15,)),
        ] + [dma] * 8 + [pltpu.SemaphoreType.DMA((6,)), dma, dma, pltpu.SemaphoreType.DMA((8,))],
        compiler_params=pltpu.CompilerParams(
            collective_id=0, has_side_effects=True, vmem_limit_bytes=60 * 2**20
        ),
    )(
        site_charge, corr, solute_pot, chi, home_slab.reshape(1, frags), brick_index.reshape(1, frags),
        block_slot, basis_values, fock_in, *[jnp.asarray(table) for table in tables()],
    )


def solution(mesh):
    return jax.shard_map(
        shards,
        mesh=mesh,
        in_specs=(
            P(None, "px", "py", None),
            P(None, "px", "py", None),
            P(None, None, None, "py", "px", None),
            P(),
            P(("px", "py"), None),
            P(("px", "py")),
            P(("px", "py"), None),
            P(("px", "py"), None, None),
            P(("px", "py"), None, None),
        ),
        out_specs=(P(None, "px", "py", None), P("px", "py", None), P(("px", "py"), None, None)),
        check_vma=False,
    )
```

```python
import functools
import jax
import jax.numpy as jnp
import numpy as np
from jax import lax
from jax.experimental import pallas as pl
from jax.experimental.pallas import tpu as pltpu
from jax.sharding import PartitionSpec as P

BRICK = 8
MOST = 4
N = 256
PX = 32
PY = 8
SITES = 3
FIELDS = 4
R = 16
MESH = pl.DeviceIdType.MESH
F32 = jnp.float32
BF16 = jnp.bfloat16
WIRE = jnp.bfloat16
FINE, STEEP, SLOPE = 11.0, 8.0, 3.0
CENTRE_X, CENTRE_Z, CENTRE_Y, CENTRE_BACK = 5.0, 9.0, -5.0, -1.0


def split(values):
    high = values.astype(BF16)
    return high, (values - high.astype(F32)).astype(BF16)


def np_split(values):
    high = values.astype(np.float32).astype(BF16)
    low = (values - high.astype(np.float64)).astype(np.float32).astype(BF16)
    return high, low


def tables():
    index = np.arange(N)
    angle = (index[:, None] * index[None, :] % N) * (2.0 * np.pi / N)
    cos, sin = np.cos(angle), np.sin(angle)
    half_re = cos[:, : N // 2].copy()
    half_im = -sin[:, : N // 2]
    half_im[:, 0] = cos[:, N // 2]
    halves = np.stack([half_re.reshape(N, PY, R), half_im.reshape(N, PY, R)], axis=2)
    spread = np.broadcast_to(halves[:, :, :, None, :], (N, PY, 2, FIELDS, R))
    spread = spread.reshape(N, PY * 128)
    order = index % PX * 8 + index // PX
    return np_split(spread) + np_split(cos) + np_split(sin) + np_split(cos[:, order]) + np_split(sin[:, order])


def encode(values, centre):
    power = jnp.log2(jnp.abs(values)) - centre
    power = SLOPE * power + (STEEP - SLOPE) * jnp.clip(power, -FINE, FINE)
    coded = jnp.exp2(power)
    return jnp.where(values < 0, -coded, coded).astype(WIRE)


def decode(coded, centre):
    coded = coded.astype(F32)
    power = jnp.log2(jnp.abs(coded))
    fine = jnp.clip(power, -FINE * STEEP, FINE * STEEP)
    values = jnp.exp2(power * (1.0 / SLOPE) + fine * (1.0 / STEEP - 1.0 / SLOPE) + centre)
    return jnp.where(coded < 0, -values, values)


def dot(left, right):
    return jnp.dot(left, right, preferred_element_type=F32)


def dot_nt(left, right):
    return lax.dot_general(left, right, (((1,), (1,)), ((), ())), preferred_element_type=F32)


def dot3(product, left, right):
    return product(left[0], right[0]) + product(left[0], right[1]) + product(left[1], right[0])


def closure(corr, solute_pot):
    excess = corr - solute_pot.astype(F32)
    low = jnp.minimum(excess, 0.0)
    series = jnp.full_like(low, 1.0 / 362880.0)
    for denominator in (40320.0, 5040.0, 720.0, 120.0, 24.0, 6.0, 2.0, 1.0):
        series = series * low + 1.0 / denominator
    grown = jnp.where(low > -0.5, series * low, jnp.exp(low) - 1.0)
    return jnp.where(excess > 0, excess, grown) - corr


def field_kernel(
    charge_ref, corr_hbm, solute_hbm, chi_hbm, home_hbm, brick_hbm, slot_hbm, basis_hbm, fock_hbm,
    xh_hbm, xl_hbm, ch_hbm, cl_hbm, sh_hbm, sl_hbm, och_hbm, ocl_hbm, osh_hbm, osl_hbm,
    corr_hbm_out, potential_hbm_out, fock_hbm_out,
    corr_out, potential_out, fock_out,
    corr_ref, solute_ref, chi0, chi1, home_ref, brick_ref, slot_ref, basis_ref, fock_ref,
    xh_ref, xl_ref, ch_ref, cl_ref, sh_ref, sl_ref, och_ref, ocl_ref, osh_ref, osl_ref,
    s1, b1, s2, b2, ys, plain_k, turned_k, s3p, b3p, ysp, s4p, b4p, s3, b3, yc, s4, b4,
    ask_out, ask_in, ask_smem, info, info_smem, pot_ref, shuffled, brick_out, brick_in, turned_basis, tiles, samples,
    in_sem, send1, recv1, send2, recv2, send3, recv3, send4, recv4, pot_sem, brick_sem, corr_sem, potential_sem, fock_sem,
):
    px = lax.axis_index("px")
    py = lax.axis_index("py")
    barrier = pltpu.get_barrier_semaphore()

    def greet_px(step, carry):
        pl.semaphore_signal(barrier, inc=1, device_id=(lax.rem(px + step, PX), py), device_id_type=MESH)
        return carry

    def greet_py(step, carry):
        pl.semaphore_signal(barrier, inc=1, device_id=(px, lax.rem(py + step, PY)), device_id_type=MESH)
        return carry

    pairs = (
        (corr_hbm, corr_ref), (solute_hbm, solute_ref), (xh_hbm, xh_ref), (xl_hbm, xl_ref),
        (ch_hbm, ch_ref), (cl_hbm, cl_ref), (sh_hbm, sh_ref), (sl_hbm, sl_ref),
        (home_hbm, home_ref), (brick_hbm, brick_ref), (slot_hbm, slot_ref),
        (chi_hbm.at[:, :, 0], chi0), (chi_hbm.at[:, :, 1, 0], chi1),
        (basis_hbm, basis_ref), (fock_hbm, fock_ref),
        (och_hbm, och_ref), (ocl_hbm, ocl_ref), (osh_hbm, osh_ref), (osl_hbm, osl_ref),
    )
    loads = [pltpu.make_async_copy(source, to, in_sem.at[i]) for i, (source, to) in enumerate(pairs)]
    for load in loads[:11]:
        load.start()
    lax.fori_loop(1, PX, greet_px, 0)
    lax.fori_loop(1, PY, greet_py, 0)
    for load in loads[11:]:
        load.start()
    for load in loads[:4]:
        load.wait()

    lane = lax.broadcasted_iota(jnp.int32, (1, 128), 1)
    lane_re = lane < 64
    lane_field = lax.rem(lane // R, FIELDS)
    lane_spec = (lax.rem(lane, R) == 0) & (py == 0)

    lane_site = jnp.concatenate([lane_field, lane_field], axis=1)

    def x_forward(yp, carry):
        parts = []
        for site in range(SITES):
            rows = closure(corr_ref[site, pl.ds(2 * yp, 2)], solute_ref[site, pl.ds(2 * yp, 2)])
            parts.append(rows.reshape(64, N))
        data = split(jnp.concatenate(parts, axis=0))
        for pair in range(PY // 2):
            wide = dot3(dot, data, (xh_ref[:, 256 * pair:256 * pair + 256], xl_ref[:, 256 * pair:256 * pair + 256]))
            rows = jnp.where(lane_site == 0, wide[0:64], jnp.where(lane_site == 1, wide[64:128], wide[128:192]))
            rows = encode(jnp.where(lane_site == 3, 0.0, rows), CENTRE_X)
            s1[2 * pair, pl.ds(2 * yp, 2)] = rows[:, 0:128].reshape(2, 32, 128)
            s1[2 * pair + 1, pl.ds(2 * yp, 2)] = rows[:, 128:256].reshape(2, 32, 128)

        @pl.when(yp == 0)
        def _():
            pl.semaphore_wait(barrier, PX + PY - 2)

        pltpu.make_async_copy(
            s1.at[py, pl.ds(2 * yp, 2)], b1.at[pl.ds(2 * yp, 2), pl.ds(32 * py, 32)], recv1.at[yp]
        ).start()

        def send(step, inner):
            other = lax.rem(py + step, PY)
            pltpu.make_async_remote_copy(
                src_ref=s1.at[other, pl.ds(2 * yp, 2)],
                dst_ref=b1.at[pl.ds(2 * yp, 2), pl.ds(32 * py, 32)],
                send_sem=send1.at[yp], recv_sem=recv1.at[yp],
                device_id=(px, other), device_id_type=MESH,
            ).start()
            return inner

        return lax.fori_loop(1, PY, send, carry)

    lax.fori_loop(0, 4, x_forward, 0)

    for load in loads[8:11]:
        load.wait()
    home = home_ref[...]
    brick = brick_ref[...]
    down = lax.broadcasted_iota(jnp.int32, (32, 32), 0)
    across = lax.broadcasted_iota(jnp.int32, (32, 32), 1)
    home_down = jnp.sum(jnp.where(down == across, home, 0), axis=1, keepdims=True)
    place = jnp.sum(jnp.where((home_down == home) & (down < across), 1, 0), axis=0, keepdims=True)
    wide_lane = lax.broadcasted_iota(jnp.int32, (32, 128), 1)
    asked = jnp.zeros((32, 128), jnp.int32)
    for k in range(MOST):
        found = jnp.sum(jnp.where((home == down) & (place == k), brick, 0), axis=1, keepdims=True)
        asked = jnp.where(wide_lane == k, jnp.clip(found, 0, 127), asked)
    for other in range(PX):
        ask_out[other] = asked[other:other + 1]
    table = jnp.zeros((32, 128), jnp.int32)
    for k, (value, most) in enumerate(((across, 31), (home, PX - 1), (place, MOST - 1))):
        found = jnp.sum(jnp.where(slot_ref[...] == down, value, 0), axis=1, keepdims=True)
        table = jnp.where(wide_lane == k, jnp.clip(found, 0, most), table)
    info[...] = table
    info_copy = pltpu.make_async_copy(info, info_smem, brick_sem.at[0])
    info_copy.start()
    pltpu.make_async_copy(ask_out.at[px], ask_in.at[px], brick_sem.at[2]).start()

    def ask(step, carry):
        other = lax.rem(px + step, PX)
        pltpu.make_async_remote_copy(
            src_ref=ask_out.at[other], dst_ref=ask_in.at[px],
            send_sem=brick_sem.at[1], recv_sem=brick_sem.at[2],
            device_id=(other, py), device_id_type=MESH,
        ).start()
        return carry

    lax.fori_loop(1, PX, ask, 0)
    for load in loads[4:8]:
        load.wait()

    cos = (ch_ref[...], cl_ref[...])
    sin = (sh_ref[...], sl_ref[...])
    wave = lax.broadcasted_iota(jnp.int32, (N, 1), 0)
    wave_edge = (wave == 0) | (wave == N // 2)
    wave_low = wave < N // 2
    wave_high = wave > N // 2

    def z_forward(yp, carry):
        chunk = b1.at[pl.ds(2 * yp, 2)]
        pltpu.make_async_copy(chunk, chunk, recv1.at[yp]).wait()
        data = split(jnp.concatenate([decode(b1[2 * yp + u], CENTRE_X) for u in range(2)], axis=1))
        cos_data = dot3(dot, cos, data)
        sin_data = dot3(dot, sin, data)
        halves = []
        for u in range(2):
            cd = cos_data[:, 128 * u:128 * u + 128]
            sd = sin_data[:, 128 * u:128 * u + 128]
            cd_turn = pltpu.roll(cd, 64, 1)
            sd_turn = pltpu.roll(sd, 64, 1)
            usual = jnp.where(lane_re, cd + sd_turn, cd - sd_turn)
            packed_re = jnp.where(wave_high, cd_turn, cd)
            packed_im = jnp.where(wave_edge, cd, jnp.where(wave_low, -sd_turn, -sd))
            packed = jnp.where(lane_re, packed_re, packed_im)
            halves.append(jnp.where(lane_spec, packed, usual).reshape(PX, 8, 128))
        s2[:, yp] = encode(jnp.concatenate(halves, axis=1), CENTRE_Z)
        pltpu.make_async_copy(s2.at[px, yp], b2.at[px, yp], recv2.at[yp]).start()

        def send(step, inner):
            other = lax.rem(px + step, PX)
            pltpu.make_async_remote_copy(
                src_ref=s2.at[other, yp], dst_ref=b2.at[px, yp],
                send_sem=send2.at[yp], recv_sem=recv2.at[yp],
                device_id=(other, py), device_id_type=MESH,
            ).start()
            return inner

        return lax.fori_loop(1, PX, send, carry)

    lax.fori_loop(0, 4, z_forward, 0)

    def collect(buffer, sem, centre, ys, parts):
        def body(part, carry):
            chunk = buffer.at[:, part]
            pltpu.make_async_copy(chunk, chunk, sem.at[part]).wait()

            def place(group, inner):
                sources = pl.ds(8 * group, 8)
                ys[sources, pl.ds(pl.multiple_of(16 * part, 16), 16), :] = decode(buffer[sources, part], centre)
                return inner

            return lax.fori_loop(0, PX // 8, place, carry)

        lax.fori_loop(0, parts, body, 0)

    pencils = ys.reshape(PX * 64, 128)

    def turn_basis(item, carry):
        turned_basis[item] = basis_ref[item].T
        return carry

    loads[13].wait()
    lax.fori_loop(0, 32, turn_basis, 0)
    collect(b2, recv2, CENTRE_Z, ys, 4)
    loads[11].wait()
    loads[12].wait()

    row = lax.broadcasted_iota(jnp.int32, (R, 1), 0)
    first = (row == 0) & (py == 0)
    wave_y = lax.broadcasted_iota(jnp.int32, (1, N), 1)
    unit = 2.0 * np.pi / N

    def signed_square(index):
        shifted = (lax.rem(index + N // 2, N) - N // 2).astype(F32) * unit
        return shifted * shifted

    square_y = signed_square(wave_y)
    scale = jnp.where(first, 2.0 ** -24, 2.0 ** -23)

    def mix(chi_of, x_re, x_im, screened):
        out_re, out_im = [], []
        pot_re = pot_im = 0.0
        for a in range(SITES):
            t_re = t_im = 0.0
            for b in range(SITES):
                factor = chi_of(a, b)
                t_re = t_re + factor * x_re[b]
                t_im = t_im + factor * x_im[b]
            out_re.append((t_re - x_re[a]) * scale)
            out_im.append((t_im - x_im[a]) * scale)
            pot_re = pot_re + charge_ref[a] * t_re
            pot_im = pot_im + charge_ref[a] * t_im
        out_re.append(pot_re * (screened * scale))
        out_im.append(pot_im * (screened * scale))
        return out_re, out_im

    def y_forward(quad, carry):
        for pair in range(2):
            rows = jnp.concatenate(
                [pencils[pl.ds(4 * quad + 2 * pair + u, N, stride=8), :].T for u in range(2)], axis=0
            )
            data = split(rows)
            cos_data = dot3(dot, data, cos)
            sin_data = dot3(dot, data, sin)
            for u in range(2):
                k = 2 * pair + u
                kz = 4 * quad + k
                kz_all = px * 8 + kz
                base = 128 * u
                pick = lambda array, c, s: array[base + 64 * c + 16 * s:base + 64 * c + 16 * s + 16]
                c_re = [pick(cos_data, 0, s) for s in range(SITES)]
                c_im = [pick(cos_data, 1, s) for s in range(SITES)]
                s_re = [pick(sin_data, 0, s) for s in range(SITES)]
                s_im = [pick(sin_data, 1, s) for s in range(SITES)]
                x_re = [c_re[s] + s_im[s] for s in range(SITES)]
                x_im = [c_im[s] - s_re[s] for s in range(SITES)]
                upper = first & (kz_all > N // 2)
                kx = jnp.where(upper, N // 2, py * R + row)
                square_z = signed_square(jnp.full((1, 1), kz_all, jnp.int32))
                rest = square_z + square_y + 1.0
                screened = (4.0 * np.pi) / (signed_square(kx) + rest)
                chi_of = lambda a, b: jnp.where(upper, chi1[a, b, pl.ds(kz, 1), :], chi0[a, b, :, kz, :])
                if k == 0:
                    edge = first & ((kz_all == 0) | (kz_all == N // 2))
                    b_re = [c_im[s] for s in range(SITES)]
                    b_im = [-s_im[s] for s in range(SITES)]
                    x_re = [jnp.where(edge, c_re[s], x_re[s]) for s in range(SITES)]
                    x_im = [jnp.where(edge, -s_re[s], x_im[s]) for s in range(SITES)]
                    f_re, f_im = mix(chi_of, x_re, x_im, screened)
                    screened = (4.0 * np.pi) / (np.pi ** 2 + rest)
                    g_re, g_im = mix(lambda a, b: chi1[a, b, pl.ds(kz, 1), :], b_re, b_im, screened)
                    other_plain = [jnp.where(edge, g_re[f], f_im[f]) for f in range(FIELDS)]
                    other_turned = [jnp.where(edge, -g_im[f], f_re[f]) for f in range(FIELDS)]
                else:
                    f_re, f_im = mix(chi_of, x_re, x_im, screened)
                    other_plain, other_turned = f_im, f_re
                for f in range(FIELDS):
                    if f == SITES:
                        group, slot = 6 + quad, k
                    elif k < 3:
                        group, slot = 3 * quad + k, f
                    else:
                        group, slot = 3 * quad + f, 3
                    plain_k[group, pl.ds(16 * slot, 16), :] = f_re[f]
                    plain_k[group, pl.ds(64 + 16 * slot, 16), :] = other_plain[f]
                    turned_k[group, pl.ds(16 * slot, 16), :] = -f_im[f]
                    turned_k[group, pl.ds(64 + 16 * slot, 16), :] = other_turned[f]
        return carry

    lax.fori_loop(0, 2, y_forward, 0)

    def y_backward(unit):
        groups = pl.ds(2 * unit, 2)
        plain = split(plain_k[groups].reshape(256, N))
        turned = split(turned_k[groups].reshape(256, N))
        back = dot3(dot_nt, cos, plain) + dot3(dot_nt, sin, turned)
        return encode(
            jnp.concatenate([back[:, 128 * u:128 * u + 128].reshape(PX, 8, 128) for u in range(2)], axis=1),
            CENTRE_Y,
        )

    s3p[...] = y_backward(3)
    pltpu.make_async_copy(s3p.at[px], b3p.at[px], pot_sem.at[1]).start()

    def send_potential(step, carry):
        other = lax.rem(px + step, PX)
        pltpu.make_async_remote_copy(
            src_ref=s3p.at[other], dst_ref=b3p.at[px],
            send_sem=pot_sem.at[0], recv_sem=pot_sem.at[1],
            device_id=(other, py), device_id_type=MESH,
        ).start()
        return carry

    lax.fori_loop(1, PX, send_potential, 0)

    def y_corr(unit, carry):
        s3[:, unit] = y_backward(unit)
        pltpu.make_async_copy(s3.at[px, unit], b3.at[px, unit], recv3.at[unit]).start()

        def send(step, inner):
            other = lax.rem(px + step, PX)
            pltpu.make_async_remote_copy(
                src_ref=s3.at[other, unit], dst_ref=b3.at[px, unit],
                send_sem=send3.at[unit], recv_sem=recv3.at[unit],
                device_id=(other, py), device_id_type=MESH,
            ).start()
            return inner

        return lax.fori_loop(1, PX, send, carry)

    lax.fori_loop(0, 3, y_corr, 0)

    for load in loads[15:19]:
        load.wait()
    cos_order = (och_ref[...], ocl_ref[...])
    sin_order = (osh_ref[...], osl_ref[...])
    order = lax.rem(wave, PX) * 8 + wave // PX
    order_edge = (order == 0) | (order == N // 2)
    order_low = order < N // 2
    order_high = order > N // 2

    def z_inverse(columns):
        plain, turned = [], []
        for data in columns:
            turn = pltpu.roll(data, 64, 1)
            packed_re = jnp.where(order_edge, data, jnp.where(order_low, data + data, 0.0))
            packed_im = jnp.where(order_edge, data, jnp.where(order_low, 0.0, turn + turn))
            other_re = jnp.where(order_low & ~order_edge, -2.0 * turn, 0.0)
            other_im = jnp.where(order_high, -2.0 * data, 0.0)
            plain.append(jnp.where(lane_spec, jnp.where(lane_re, packed_re, packed_im), data))
            turned.append(jnp.where(
                lane_spec, jnp.where(lane_re, other_re, other_im), jnp.where(lane_re, -turn, turn)
            ))
        plain = split(jnp.concatenate(plain, axis=1))
        turned = split(jnp.concatenate(turned, axis=1))
        return dot3(dot, cos_order, plain) + dot3(dot, sin_order, turned)

    def shift(data, slots):
        return pltpu.roll(data, 16 * slots % 128, 1) if slots else data

    def x_inverse(rows, count):
        field = jnp.concatenate([lane_field] * PY, axis=1)
        data = split(jnp.concatenate([jnp.where(field == f, rows, 0.0) for f in range(count)], axis=0))
        return dot3(dot_nt, data, (xh_ref[...], xl_ref[...]))

    pltpu.make_async_copy(b3p, b3p, pot_sem.at[1]).wait()
    ysp[...] = decode(b3p[...], CENTRE_Y)
    tiles_in = ysp.reshape(PX * 16, 128)
    columns = []
    for yq in range(2):
        parts = []
        for quad in range(2):
            rows = [tiles_in[pl.ds(8 * quad + 4 * yq + j, PX, stride=16), :] for j in range(4)]
            for k in range(4):
                part = shift(rows[0], -k)
                for j in range(1, 4):
                    part = jnp.where(lane_field == j, shift(rows[j], j - k), part)
                parts.append(part)
        columns.append(jnp.concatenate(parts, axis=0))
    back = encode(z_inverse(columns), CENTRE_BACK)
    s4p[0] = back[:, 0:128]
    s4p[1] = back[:, 128:256]
    pltpu.make_async_copy(s4p.at[:, pl.ds(32 * py, 32)], b4p.at[py], pot_sem.at[3]).start()

    def send_rows(step, carry):
        other = lax.rem(py + step, PY)
        pltpu.make_async_remote_copy(
            src_ref=s4p.at[:, pl.ds(32 * other, 32)], dst_ref=b4p.at[py],
            send_sem=pot_sem.at[2], recv_sem=pot_sem.at[3],
            device_id=(px, other), device_id_type=MESH,
        ).start()
        return carry

    lax.fori_loop(1, PY, send_rows, 0)
    pltpu.make_async_copy(b4p, b4p, pot_sem.at[3]).wait()
    back = x_inverse(
        jnp.concatenate([decode(b4p[j], CENTRE_BACK).reshape(64, 128) for j in range(PY)], axis=1), FIELDS
    )
    for y in range(8):
        start = 64 * (y % 4) + 32 * (y // 4)
        slab = back[start:start + 32]
        potential_out[y] = slab
        pot_ref[0, y] = slab[:, 0:128]
        pot_ref[1, y] = slab[:, 128:256]
    potential_copy = pltpu.make_async_copy(potential_out, potential_hbm_out, potential_sem.at[0])
    potential_copy.start()

    pltpu.make_async_copy(ask_in, ask_in, brick_sem.at[2]).wait()
    ask_copy = pltpu.make_async_copy(ask_in, ask_smem, brick_sem.at[3])
    ask_copy.start()
    lane_row = lane // 32

    def shuffle(bz, carry):
        for half in range(2):
            slabs = [pot_ref[half, y, pl.ds(8 * bz, 8), :] for y in range(8)]
            for quad in range(4):
                rows = []
                for u in range(2):
                    row = slabs[u]
                    if quad:
                        row = pltpu.roll(row, 128 - 32 * quad, 1)
                    for yg in range(1, 4):
                        move = 32 * ((yg - quad) % 4)
                        other = slabs[2 * yg + u]
                        other = pltpu.roll(other, move, 1) if move else other
                        row = jnp.where(lane_row == yg, other, row)
                    rows.append(row)
                shuffled[8 * bz + 4 * half + quad] = jnp.concatenate(rows, axis=0)
        return carry

    lax.fori_loop(0, 4, shuffle, 0)
    ask_copy.wait()
    lane_place = lax.rem(lane // BRICK, MOST)

    def answer(step, carry):
        other = lax.rem(px + step, PX)
        tile = jnp.zeros((16, 128), F32)
        for k in range(MOST):
            index = ask_smem[other, 0, k]
            moved = pltpu.roll(shuffled[index // 4], lax.rem(BRICK * (k - lax.rem(index, 4)) + 128, 128), 1)
            tile = jnp.where(lane_place == k, moved, tile)
        brick_out[other] = tile.astype(BF16)

        @pl.when(step > 0)
        def _():
            pltpu.make_async_remote_copy(
                src_ref=brick_out.at[other], dst_ref=brick_in.at[px],
                send_sem=brick_sem.at[4], recv_sem=brick_sem.at[5],
                device_id=(other, py), device_id_type=MESH,
            ).start()

        return carry

    lax.fori_loop(0, PX, answer, 0, unroll=2)
    pltpu.make_async_copy(brick_out.at[px], brick_in.at[px], brick_sem.at[5]).start()

    collect(b3, recv3, CENTRE_Y, yc, 3)
    packed = yc.reshape(PX * 48, 128)

    def z_backward(yp, carry):
        columns = []
        for u in range(2):
            parts = []
            for quad in range(2):
                rows = [packed[pl.ds(24 * quad + 8 * g + 2 * yp + u, PX, stride=48), :] for g in range(3)]
                last = shift(rows[0], -3)
                for f in range(1, 3):
                    last = jnp.where(lane_field == f, shift(rows[f], f - 3), last)
                parts += rows + [last]
            columns.append(jnp.concatenate(parts, axis=0))
        back = z_inverse(columns)
        parts = []
        for u in range(2):
            rows = back[:, 128 * u:128 * u + 128].reshape(PY, 4, 8, 128)
            last = rows[:, 3].reshape(64, 128)
            for g in range(3):
                part = jnp.where(lane_field == 3, shift(last, 3 - g), rows[:, g].reshape(64, 128))
                parts.append(part.reshape(PY, 8, 128))
        s4[yp] = encode(jnp.concatenate(parts, axis=1), CENTRE_BACK)
        pltpu.make_async_copy(s4.at[yp, py], b4.at[py, yp], recv4.at[yp]).start()

        def send(step, inner):
            other = lax.rem(py + step, PY)
            pltpu.make_async_remote_copy(
                src_ref=s4.at[yp, other], dst_ref=b4.at[py, yp],
                send_sem=send4.at[yp], recv_sem=recv4.at[yp],
                device_id=(px, other), device_id_type=MESH,
            ).start()
            return inner

        return lax.fori_loop(1, PY, send, carry)

    lax.fori_loop(0, 4, z_backward, 0)
    info_copy.wait()
    loads[14].wait()
    pltpu.make_async_copy(brick_in, brick_in, brick_sem.at[5]).wait()

    def take(slot, carry):
        tile = brick_in[info_smem[slot, 1]].astype(F32)
        tile = pltpu.roll(tile, lax.rem(128 - BRICK * info_smem[slot, 2], 128), 1)
        tiles[pl.ds(pl.multiple_of(16 * slot, 16), 16), :] = tile.astype(BF16)
        return carry

    lax.fori_loop(0, 32, take, 0, unroll=4)
    cell = lax.broadcasted_iota(jnp.int32, (128, 512), 1)
    origin = lax.broadcasted_iota(jnp.int32, (128, 512), 0)
    spread = (origin == 32 * (cell // 128) + lax.rem(cell, BRICK)).astype(F32).astype(BF16)
    wide = dot(tiles[...], spread)
    tile_row = lax.broadcasted_iota(jnp.int32, (512, 512), 0)
    tile_cell = lax.broadcasted_iota(jnp.int32, (512, 512), 1)
    wide = jnp.where(lax.rem(tile_row, 16) == lax.rem(tile_cell, 128) // BRICK, wide, 0.0).astype(BF16)
    slot_down = lax.broadcasted_iota(jnp.int32, (32, 512), 0)
    slot_cell = lax.broadcasted_iota(jnp.int32, (32, 512), 1)
    samples[...] = dot((slot_down == slot_cell // 16).astype(F32).astype(BF16), wide)

    def embed(group, carry):
        for item in range(4):
            slot = 4 * group + item
            fragment = info_smem[slot, 0]
            weighted = turned_basis[fragment] * samples[pl.ds(slot, 1), :].astype(BF16)
            fock_out[slot] = fock_ref[slot] + dot(weighted, basis_ref[fragment]).T
        slots = pl.ds(4 * group, 4)
        pltpu.make_async_copy(fock_out.at[slots], fock_hbm_out.at[slots], fock_sem.at[group]).start()
        return carry

    lax.fori_loop(0, 8, embed, 0)

    def x_backward(yp, carry):
        chunk = b4.at[:, yp]
        pltpu.make_async_copy(chunk, chunk, recv4.at[yp]).wait()
        wide = []
        for j in range(PY):
            rows = decode(b4[j, yp], CENTRE_BACK)
            parts = []
            for u in range(2):
                three = [rows[24 * u + 8 * g:24 * u + 8 * g + 8] for g in range(3)]
                last = shift(three[0], -3)
                for f in range(1, 3):
                    last = jnp.where(lane_field == f, shift(three[f], f - 3), last)
                parts += three + [last]
            wide.append(jnp.concatenate(parts, axis=0))
        back = x_inverse(jnp.concatenate(wide, axis=1), SITES)
        slabs = pl.ds(2 * yp, 2)
        for f in range(SITES):
            corr_out[f, slabs] = back[64 * f:64 * f + 64].reshape(2, 32, N)
        pltpu.make_async_copy(corr_out.at[:, slabs], corr_hbm_out.at[:, slabs], corr_sem.at[yp]).start()
        return carry

    lax.fori_loop(0, 4, x_backward, 0)
    potential_copy.wait()
    for part in range(4):
        slabs = pl.ds(2 * part, 2)
        pltpu.make_async_copy(corr_out.at[:, slabs], corr_hbm_out.at[:, slabs], corr_sem.at[part]).wait()
    for part in range(8):
        slots = pl.ds(4 * part, 4)
        pltpu.make_async_copy(fock_out.at[slots], fock_hbm_out.at[slots], fock_sem.at[part]).wait()

    for part in range(4):
        sent = s1.at[pl.ds(0, PY - 1), pl.ds(0, 2)]
        pltpu.make_async_copy(sent, sent, send1.at[part]).wait()
        sent = s2.at[pl.ds(0, PX - 1), 0]
        pltpu.make_async_copy(sent, sent, send2.at[part]).wait()
        if part < 3:
            sent = s3.at[pl.ds(0, PX - 1), 0]
            pltpu.make_async_copy(sent, sent, send3.at[part]).wait()
        sent = s4.at[0, pl.ds(0, PY - 1)]
        pltpu.make_async_copy(sent, sent, send4.at[part]).wait()
    sent = s3p.at[pl.ds(0, PX - 1)]
    pltpu.make_async_copy(sent, sent, pot_sem.at[0]).wait()
    sent = s4p.at[:, pl.ds(0, 32 * (PY - 1))]
    pltpu.make_async_copy(sent, sent, pot_sem.at[2]).wait()
    sent = ask_out.at[pl.ds(0, PX - 1)]
    pltpu.make_async_copy(sent, sent, brick_sem.at[1]).wait()
    sent = brick_out.at[pl.ds(0, PX - 1)]
    pltpu.make_async_copy(sent, sent, brick_sem.at[4]).wait()


def shards(
    corr, solute_pot, chi, site_charge, home_slab, brick_index, block_slot, basis_values, fock_in
):
    hbm = pl.BlockSpec(memory_space=pltpu.HBM)
    dma = pltpu.SemaphoreType.DMA((4,))
    frags = home_slab.shape[0]
    return pl.pallas_call(
        field_kernel,
        name="fields",
        out_shape=(
            jax.ShapeDtypeStruct((SITES, 8, 32, N), F32),
            jax.ShapeDtypeStruct((8, 32, N), F32),
            jax.ShapeDtypeStruct(fock_in.shape, F32),
        ),
        in_specs=[pl.BlockSpec(memory_space=pltpu.SMEM)] + [hbm] * 18,
        out_specs=(hbm,) * 3,
        scratch_shapes=[
            pltpu.VMEM(corr.shape, F32),
            pltpu.VMEM(corr.shape[1:], F32),
            pltpu.VMEM(fock_in.shape, F32),
            pltpu.VMEM(corr.shape, F32),
            pltpu.VMEM(solute_pot.shape, BF16),
            pltpu.VMEM((SITES, SITES, R, 8, N), F32),
            pltpu.VMEM((SITES, SITES, 8, N), F32),
            pltpu.VMEM((1, frags), jnp.int32),
            pltpu.VMEM((1, frags), jnp.int32),
            pltpu.VMEM((1, frags), jnp.int32),
            pltpu.VMEM(basis_values.shape, BF16),
            pltpu.VMEM(fock_in.shape, F32),
            pltpu.VMEM((N, PY * 128), BF16),
            pltpu.VMEM((N, PY * 128), BF16),
        ] + [pltpu.VMEM((N, N), BF16)] * 8 + [
            pltpu.VMEM((PY, 8, 32, 128), WIRE),
            pltpu.VMEM((8, N, 128), WIRE),
            pltpu.VMEM((PX, 4, 16, 128), WIRE),
            pltpu.VMEM((PX, 4, 16, 128), WIRE),
            pltpu.VMEM((PX, 64, 128), F32),
            pltpu.VMEM((8, 128, N), F32),
            pltpu.VMEM((8, 128, N), F32),
            pltpu.VMEM((PX, 16, 128), WIRE),
            pltpu.VMEM((PX, 16, 128), WIRE),
            pltpu.VMEM((PX, 16, 128), F32),
            pltpu.VMEM((2, N, 128), WIRE),
            pltpu.VMEM((PY, 2, 32, 128), WIRE),
            pltpu.VMEM((PX, 3, 16, 128), WIRE),
            pltpu.VMEM((PX, 3, 16, 128), WIRE),
            pltpu.VMEM((PX, 48, 128), F32),
            pltpu.VMEM((4, PY, 48, 128), WIRE),
            pltpu.VMEM((PY, 4, 48, 128), WIRE),
            pltpu.VMEM((PX, 1, 128), jnp.int32),
            pltpu.VMEM((PX, 1, 128), jnp.int32),
            pltpu.SMEM((PX, 1, 128), jnp.int32),
            pltpu.VMEM((frags, 128), jnp.int32),
            pltpu.SMEM((frags, 128), jnp.int32),
            pltpu.VMEM((2, 8, 32, 128), F32),
            pltpu.VMEM((32, 16, 128), F32),
            pltpu.VMEM((PX, 16, 128), BF16),
            pltpu.VMEM((PX, 16, 128), BF16),
            pltpu.VMEM((frags, 128, 512), BF16),
            pltpu.VMEM((frags * 16, 128), BF16),
            pltpu.VMEM((frags, 512), F32),
            pltpu.SemaphoreType.DMA((19,)),
        ] + [dma] * 9 + [pltpu.SemaphoreType.DMA((6,)), dma, dma, pltpu.SemaphoreType.DMA((8,))],
        compiler_params=pltpu.CompilerParams(
            collective_id=0, has_side_effects=True, vmem_limit_bytes=60 * 2**20
        ),
    )(
        site_charge, corr, solute_pot, chi, home_slab.reshape(1, frags), brick_index.reshape(1, frags),
        block_slot, basis_values, fock_in, *[jnp.asarray(table) for table in tables()],
    )


def solution(mesh):
    return jax.shard_map(
        shards,
        mesh=mesh,
        in_specs=(
            P(None, "px", "py", None),
            P(None, "px", "py", None),
            P(None, None, None, "py", "px", None),
            P(),
            P(("px", "py"), None),
            P(("px", "py")),
            P(("px", "py"), None),
            P(("px", "py"), None, None),
            P(("px", "py"), None, None),
        ),
        out_specs=(P(None, "px", "py", None), P("px", "py", None), P(("px", "py"), None, None)),
        check_vma=False,
    )
```

```python
import functools
import jax
import jax.numpy as jnp
import numpy as np
from jax import lax
from jax.experimental import pallas as pl
from jax.experimental.pallas import tpu as pltpu
from jax.sharding import PartitionSpec as P

BRICK = 8
MOST = 4
N = 256
PX = 32
PY = 8
SITES = 3
FIELDS = 4
R = 16
MESH = pl.DeviceIdType.MESH
F32 = jnp.float32
BF16 = jnp.bfloat16
WIRE = jnp.bfloat16
FINE, STEEP, SLOPE = 11.0, 8.0, 3.0
CENTRE_X, CENTRE_Z, CENTRE_Y, CENTRE_BACK = 5.0, 9.0, -5.0, -1.0


def split(values):
    high = values.astype(BF16)
    return high, (values - high.astype(F32)).astype(BF16)


def np_split(values):
    high = values.astype(np.float32).astype(BF16)
    low = (values - high.astype(np.float64)).astype(np.float32).astype(BF16)
    return high, low


def tables():
    index = np.arange(N)
    angle = (index[:, None] * index[None, :] % N) * (2.0 * np.pi / N)
    cos, sin = np.cos(angle), np.sin(angle)
    half_re = cos[:, : N // 2].copy()
    half_im = -sin[:, : N // 2]
    half_im[:, 0] = cos[:, N // 2]
    halves = np.stack([half_re.reshape(N, PY, R), half_im.reshape(N, PY, R)], axis=2)
    spread = np.broadcast_to(halves[:, :, :, None, :], (N, PY, 2, FIELDS, R))
    spread = spread.reshape(N, PY * 128)
    order = index % PX * 8 + index // PX
    return np_split(spread) + np_split(cos) + np_split(sin) + np_split(cos[:, order]) + np_split(sin[:, order])


def encode(values, centre):
    power = jnp.log2(jnp.abs(values)) - centre
    power = SLOPE * power + (STEEP - SLOPE) * jnp.clip(power, -FINE, FINE)
    coded = jnp.exp2(power)
    return jnp.where(values < 0, -coded, coded).astype(WIRE)


def decode(coded, centre):
    coded = coded.astype(F32)
    power = jnp.log2(jnp.abs(coded))
    fine = jnp.clip(power, -FINE * STEEP, FINE * STEEP)
    values = jnp.exp2(power * (1.0 / SLOPE) + fine * (1.0 / STEEP - 1.0 / SLOPE) + centre)
    return jnp.where(coded < 0, -values, values)


def dot(left, right):
    return jnp.dot(left, right, preferred_element_type=F32)


def dot_nt(left, right):
    return lax.dot_general(left, right, (((1,), (1,)), ((), ())), preferred_element_type=F32)


def dot3(product, left, right):
    return product(left[0], right[0]) + product(left[0], right[1]) + product(left[1], right[0])


def closure(corr, solute_pot):
    excess = corr - solute_pot.astype(F32)
    low = jnp.minimum(excess, 0.0)
    series = jnp.full_like(low, 1.0 / 362880.0)
    for denominator in (40320.0, 5040.0, 720.0, 120.0, 24.0, 6.0, 2.0, 1.0):
        series = series * low + 1.0 / denominator
    grown = jnp.where(low > -0.5, series * low, jnp.exp(low) - 1.0)
    return jnp.where(excess > 0, excess, grown) - corr


def field_kernel(
    charge_ref, corr_hbm, solute_hbm, chi_hbm, home_hbm, brick_hbm, slot_hbm, basis_hbm, fock_hbm,
    xh_hbm, xl_hbm, ch_hbm, cl_hbm, sh_hbm, sl_hbm, och_hbm, ocl_hbm, osh_hbm, osl_hbm,
    corr_hbm_out, potential_hbm_out, fock_hbm_out,
    corr_out, potential_out, fock_out,
    corr_ref, solute_ref, chi0, chi1, home_ref, brick_ref, slot_ref, basis_ref, fock_ref,
    xh_ref, xl_ref, ch_ref, cl_ref, sh_ref, sl_ref, och_ref, ocl_ref, osh_ref, osl_ref,
    s1, b1, s2, b2, ys, plain_k, turned_k, s3p, b3p, ysp, s4p, b4p, s3, b3, yc, s4, b4, weights,
    ask_out, ask_in, ask_smem, info, info_smem, pot_ref, shuffled, brick_out, brick_in, turned_basis, tiles, samples,
    in_sem, send1, recv1, send2, recv2, send3, recv3, send4, recv4, pot_sem, brick_sem, corr_sem, potential_sem, fock_sem,
):
    px = lax.axis_index("px")
    py = lax.axis_index("py")
    barrier = pltpu.get_barrier_semaphore()

    def greet_px(step, carry):
        pl.semaphore_signal(barrier, inc=1, device_id=(lax.rem(px + step, PX), py), device_id_type=MESH)
        return carry

    def greet_py(step, carry):
        pl.semaphore_signal(barrier, inc=1, device_id=(px, lax.rem(py + step, PY)), device_id_type=MESH)
        return carry

    pairs = (
        (corr_hbm, corr_ref), (solute_hbm, solute_ref), (xh_hbm, xh_ref), (xl_hbm, xl_ref),
        (ch_hbm, ch_ref), (cl_hbm, cl_ref), (sh_hbm, sh_ref), (sl_hbm, sl_ref),
        (home_hbm, home_ref), (brick_hbm, brick_ref), (slot_hbm, slot_ref),
        (chi_hbm.at[:, :, 0], chi0), (chi_hbm.at[:, :, 1, 0], chi1),
        (basis_hbm, basis_ref), (fock_hbm, fock_ref),
        (och_hbm, och_ref), (ocl_hbm, ocl_ref), (osh_hbm, osh_ref), (osl_hbm, osl_ref),
    )
    loads = [pltpu.make_async_copy(source, to, in_sem.at[i]) for i, (source, to) in enumerate(pairs)]
    for load in loads[:11]:
        load.start()
    lax.fori_loop(1, PX, greet_px, 0)
    lax.fori_loop(1, PY, greet_py, 0)
    for load in loads[11:]:
        load.start()
    for load in loads[:4]:
        load.wait()

    lane = lax.broadcasted_iota(jnp.int32, (1, 128), 1)
    lane_re = lane < 64
    lane_field = lax.rem(lane // R, FIELDS)
    lane_spec = (lax.rem(lane, R) == 0) & (py == 0)

    lane_site = jnp.concatenate([lane_field, lane_field], axis=1)

    def x_forward(yp, carry):
        parts = []
        for site in range(SITES):
            rows = closure(corr_ref[site, pl.ds(2 * yp, 2)], solute_ref[site, pl.ds(2 * yp, 2)])
            parts.append(rows.reshape(64, N))
        data = split(jnp.concatenate(parts, axis=0))
        for pair in range(PY // 2):
            wide = dot3(dot, data, (xh_ref[:, 256 * pair:256 * pair + 256], xl_ref[:, 256 * pair:256 * pair + 256]))
            rows = jnp.where(lane_site == 0, wide[0:64], jnp.where(lane_site == 1, wide[64:128], wide[128:192]))
            rows = encode(jnp.where(lane_site == 3, 0.0, rows), CENTRE_X)
            s1[2 * pair, pl.ds(2 * yp, 2)] = rows[:, 0:128].reshape(2, 32, 128)
            s1[2 * pair + 1, pl.ds(2 * yp, 2)] = rows[:, 128:256].reshape(2, 32, 128)

        @pl.when(yp == 0)
        def _():
            pl.semaphore_wait(barrier, PX + PY - 2)

        pltpu.make_async_copy(
            s1.at[py, pl.ds(2 * yp, 2)], b1.at[pl.ds(2 * yp, 2), pl.ds(32 * py, 32)], recv1.at[yp]
        ).start()

        def send(step, inner):
            other = lax.rem(py + step, PY)
            pltpu.make_async_remote_copy(
                src_ref=s1.at[other, pl.ds(2 * yp, 2)],
                dst_ref=b1.at[pl.ds(2 * yp, 2), pl.ds(32 * py, 32)],
                send_sem=send1.at[yp], recv_sem=recv1.at[yp],
                device_id=(px, other), device_id_type=MESH,
            ).start()
            return inner

        return lax.fori_loop(1, PY, send, carry)

    lax.fori_loop(0, 4, x_forward, 0)

    for load in loads[8:11]:
        load.wait()
    home = home_ref[...]
    brick = brick_ref[...]
    down = lax.broadcasted_iota(jnp.int32, (32, 32), 0)
    across = lax.broadcasted_iota(jnp.int32, (32, 32), 1)
    home_down = jnp.sum(jnp.where(down == across, home, 0), axis=1, keepdims=True)
    place = jnp.sum(jnp.where((home_down == home) & (down < across), 1, 0), axis=0, keepdims=True)
    wide_lane = lax.broadcasted_iota(jnp.int32, (32, 128), 1)
    asked = jnp.zeros((32, 128), jnp.int32)
    for k in range(MOST):
        found = jnp.sum(jnp.where((home == down) & (place == k), brick, 0), axis=1, keepdims=True)
        asked = jnp.where(wide_lane == k, jnp.clip(found, 0, 127), asked)
    for other in range(PX):
        ask_out[other] = asked[other:other + 1]
    table = jnp.zeros((32, 128), jnp.int32)
    for k, (value, most) in enumerate(((across, 31), (home, PX - 1), (place, MOST - 1))):
        found = jnp.sum(jnp.where(slot_ref[...] == down, value, 0), axis=1, keepdims=True)
        table = jnp.where(wide_lane == k, jnp.clip(found, 0, most), table)
    info[...] = table
    info_copy = pltpu.make_async_copy(info, info_smem, brick_sem.at[0])
    info_copy.start()
    pltpu.make_async_copy(ask_out.at[px], ask_in.at[px], brick_sem.at[2]).start()

    def ask(step, carry):
        other = lax.rem(px + step, PX)
        pltpu.make_async_remote_copy(
            src_ref=ask_out.at[other], dst_ref=ask_in.at[px],
            send_sem=brick_sem.at[1], recv_sem=brick_sem.at[2],
            device_id=(other, py), device_id_type=MESH,
        ).start()
        return carry

    lax.fori_loop(1, PX, ask, 0)
    for load in loads[4:8]:
        load.wait()

    cos = (ch_ref[...], cl_ref[...])
    sin = (sh_ref[...], sl_ref[...])
    wave = lax.broadcasted_iota(jnp.int32, (N, 1), 0)
    wave_edge = (wave == 0) | (wave == N // 2)
    wave_low = wave < N // 2
    wave_high = wave > N // 2

    def z_forward(yp, carry):
        chunk = b1.at[pl.ds(2 * yp, 2)]
        pltpu.make_async_copy(chunk, chunk, recv1.at[yp]).wait()
        data = split(jnp.concatenate([decode(b1[2 * yp + u], CENTRE_X) for u in range(2)], axis=1))
        cos_data = dot3(dot, cos, data)
        sin_data = dot3(dot, sin, data)
        halves = []
        for u in range(2):
            cd = cos_data[:, 128 * u:128 * u + 128]
            sd = sin_data[:, 128 * u:128 * u + 128]
            cd_turn = pltpu.roll(cd, 64, 1)
            sd_turn = pltpu.roll(sd, 64, 1)
            usual = jnp.where(lane_re, cd + sd_turn, cd - sd_turn)
            packed_re = jnp.where(wave_high, cd_turn, cd)
            packed_im = jnp.where(wave_edge, cd, jnp.where(wave_low, -sd_turn, -sd))
            packed = jnp.where(lane_re, packed_re, packed_im)
            halves.append(jnp.where(lane_spec, packed, usual).reshape(PX, 8, 128))
        s2[:, yp] = encode(jnp.concatenate(halves, axis=1), CENTRE_Z)
        pltpu.make_async_copy(s2.at[px, yp], b2.at[px, yp], recv2.at[yp]).start()

        def send(step, inner):
            other = lax.rem(px + step, PX)
            pltpu.make_async_remote_copy(
                src_ref=s2.at[other, yp], dst_ref=b2.at[px, yp],
                send_sem=send2.at[yp], recv_sem=recv2.at[yp],
                device_id=(other, py), device_id_type=MESH,
            ).start()
            return inner

        return lax.fori_loop(1, PX, send, carry)

    lax.fori_loop(0, 4, z_forward, 0)

    def collect(buffer, sem, centre, ys, parts):
        def body(part, carry):
            chunk = buffer.at[:, part]
            pltpu.make_async_copy(chunk, chunk, sem.at[part]).wait()

            def place(group, inner):
                sources = pl.ds(8 * group, 8)
                ys[sources, pl.ds(pl.multiple_of(16 * part, 16), 16), :] = decode(buffer[sources, part], centre)
                return inner

            return lax.fori_loop(0, PX // 8, place, carry)

        lax.fori_loop(0, parts, body, 0)

    pencils = ys.reshape(PX * 64, 128)

    def turn_basis(item, carry):
        turned_basis[item] = basis_ref[item].T
        return carry

    loads[13].wait()
    lax.fori_loop(0, 32, turn_basis, 0)
    collect(b2, recv2, CENTRE_Z, ys, 4)
    loads[11].wait()
    loads[12].wait()

    row = lax.broadcasted_iota(jnp.int32, (R, 1), 0)
    first = (row == 0) & (py == 0)
    wave_y = lax.broadcasted_iota(jnp.int32, (1, N), 1)
    unit = 2.0 * np.pi / N

    def signed_square(index):
        shifted = (lax.rem(index + N // 2, N) - N // 2).astype(F32) * unit
        return shifted * shifted

    square_y = signed_square(wave_y)
    scale = jnp.where(first, 2.0 ** -24, 2.0 ** -23)

    def mix(chi_of, x_re, x_im, screened):
        out_re, out_im = [], []
        pot_re = pot_im = 0.0
        for a in range(SITES):
            t_re = t_im = 0.0
            for b in range(SITES):
                factor = chi_of(a, b)
                t_re = t_re + factor * x_re[b]
                t_im = t_im + factor * x_im[b]
            out_re.append((t_re - x_re[a]) * scale)
            out_im.append((t_im - x_im[a]) * scale)
            pot_re = pot_re + charge_ref[a] * t_re
            pot_im = pot_im + charge_ref[a] * t_im
        out_re.append(pot_re * (screened * scale))
        out_im.append(pot_im * (screened * scale))
        return out_re, out_im

    def y_forward(quad, carry):
        for pair in range(2):
            rows = jnp.concatenate(
                [pencils[pl.ds(4 * quad + 2 * pair + u, N, stride=8), :].T for u in range(2)], axis=0
            )
            data = split(rows)
            cos_data = dot3(dot, data, cos)
            sin_data = dot3(dot, data, sin)
            for u in range(2):
                k = 2 * pair + u
                kz = 4 * quad + k
                kz_all = px * 8 + kz
                base = 128 * u
                pick = lambda array, c, s: array[base + 64 * c + 16 * s:base + 64 * c + 16 * s + 16]
                c_re = [pick(cos_data, 0, s) for s in range(SITES)]
                c_im = [pick(cos_data, 1, s) for s in range(SITES)]
                s_re = [pick(sin_data, 0, s) for s in range(SITES)]
                s_im = [pick(sin_data, 1, s) for s in range(SITES)]
                x_re = [c_re[s] + s_im[s] for s in range(SITES)]
                x_im = [c_im[s] - s_re[s] for s in range(SITES)]
                upper = first & (kz_all > N // 2)
                kx = jnp.where(upper, N // 2, py * R + row)
                square_z = signed_square(jnp.full((1, 1), kz_all, jnp.int32))
                rest = square_z + square_y + 1.0
                screened = (4.0 * np.pi) / (signed_square(kx) + rest)
                chi_of = lambda a, b: jnp.where(upper, chi1[a, b, pl.ds(kz, 1), :], chi0[a, b, :, kz, :])
                if k == 0:
                    edge = first & ((kz_all == 0) | (kz_all == N // 2))
                    b_re = [c_im[s] for s in range(SITES)]
                    b_im = [-s_im[s] for s in range(SITES)]
                    x_re = [jnp.where(edge, c_re[s], x_re[s]) for s in range(SITES)]
                    x_im = [jnp.where(edge, -s_re[s], x_im[s]) for s in range(SITES)]
                    f_re, f_im = mix(chi_of, x_re, x_im, screened)
                    screened = (4.0 * np.pi) / (np.pi ** 2 + rest)
                    g_re, g_im = mix(lambda a, b: chi1[a, b, pl.ds(kz, 1), :], b_re, b_im, screened)
                    other_plain = [jnp.where(edge, g_re[f], f_im[f]) for f in range(FIELDS)]
                    other_turned = [jnp.where(edge, -g_im[f], f_re[f]) for f in range(FIELDS)]
                else:
                    f_re, f_im = mix(chi_of, x_re, x_im, screened)
                    other_plain, other_turned = f_im, f_re
                for f in range(FIELDS):
                    if f == SITES:
                        group, slot = 6 + quad, k
                    elif k < 3:
                        group, slot = 3 * quad + k, f
                    else:
                        group, slot = 3 * quad + f, 3
                    plain_k[group, pl.ds(16 * slot, 16), :] = f_re[f]
                    plain_k[group, pl.ds(64 + 16 * slot, 16), :] = other_plain[f]
                    turned_k[group, pl.ds(16 * slot, 16), :] = -f_im[f]
                    turned_k[group, pl.ds(64 + 16 * slot, 16), :] = other_turned[f]
        return carry

    lax.fori_loop(0, 2, y_forward, 0)

    def y_backward(unit):
        groups = pl.ds(2 * unit, 2)
        plain = split(plain_k[groups].reshape(256, N))
        turned = split(turned_k[groups].reshape(256, N))
        back = dot3(dot_nt, cos, plain) + dot3(dot_nt, sin, turned)
        return encode(
            jnp.concatenate([back[:, 128 * u:128 * u + 128].reshape(PX, 8, 128) for u in range(2)], axis=1),
            CENTRE_Y,
        )

    s3p[...] = y_backward(3)
    pltpu.make_async_copy(s3p.at[px], b3p.at[px], pot_sem.at[1]).start()

    def send_potential(step, carry):
        other = lax.rem(px + step, PX)
        pltpu.make_async_remote_copy(
            src_ref=s3p.at[other], dst_ref=b3p.at[px],
            send_sem=pot_sem.at[0], recv_sem=pot_sem.at[1],
            device_id=(other, py), device_id_type=MESH,
        ).start()
        return carry

    lax.fori_loop(1, PX, send_potential, 0)

    def y_corr(unit, carry):
        s3[:, unit] = y_backward(unit)
        pltpu.make_async_copy(s3.at[px, unit], b3.at[px, unit], recv3.at[unit]).start()

        def send(step, inner):
            other = lax.rem(px + step, PX)
            pltpu.make_async_remote_copy(
                src_ref=s3.at[other, unit], dst_ref=b3.at[px, unit],
                send_sem=send3.at[unit], recv_sem=recv3.at[unit],
                device_id=(other, py), device_id_type=MESH,
            ).start()
            return inner

        return lax.fori_loop(1, PX, send, carry)

    lax.fori_loop(0, 3, y_corr, 0)

    for load in loads[15:19]:
        load.wait()
    cos_order = (och_ref[...], ocl_ref[...])
    sin_order = (osh_ref[...], osl_ref[...])
    order = lax.rem(wave, PX) * 8 + wave // PX
    order_edge = (order == 0) | (order == N // 2)
    order_low = order < N // 2
    order_high = order > N // 2

    zero, one, two = jnp.zeros((N, 128), F32), jnp.ones((N, 128), F32), jnp.full((N, 128), 2.0, F32)
    packed_re = jnp.where(order_edge, one, jnp.where(order_low, two, zero))
    packed_im = jnp.where(order_edge, one, zero)
    weights[0] = jnp.where(lane_spec, jnp.where(lane_re, packed_re, packed_im), one)
    weights[1] = jnp.where(lane_spec & ~lane_re & order_high, two, zero)
    weights[2] = jnp.where(lane_spec & ~lane_re & order_high, -two, zero)
    usual = jnp.where(lane_re, -one, one)
    weights[3] = jnp.where(lane_spec, jnp.where(lane_re & order_low & ~order_edge, -two, zero), usual)

    def z_inverse(columns):
        plain, turned = [], []
        for data in columns:
            turn = pltpu.roll(data, 64, 1)
            plain.append(data * weights[0] + turn * weights[1])
            turned.append(data * weights[2] + turn * weights[3])
        plain = split(jnp.concatenate(plain, axis=1))
        turned = split(jnp.concatenate(turned, axis=1))
        return dot3(dot, cos_order, plain) + dot3(dot, sin_order, turned)

    def shift(data, slots):
        return pltpu.roll(data, 16 * slots % 128, 1) if slots else data

    def x_inverse(rows, count):
        field = jnp.concatenate([lane_field] * PY, axis=1)
        data = split(jnp.concatenate([jnp.where(field == f, rows, 0.0) for f in range(count)], axis=0))
        return dot3(dot_nt, data, (xh_ref[...], xl_ref[...]))

    pltpu.make_async_copy(b3p, b3p, pot_sem.at[1]).wait()
    ysp[...] = decode(b3p[...], CENTRE_Y)
    tiles_in = ysp.reshape(PX * 16, 128)
    columns = []
    for yq in range(2):
        parts = []
        for quad in range(2):
            rows = [tiles_in[pl.ds(8 * quad + 4 * yq + j, PX, stride=16), :] for j in range(4)]
            for k in range(4):
                part = shift(rows[0], -k)
                for j in range(1, 4):
                    part = jnp.where(lane_field == j, shift(rows[j], j - k), part)
                parts.append(part)
        columns.append(jnp.concatenate(parts, axis=0))
    back = encode(z_inverse(columns), CENTRE_BACK)
    s4p[0] = back[:, 0:128]
    s4p[1] = back[:, 128:256]
    pltpu.make_async_copy(s4p.at[:, pl.ds(32 * py, 32)], b4p.at[py], pot_sem.at[3]).start()

    def send_rows(step, carry):
        other = lax.rem(py + step, PY)
        pltpu.make_async_remote_copy(
            src_ref=s4p.at[:, pl.ds(32 * other, 32)], dst_ref=b4p.at[py],
            send_sem=pot_sem.at[2], recv_sem=pot_sem.at[3],
            device_id=(px, other), device_id_type=MESH,
        ).start()
        return carry

    lax.fori_loop(1, PY, send_rows, 0)
    pltpu.make_async_copy(b4p, b4p, pot_sem.at[3]).wait()
    back = x_inverse(
        jnp.concatenate([decode(b4p[j], CENTRE_BACK).reshape(64, 128) for j in range(PY)], axis=1), FIELDS
    )
    for y in range(8):
        start = 64 * (y % 4) + 32 * (y // 4)
        slab = back[start:start + 32]
        potential_out[y] = slab
        pot_ref[0, y] = slab[:, 0:128]
        pot_ref[1, y] = slab[:, 128:256]
    potential_copy = pltpu.make_async_copy(potential_out, potential_hbm_out, potential_sem.at[0])
    potential_copy.start()

    pltpu.make_async_copy(ask_in, ask_in, brick_sem.at[2]).wait()
    ask_copy = pltpu.make_async_copy(ask_in, ask_smem, brick_sem.at[3])
    ask_copy.start()
    lane_row = lane // 32

    def shuffle(bz, carry):
        for half in range(2):
            slabs = [pot_ref[half, y, pl.ds(8 * bz, 8), :] for y in range(8)]
            for quad in range(4):
                rows = []
                for u in range(2):
                    row = slabs[u]
                    if quad:
                        row = pltpu.roll(row, 128 - 32 * quad, 1)
                    for yg in range(1, 4):
                        move = 32 * ((yg - quad) % 4)
                        other = slabs[2 * yg + u]
                        other = pltpu.roll(other, move, 1) if move else other
                        row = jnp.where(lane_row == yg, other, row)
                    rows.append(row)
                shuffled[8 * bz + 4 * half + quad] = jnp.concatenate(rows, axis=0)
        return carry

    lax.fori_loop(0, 4, shuffle, 0)
    ask_copy.wait()
    lane_place = lax.rem(lane // BRICK, MOST)

    def answer(step, carry):
        other = lax.rem(px + step, PX)
        tile = jnp.zeros((16, 128), F32)
        for k in range(MOST):
            index = ask_smem[other, 0, k]
            moved = pltpu.roll(shuffled[index // 4], lax.rem(BRICK * (k - lax.rem(index, 4)) + 128, 128), 1)
            tile = jnp.where(lane_place == k, moved, tile)
        brick_out[other] = tile.astype(BF16)

        @pl.when(step > 0)
        def _():
            pltpu.make_async_remote_copy(
                src_ref=brick_out.at[other], dst_ref=brick_in.at[px],
                send_sem=brick_sem.at[4], recv_sem=brick_sem.at[5],
                device_id=(other, py), device_id_type=MESH,
            ).start()

        return carry

    lax.fori_loop(0, PX, answer, 0, unroll=4)
    pltpu.make_async_copy(brick_out.at[px], brick_in.at[px], brick_sem.at[5]).start()

    collect(b3, recv3, CENTRE_Y, yc, 3)
    packed = yc.reshape(PX * 48, 128)

    def z_backward(yp, carry):
        columns = []
        for u in range(2):
            parts = []
            for quad in range(2):
                rows = [packed[pl.ds(24 * quad + 8 * g + 2 * yp + u, PX, stride=48), :] for g in range(3)]
                last = shift(rows[0], -3)
                for f in range(1, 3):
                    last = jnp.where(lane_field == f, shift(rows[f], f - 3), last)
                parts += rows + [last]
            columns.append(jnp.concatenate(parts, axis=0))
        back = z_inverse(columns)
        parts = []
        for u in range(2):
            rows = back[:, 128 * u:128 * u + 128].reshape(PY, 4, 8, 128)
            last = rows[:, 3].reshape(64, 128)
            for g in range(3):
                part = jnp.where(lane_field == 3, shift(last, 3 - g), rows[:, g].reshape(64, 128))
                parts.append(part.reshape(PY, 8, 128))
        s4[yp] = encode(jnp.concatenate(parts, axis=1), CENTRE_BACK)
        pltpu.make_async_copy(s4.at[yp, py], b4.at[py, yp], recv4.at[yp]).start()

        def send(step, inner):
            other = lax.rem(py + step, PY)
            pltpu.make_async_remote_copy(
                src_ref=s4.at[yp, other], dst_ref=b4.at[py, yp],
                send_sem=send4.at[yp], recv_sem=recv4.at[yp],
                device_id=(px, other), device_id_type=MESH,
            ).start()
            return inner

        return lax.fori_loop(1, PY, send, carry)

    lax.fori_loop(0, 4, z_backward, 0)
    info_copy.wait()
    loads[14].wait()
    pltpu.make_async_copy(brick_in, brick_in, brick_sem.at[5]).wait()

    def take(slot, carry):
        tile = brick_in[info_smem[slot, 1]].astype(F32)
        tile = pltpu.roll(tile, lax.rem(128 - BRICK * info_smem[slot, 2], 128), 1)
        tiles[pl.ds(pl.multiple_of(16 * slot, 16), 16), :] = tile.astype(BF16)
        return carry

    lax.fori_loop(0, 32, take, 0, unroll=8)
    cell = lax.broadcasted_iota(jnp.int32, (128, 512), 1)
    origin = lax.broadcasted_iota(jnp.int32, (128, 512), 0)
    spread = (origin == 32 * (cell // 128) + lax.rem(cell, BRICK)).astype(F32).astype(BF16)
    wide = dot(tiles[...], spread)
    tile_row = lax.broadcasted_iota(jnp.int32, (512, 512), 0)
    tile_cell = lax.broadcasted_iota(jnp.int32, (512, 512), 1)
    wide = jnp.where(lax.rem(tile_row, 16) == lax.rem(tile_cell, 128) // BRICK, wide, 0.0).astype(BF16)
    slot_down = lax.broadcasted_iota(jnp.int32, (32, 512), 0)
    slot_cell = lax.broadcasted_iota(jnp.int32, (32, 512), 1)
    samples[...] = dot((slot_down == slot_cell // 16).astype(F32).astype(BF16), wide)

    def embed(group, carry):
        for item in range(4):
            slot = 4 * group + item
            fragment = info_smem[slot, 0]
            weighted = turned_basis[fragment] * samples[pl.ds(slot, 1), :].astype(BF16)
            fock_out[slot] = fock_ref[slot] + dot(weighted, basis_ref[fragment]).T
        slots = pl.ds(4 * group, 4)
        pltpu.make_async_copy(fock_out.at[slots], fock_hbm_out.at[slots], fock_sem.at[group]).start()
        return carry

    lax.fori_loop(0, 8, embed, 0)

    def x_backward(yp, carry):
        chunk = b4.at[:, yp]
        pltpu.make_async_copy(chunk, chunk, recv4.at[yp]).wait()
        wide = []
        for j in range(PY):
            rows = decode(b4[j, yp], CENTRE_BACK)
            parts = []
            for u in range(2):
                three = [rows[24 * u + 8 * g:24 * u + 8 * g + 8] for g in range(3)]
                last = shift(three[0], -3)
                for f in range(1, 3):
                    last = jnp.where(lane_field == f, shift(three[f], f - 3), last)
                parts += three + [last]
            wide.append(jnp.concatenate(parts, axis=0))
        back = x_inverse(jnp.concatenate(wide, axis=1), SITES)
        slabs = pl.ds(2 * yp, 2)
        for f in range(SITES):
            corr_out[f, slabs] = back[64 * f:64 * f + 64].reshape(2, 32, N)
        pltpu.make_async_copy(corr_out.at[:, slabs], corr_hbm_out.at[:, slabs], corr_sem.at[yp]).start()
        return carry

    lax.fori_loop(0, 4, x_backward, 0)
    potential_copy.wait()
    for part in range(4):
        slabs = pl.ds(2 * part, 2)
        pltpu.make_async_copy(corr_out.at[:, slabs], corr_hbm_out.at[:, slabs], corr_sem.at[part]).wait()
    for part in range(8):
        slots = pl.ds(4 * part, 4)
        pltpu.make_async_copy(fock_out.at[slots], fock_hbm_out.at[slots], fock_sem.at[part]).wait()

    for part in range(4):
        sent = s1.at[pl.ds(0, PY - 1), pl.ds(0, 2)]
        pltpu.make_async_copy(sent, sent, send1.at[part]).wait()
        sent = s2.at[pl.ds(0, PX - 1), 0]
        pltpu.make_async_copy(sent, sent, send2.at[part]).wait()
        if part < 3:
            sent = s3.at[pl.ds(0, PX - 1), 0]
            pltpu.make_async_copy(sent, sent, send3.at[part]).wait()
        sent = s4.at[0, pl.ds(0, PY - 1)]
        pltpu.make_async_copy(sent, sent, send4.at[part]).wait()
    sent = s3p.at[pl.ds(0, PX - 1)]
    pltpu.make_async_copy(sent, sent, pot_sem.at[0]).wait()
    sent = s4p.at[:, pl.ds(0, 32 * (PY - 1))]
    pltpu.make_async_copy(sent, sent, pot_sem.at[2]).wait()
    sent = ask_out.at[pl.ds(0, PX - 1)]
    pltpu.make_async_copy(sent, sent, brick_sem.at[1]).wait()
    sent = brick_out.at[pl.ds(0, PX - 1)]
    pltpu.make_async_copy(sent, sent, brick_sem.at[4]).wait()


def store_kernel(*refs):
    sources, targets, held, in_sem, out_sem = refs[:3], refs[3:6], refs[6:9], refs[9], refs[10]
    loads, stores = [], []
    for i in range(3):
        count = (3, 1, 8)[i]
        step = sources[i].shape[0] // count
        for part in range(count):
            rows = pl.ds(part * step, step)
            sem = len(loads)
            loads.append(pltpu.make_async_copy(sources[i].at[rows], held[i].at[rows], in_sem.at[sem]))
            stores.append(pltpu.make_async_copy(held[i].at[rows], targets[i].at[rows], out_sem.at[sem]))
    for load in loads:
        load.start()
    for load, store in zip(loads, stores):
        load.wait()
        store.start()
    for store in stores:
        store.wait()


def shards(
    corr, solute_pot, chi, site_charge, home_slab, brick_index, block_slot, basis_values, fock_in
):
    hbm = pl.BlockSpec(memory_space=pltpu.HBM)
    dma = pltpu.SemaphoreType.DMA((4,))
    frags = home_slab.shape[0]
    results = pl.pallas_call(
        field_kernel,
        name="fields",
        out_shape=(
            jax.ShapeDtypeStruct((SITES, 8, 32, N), F32),
            jax.ShapeDtypeStruct((8, 32, N), F32),
            jax.ShapeDtypeStruct(fock_in.shape, F32),
        ),
        in_specs=[pl.BlockSpec(memory_space=pltpu.SMEM)] + [hbm] * 18,
        out_specs=(hbm,) * 3,
        scratch_shapes=[
            pltpu.VMEM(corr.shape, F32),
            pltpu.VMEM(corr.shape[1:], F32),
            pltpu.VMEM(fock_in.shape, F32),
            pltpu.VMEM(corr.shape, F32),
            pltpu.VMEM(solute_pot.shape, BF16),
            pltpu.VMEM((SITES, SITES, R, 8, N), F32),
            pltpu.VMEM((SITES, SITES, 8, N), F32),
            pltpu.VMEM((1, frags), jnp.int32),
            pltpu.VMEM((1, frags), jnp.int32),
            pltpu.VMEM((1, frags), jnp.int32),
            pltpu.VMEM(basis_values.shape, BF16),
            pltpu.VMEM(fock_in.shape, F32),
            pltpu.VMEM((N, PY * 128), BF16),
            pltpu.VMEM((N, PY * 128), BF16),
        ] + [pltpu.VMEM((N, N), BF16)] * 8 + [
            pltpu.VMEM((PY, 8, 32, 128), WIRE),
            pltpu.VMEM((8, N, 128), WIRE),
            pltpu.VMEM((PX, 4, 16, 128), WIRE),
            pltpu.VMEM((PX, 4, 16, 128), WIRE),
            pltpu.VMEM((PX, 64, 128), F32),
            pltpu.VMEM((8, 128, N), F32),
            pltpu.VMEM((8, 128, N), F32),
            pltpu.VMEM((PX, 16, 128), WIRE),
            pltpu.VMEM((PX, 16, 128), WIRE),
            pltpu.VMEM((PX, 16, 128), F32),
            pltpu.VMEM((2, N, 128), WIRE),
            pltpu.VMEM((PY, 2, 32, 128), WIRE),
            pltpu.VMEM((PX, 3, 16, 128), WIRE),
            pltpu.VMEM((PX, 3, 16, 128), WIRE),
            pltpu.VMEM((PX, 48, 128), F32),
            pltpu.VMEM((4, PY, 48, 128), WIRE),
            pltpu.VMEM((PY, 4, 48, 128), WIRE),
            pltpu.VMEM((4, N, 128), F32),
            pltpu.VMEM((PX, 1, 128), jnp.int32),
            pltpu.VMEM((PX, 1, 128), jnp.int32),
            pltpu.SMEM((PX, 1, 128), jnp.int32),
            pltpu.VMEM((frags, 128), jnp.int32),
            pltpu.SMEM((frags, 128), jnp.int32),
            pltpu.VMEM((2, 8, 32, 128), F32),
            pltpu.VMEM((32, 16, 128), F32),
            pltpu.VMEM((PX, 16, 128), BF16),
            pltpu.VMEM((PX, 16, 128), BF16),
            pltpu.VMEM((frags, 128, 512), BF16),
            pltpu.VMEM((frags * 16, 128), BF16),
            pltpu.VMEM((frags, 512), F32),
            pltpu.SemaphoreType.DMA((19,)),
        ] + [dma] * 9 + [pltpu.SemaphoreType.DMA((6,)), dma, dma, pltpu.SemaphoreType.DMA((8,))],
        compiler_params=pltpu.CompilerParams(
            collective_id=0, has_side_effects=True, vmem_limit_bytes=60 * 2**20
        ),
    )(
        site_charge, corr, solute_pot, chi, home_slab.reshape(1, frags), brick_index.reshape(1, frags),
        block_slot, basis_values, fock_in, *[jnp.asarray(table) for table in tables()],
    )
    shapes = [jax.ShapeDtypeStruct(result.shape, F32) for result in results]
    return pl.pallas_call(
        store_kernel,
        name="store",
        out_shape=tuple(shapes),
        in_specs=[hbm] * 3,
        out_specs=(hbm,) * 3,
        scratch_shapes=[pltpu.VMEM(shape.shape, F32) for shape in shapes] + [pltpu.SemaphoreType.DMA((12,))] * 2,
        compiler_params=pltpu.CompilerParams(vmem_limit_bytes=60 * 2**20),
    )(*results)


def solution(mesh):
    return jax.shard_map(
        shards,
        mesh=mesh,
        in_specs=(
            P(None, "px", "py", None),
            P(None, "px", "py", None),
            P(None, None, None, "py", "px", None),
            P(),
            P(("px", "py"), None),
            P(("px", "py")),
            P(("px", "py"), None),
            P(("px", "py"), None, None),
            P(("px", "py"), None, None),
        ),
        out_specs=(P(None, "px", "py", None), P("px", "py", None), P(("px", "py"), None, None)),
        check_vma=False,
    )
```

```python
import functools
import jax
import jax.numpy as jnp
import numpy as np
from jax import lax
from jax.experimental import pallas as pl
from jax.experimental.pallas import tpu as pltpu
from jax.sharding import PartitionSpec as P

BRICK = 8
MOST = 4
N = 256
PX = 32
PY = 8
SITES = 3
FIELDS = 4
R = 16
MESH = pl.DeviceIdType.MESH
F32 = jnp.float32
BF16 = jnp.bfloat16
WIRE = jnp.bfloat16
FINE, STEEP, SLOPE = 11.0, 8.0, 3.0
CENTRE_X, CENTRE_Z, CENTRE_Y, CENTRE_BACK = 5.0, 9.0, -5.0, -1.0


def split(values):
    high = values.astype(BF16)
    return high, (values - high.astype(F32)).astype(BF16)


def np_split(values):
    high = values.astype(np.float32).astype(BF16)
    low = (values - high.astype(np.float64)).astype(np.float32).astype(BF16)
    return high, low


def tables():
    index = np.arange(N)
    angle = (index[:, None] * index[None, :] % N) * (2.0 * np.pi / N)
    cos, sin = np.cos(angle), np.sin(angle)
    half_re = cos[:, : N // 2].copy()
    half_im = -sin[:, : N // 2]
    half_im[:, 0] = cos[:, N // 2]
    halves = np.stack([half_re.reshape(N, PY, R), half_im.reshape(N, PY, R)], axis=2)
    spread = np.broadcast_to(halves[:, :, :, None, :], (N, PY, 2, FIELDS, R))
    spread = spread.reshape(N, PY * 128)
    order = index % PX * 8 + index // PX
    return np_split(spread) + np_split(cos) + np_split(sin) + np_split(cos[:, order]) + np_split(sin[:, order])


def encode(values, centre):
    power = jnp.log2(jnp.abs(values)) - centre
    power = SLOPE * power + (STEEP - SLOPE) * jnp.clip(power, -FINE, FINE)
    coded = jnp.exp2(power)
    return jnp.where(values < 0, -coded, coded).astype(WIRE)


def decode(coded, centre):
    coded = coded.astype(F32)
    power = jnp.log2(jnp.abs(coded))
    fine = jnp.clip(power, -FINE * STEEP, FINE * STEEP)
    values = jnp.exp2(power * (1.0 / SLOPE) + fine * (1.0 / STEEP - 1.0 / SLOPE) + centre)
    return jnp.where(coded < 0, -values, values)


def dot(left, right):
    return jnp.dot(left, right, preferred_element_type=F32)


def dot_nt(left, right):
    return lax.dot_general(left, right, (((1,), (1,)), ((), ())), preferred_element_type=F32)


def dot3(product, left, right):
    return product(left[0], right[0]) + product(left[0], right[1]) + product(left[1], right[0])


def closure(corr, solute_pot):
    excess = corr - solute_pot.astype(F32)
    low = jnp.minimum(excess, 0.0)
    series = jnp.full_like(low, 1.0 / 362880.0)
    for denominator in (40320.0, 5040.0, 720.0, 120.0, 24.0, 6.0, 2.0, 1.0):
        series = series * low + 1.0 / denominator
    grown = jnp.where(low > -0.5, series * low, jnp.exp(low) - 1.0)
    return jnp.where(excess > 0, excess, grown) - corr


def field_kernel(
    charge_ref, corr_hbm, solute_hbm, chi_hbm, home_hbm, brick_hbm, slot_hbm, basis_hbm, fock_hbm,
    xh_hbm, xl_hbm, ch_hbm, cl_hbm, sh_hbm, sl_hbm, och_hbm, ocl_hbm, osh_hbm, osl_hbm,
    corr_hbm_out, potential_hbm_out, fock_hbm_out,
    corr_out, potential_out, fock_out,
    corr_ref, solute_ref, chi0, chi1, home_ref, brick_ref, slot_ref, basis_ref, fock_ref,
    xh_ref, xl_ref, ch_ref, cl_ref, sh_ref, sl_ref, och_ref, ocl_ref, osh_ref, osl_ref,
    s1, b1, s2, b2, held, ys, plain_k, turned_k, s3p, b3p, ysp, s4p, b4p, s3, b3, yc, s4, b4, weights,
    ask_out, ask_in, ask_smem, info, info_smem, pot_ref, shuffled, brick_out, brick_in, turned_basis, tiles, samples,
    in_sem, send1, recv1, send2, recv2, send3, recv3, send4, recv4, pot_sem, brick_sem, corr_sem, potential_sem, fock_sem,
):
    px = lax.axis_index("px")
    py = lax.axis_index("py")
    barrier = pltpu.get_barrier_semaphore()

    def greet_px(step, carry):
        pl.semaphore_signal(barrier, inc=1, device_id=(lax.rem(px + step, PX), py), device_id_type=MESH)
        return carry

    def greet_py(step, carry):
        pl.semaphore_signal(barrier, inc=1, device_id=(px, lax.rem(py + step, PY)), device_id_type=MESH)
        return carry

    pairs = (
        (corr_hbm, corr_ref), (solute_hbm, solute_ref), (xh_hbm, xh_ref), (xl_hbm, xl_ref),
        (ch_hbm, ch_ref), (cl_hbm, cl_ref), (sh_hbm, sh_ref), (sl_hbm, sl_ref),
        (home_hbm, home_ref), (brick_hbm, brick_ref), (slot_hbm, slot_ref),
        (chi_hbm.at[:, :, 0], chi0), (chi_hbm.at[:, :, 1, 0], chi1),
        (basis_hbm, basis_ref), (fock_hbm, fock_ref),
        (och_hbm, och_ref), (ocl_hbm, ocl_ref), (osh_hbm, osh_ref), (osl_hbm, osl_ref),
    )
    loads = [pltpu.make_async_copy(source, to, in_sem.at[i]) for i, (source, to) in enumerate(pairs)]
    for load in loads[:11]:
        load.start()
    lax.fori_loop(1, PX, greet_px, 0)
    lax.fori_loop(1, PY, greet_py, 0)
    for load in loads[11:]:
        load.start()
    for load in loads[:4]:
        load.wait()

    lane = lax.broadcasted_iota(jnp.int32, (1, 128), 1)
    lane_re = lane < 64
    lane_field = lax.rem(lane // R, FIELDS)
    lane_spec = (lax.rem(lane, R) == 0) & (py == 0)

    def shift(data, slots):
        return pltpu.roll(data, 16 * slots % 128, 1) if slots else data

    def pack(parts):
        return [jnp.where(lane_field == 3, shift(parts[3], 3 - g), parts[g]) for g in range(3)]

    def unpack(parts):
        last = shift(parts[0], -3)
        for f in range(1, 3):
            last = jnp.where(lane_field == f, shift(parts[f], f - 3), last)
        return parts + [last]

    lane_site = jnp.concatenate([lane_field, lane_field], axis=1)

    def x_forward(turn, carry):
        yp = lax.rem(turn + 3, 4)
        parts = []
        for site in range(SITES):
            rows = closure(corr_ref[site, pl.ds(2 * yp, 2)], solute_ref[site, pl.ds(2 * yp, 2)])
            parts.append(rows.reshape(64, N))
        data = split(jnp.concatenate(parts, axis=0))
        for pair in range(PY // 2):
            wide = dot3(dot, data, (xh_ref[:, 256 * pair:256 * pair + 256], xl_ref[:, 256 * pair:256 * pair + 256]))
            rows = jnp.where(lane_site == 0, wide[0:64], jnp.where(lane_site == 1, wide[64:128], wide[128:192]))
            for half in range(2):
                part = rows[:, 128 * half:128 * half + 128]
                packed = pack([part[8 * g:8 * g + 8] for g in range(4)])
                packed += pack([part[32 + 8 * g:40 + 8 * g] for g in range(4)])
                s1[2 * pair + half, yp] = encode(jnp.concatenate(packed, axis=0), CENTRE_X)

        @pl.when(turn == 0)
        def _():
            pl.semaphore_wait(barrier, PX + PY - 2)

        pltpu.make_async_copy(
            s1.at[py, yp], b1.at[py, yp], recv1.at[yp]
        ).start()

        def send(step, inner):
            other = lax.rem(py + step, PY)
            pltpu.make_async_remote_copy(
                src_ref=s1.at[other, yp], dst_ref=b1.at[py, yp],
                send_sem=send1.at[yp], recv_sem=recv1.at[yp],
                device_id=(px, other), device_id_type=MESH,
            ).start()
            return inner

        return lax.fori_loop(1, PY, send, carry)

    lax.fori_loop(0, 4, x_forward, 0)

    for load in loads[8:11]:
        load.wait()
    home = home_ref[...]
    brick = brick_ref[...]
    down = lax.broadcasted_iota(jnp.int32, (32, 32), 0)
    across = lax.broadcasted_iota(jnp.int32, (32, 32), 1)
    home_down = jnp.sum(jnp.where(down == across, home, 0), axis=1, keepdims=True)
    place = jnp.sum(jnp.where((home_down == home) & (down < across), 1, 0), axis=0, keepdims=True)
    wide_lane = lax.broadcasted_iota(jnp.int32, (32, 128), 1)
    asked = jnp.zeros((32, 128), jnp.int32)
    for k in range(MOST):
        found = jnp.sum(jnp.where((home == down) & (place == k), brick, 0), axis=1, keepdims=True)
        asked = jnp.where(wide_lane == k, jnp.clip(found, 0, 127), asked)
    for other in range(PX):
        ask_out[other] = asked[other:other + 1]
    table = jnp.zeros((32, 128), jnp.int32)
    for k, (value, most) in enumerate(((across, 31), (home, PX - 1), (place, MOST - 1))):
        found = jnp.sum(jnp.where(slot_ref[...] == down, value, 0), axis=1, keepdims=True)
        table = jnp.where(wide_lane == k, jnp.clip(found, 0, most), table)
    info[...] = table
    info_copy = pltpu.make_async_copy(info, info_smem, brick_sem.at[0])
    info_copy.start()
    pltpu.make_async_copy(ask_out.at[px], ask_in.at[px], brick_sem.at[2]).start()

    def ask(step, carry):
        other = lax.rem(px + step, PX)
        pltpu.make_async_remote_copy(
            src_ref=ask_out.at[other], dst_ref=ask_in.at[px],
            send_sem=brick_sem.at[1], recv_sem=brick_sem.at[2],
            device_id=(other, py), device_id_type=MESH,
        ).start()
        return carry

    lax.fori_loop(1, PX, ask, 0)
    for load in loads[4:8]:
        load.wait()

    cos = (ch_ref[...], cl_ref[...])
    sin = (sh_ref[...], sl_ref[...])
    wave = lax.broadcasted_iota(jnp.int32, (N, 1), 0)
    wave_edge = (wave == 0) | (wave == N // 2)
    wave_low = wave < N // 2
    wave_high = wave > N // 2

    def z_forward(yp):
        chunk = b1.at[:, yp]
        pltpu.make_async_copy(chunk, chunk, recv1.at[yp]).wait()
        columns = [[], []]
        for j in range(PY):
            rows = decode(b1[j, yp], CENTRE_X)
            for u in range(2):
                columns[u] += unpack([rows[24 * u + 8 * g:24 * u + 8 * g + 8] for g in range(3)])
        data = split(jnp.concatenate([jnp.concatenate(column, axis=0) for column in columns], axis=1))
        cos_data = dot3(dot, cos, data)
        sin_data = dot3(dot, sin, data)
        halves = []
        for u in range(2):
            cd = cos_data[:, 128 * u:128 * u + 128]
            sd = sin_data[:, 128 * u:128 * u + 128]
            cd_turn = pltpu.roll(cd, 64, 1)
            sd_turn = pltpu.roll(sd, 64, 1)
            usual = jnp.where(lane_re, cd + sd_turn, cd - sd_turn)
            packed_re = jnp.where(wave_high, cd_turn, cd)
            packed_im = jnp.where(wave_edge, cd, jnp.where(wave_low, -sd_turn, -sd))
            packed = jnp.where(lane_re, packed_re, packed_im)
            halves.append(jnp.where(lane_spec, packed, usual).reshape(PX, 8, 128))
        return jnp.concatenate(halves, axis=1)

    held[...] = z_forward(3)

    def z_send(yp, carry):
        rows = z_forward(yp).reshape(PX * 16, 128)
        moved = pltpu.roll(held[...].reshape(PX * 16, 128), 48 - 16 * yp, 1)
        s2[:, yp] = encode(jnp.where(lane_field == 3, moved, rows), CENTRE_Z).reshape(PX, 16, 128)
        pltpu.make_async_copy(s2.at[px, yp], b2.at[px, yp], recv2.at[yp]).start()

        def send(step, inner):
            other = lax.rem(px + step, PX)
            pltpu.make_async_remote_copy(
                src_ref=s2.at[other, yp], dst_ref=b2.at[px, yp],
                send_sem=send2.at[yp], recv_sem=recv2.at[yp],
                device_id=(other, py), device_id_type=MESH,
            ).start()
            return inner

        return lax.fori_loop(1, PX, send, carry)

    lax.fori_loop(0, 3, z_send, 0)

    def collect(buffer, sem, centre, ys, parts):
        def body(part, carry):
            chunk = buffer.at[:, part]
            pltpu.make_async_copy(chunk, chunk, sem.at[part]).wait()

            def place(group, inner):
                sources = pl.ds(8 * group, 8)
                ys[sources, pl.ds(pl.multiple_of(16 * part, 16), 16), :] = decode(buffer[sources, part], centre)
                return inner

            return lax.fori_loop(0, PX // 8, place, carry)

        lax.fori_loop(0, parts, body, 0)

    pencils = ys.reshape(PX * 64, 128)

    def turn_basis(item, carry):
        turned_basis[item] = basis_ref[item].T
        return carry

    loads[13].wait()
    lax.fori_loop(0, 32, turn_basis, 0)
    collect(b2, recv2, CENTRE_Z, ys, 3)

    def unfold(group, carry):
        sources = pl.ds(8 * group, 8)
        rows = [ys[sources, 16 * part:16 * part + 16, :].reshape(128, 128) for part in range(3)]
        ys[sources, 48:64, :] = unpack(rows)[3].reshape(8, 16, 128)
        return carry

    lax.fori_loop(0, PX // 8, unfold, 0)
    loads[11].wait()
    loads[12].wait()

    row = lax.broadcasted_iota(jnp.int32, (R, 1), 0)
    first = (row == 0) & (py == 0)
    wave_y = lax.broadcasted_iota(jnp.int32, (1, N), 1)
    unit = 2.0 * np.pi / N

    def signed_square(index):
        shifted = (lax.rem(index + N // 2, N) - N // 2).astype(F32) * unit
        return shifted * shifted

    square_y = signed_square(wave_y)
    scale = jnp.where(first, 2.0 ** -24, 2.0 ** -23)

    def mix(chi_of, x_re, x_im, screened):
        out_re, out_im = [], []
        pot_re = pot_im = 0.0
        for a in range(SITES):
            t_re = t_im = 0.0
            for b in range(SITES):
                factor = chi_of(a, b)
                t_re = t_re + factor * x_re[b]
                t_im = t_im + factor * x_im[b]
            out_re.append((t_re - x_re[a]) * scale)
            out_im.append((t_im - x_im[a]) * scale)
            pot_re = pot_re + charge_ref[a] * t_re
            pot_im = pot_im + charge_ref[a] * t_im
        out_re.append(pot_re * (screened * scale))
        out_im.append(pot_im * (screened * scale))
        return out_re, out_im

    def y_forward(quad, carry):
        for pair in range(2):
            rows = jnp.concatenate(
                [pencils[pl.ds(4 * quad + 2 * pair + u, N, stride=8), :].T for u in range(2)], axis=0
            )
            data = split(rows)
            cos_data = dot3(dot, data, cos)
            sin_data = dot3(dot, data, sin)
            for u in range(2):
                k = 2 * pair + u
                kz = 4 * quad + k
                kz_all = px * 8 + kz
                base = 128 * u
                pick = lambda array, c, s: array[base + 64 * c + 16 * s:base + 64 * c + 16 * s + 16]
                c_re = [pick(cos_data, 0, s) for s in range(SITES)]
                c_im = [pick(cos_data, 1, s) for s in range(SITES)]
                s_re = [pick(sin_data, 0, s) for s in range(SITES)]
                s_im = [pick(sin_data, 1, s) for s in range(SITES)]
                x_re = [c_re[s] + s_im[s] for s in range(SITES)]
                x_im = [c_im[s] - s_re[s] for s in range(SITES)]
                upper = first & (kz_all > N // 2)
                kx = jnp.where(upper, N // 2, py * R + row)
                square_z = signed_square(jnp.full((1, 1), kz_all, jnp.int32))
                rest = square_z + square_y + 1.0
                screened = (4.0 * np.pi) / (signed_square(kx) + rest)
                chi_of = lambda a, b: jnp.where(upper, chi1[a, b, pl.ds(kz, 1), :], chi0[a, b, :, kz, :])
                if k == 0:
                    edge = first & ((kz_all == 0) | (kz_all == N // 2))
                    b_re = [c_im[s] for s in range(SITES)]
                    b_im = [-s_im[s] for s in range(SITES)]
                    x_re = [jnp.where(edge, c_re[s], x_re[s]) for s in range(SITES)]
                    x_im = [jnp.where(edge, -s_re[s], x_im[s]) for s in range(SITES)]
                    f_re, f_im = mix(chi_of, x_re, x_im, screened)
                    screened = (4.0 * np.pi) / (np.pi ** 2 + rest)
                    g_re, g_im = mix(lambda a, b: chi1[a, b, pl.ds(kz, 1), :], b_re, b_im, screened)
                    other_plain = [jnp.where(edge, g_re[f], f_im[f]) for f in range(FIELDS)]
                    other_turned = [jnp.where(edge, -g_im[f], f_re[f]) for f in range(FIELDS)]
                else:
                    f_re, f_im = mix(chi_of, x_re, x_im, screened)
                    other_plain, other_turned = f_im, f_re
                for f in range(FIELDS):
                    if f == SITES:
                        group, slot = 6 + quad, k
                    elif k < 3:
                        group, slot = 3 * quad + k, f
                    else:
                        group, slot = 3 * quad + f, 3
                    plain_k[group, pl.ds(16 * slot, 16), :] = f_re[f]
                    plain_k[group, pl.ds(64 + 16 * slot, 16), :] = other_plain[f]
                    turned_k[group, pl.ds(16 * slot, 16), :] = -f_im[f]
                    turned_k[group, pl.ds(64 + 16 * slot, 16), :] = other_turned[f]
        return carry

    lax.fori_loop(0, 2, y_forward, 0)

    def y_backward(unit):
        groups = pl.ds(2 * unit, 2)
        plain = split(plain_k[groups].reshape(256, N))
        turned = split(turned_k[groups].reshape(256, N))
        back = dot3(dot_nt, cos, plain) + dot3(dot_nt, sin, turned)
        return encode(
            jnp.concatenate([back[:, 128 * u:128 * u + 128].reshape(PX, 8, 128) for u in range(2)], axis=1),
            CENTRE_Y,
        )

    s3p[...] = y_backward(3)
    pltpu.make_async_copy(s3p.at[px], b3p.at[px], pot_sem.at[1]).start()

    def send_potential(step, carry):
        other = lax.rem(px + step, PX)
        pltpu.make_async_remote_copy(
            src_ref=s3p.at[other], dst_ref=b3p.at[px],
            send_sem=pot_sem.at[0], recv_sem=pot_sem.at[1],
            device_id=(other, py), device_id_type=MESH,
        ).start()
        return carry

    lax.fori_loop(1, PX, send_potential, 0)

    def y_corr(unit, carry):
        s3[:, unit] = y_backward(unit)
        pltpu.make_async_copy(s3.at[px, unit], b3.at[px, unit], recv3.at[unit]).start()

        def send(step, inner):
            other = lax.rem(px + step, PX)
            pltpu.make_async_remote_copy(
                src_ref=s3.at[other, unit], dst_ref=b3.at[px, unit],
                send_sem=send3.at[unit], recv_sem=recv3.at[unit],
                device_id=(other, py), device_id_type=MESH,
            ).start()
            return inner

        return lax.fori_loop(1, PX, send, carry)

    lax.fori_loop(0, 3, y_corr, 0)

    for load in loads[15:19]:
        load.wait()
    cos_order = (och_ref[...], ocl_ref[...])
    sin_order = (osh_ref[...], osl_ref[...])
    order = lax.rem(wave, PX) * 8 + wave // PX
    order_edge = (order == 0) | (order == N // 2)
    order_low = order < N // 2
    order_high = order > N // 2

    zero, one, two = jnp.zeros((N, 128), F32), jnp.ones((N, 128), F32), jnp.full((N, 128), 2.0, F32)
    packed_re = jnp.where(order_edge, one, jnp.where(order_low, two, zero))
    packed_im = jnp.where(order_edge, one, zero)
    weights[0] = jnp.where(lane_spec, jnp.where(lane_re, packed_re, packed_im), one)
    weights[1] = jnp.where(lane_spec & ~lane_re & order_high, two, zero)
    weights[2] = jnp.where(lane_spec & ~lane_re & order_high, -two, zero)
    usual = jnp.where(lane_re, -one, one)
    weights[3] = jnp.where(lane_spec, jnp.where(lane_re & order_low & ~order_edge, -two, zero), usual)

    def z_inverse(columns):
        plain, turned = [], []
        for data in columns:
            turn = pltpu.roll(data, 64, 1)
            plain.append(data * weights[0] + turn * weights[1])
            turned.append(data * weights[2] + turn * weights[3])
        plain = split(jnp.concatenate(plain, axis=1))
        turned = split(jnp.concatenate(turned, axis=1))
        return dot3(dot, cos_order, plain) + dot3(dot, sin_order, turned)

    def x_inverse(rows, count):
        field = jnp.concatenate([lane_field] * PY, axis=1)
        masks = [(field == f).astype(F32).astype(BF16) for f in range(count)]
        data = [jnp.concatenate([part * mask for mask in masks], axis=0) for part in split(rows)]
        return dot3(dot_nt, data, (xh_ref[...], xl_ref[...]))

    pltpu.make_async_copy(b3p, b3p, pot_sem.at[1]).wait()
    ysp[...] = decode(b3p[...], CENTRE_Y)
    tiles_in = ysp.reshape(PX * 16, 128)
    columns = []
    for yq in range(2):
        parts = []
        for quad in range(2):
            rows = [tiles_in[pl.ds(8 * quad + 4 * yq + j, PX, stride=16), :] for j in range(4)]
            for k in range(4):
                part = shift(rows[0], -k)
                for j in range(1, 4):
                    part = jnp.where(lane_field == j, shift(rows[j], j - k), part)
                parts.append(part)
        columns.append(jnp.concatenate(parts, axis=0))
    back = encode(z_inverse(columns), CENTRE_BACK)
    s4p[0] = back[:, 0:128]
    s4p[1] = back[:, 128:256]
    pltpu.make_async_copy(s4p.at[:, pl.ds(32 * py, 32)], b4p.at[py], pot_sem.at[3]).start()

    def send_rows(step, carry):
        other = lax.rem(py + step, PY)
        pltpu.make_async_remote_copy(
            src_ref=s4p.at[:, pl.ds(32 * other, 32)], dst_ref=b4p.at[py],
            send_sem=pot_sem.at[2], recv_sem=pot_sem.at[3],
            device_id=(px, other), device_id_type=MESH,
        ).start()
        return carry

    lax.fori_loop(1, PY, send_rows, 0)
    pltpu.make_async_copy(b4p, b4p, pot_sem.at[3]).wait()
    back = x_inverse(
        jnp.concatenate([decode(b4p[j], CENTRE_BACK).reshape(64, 128) for j in range(PY)], axis=1), FIELDS
    )
    for y in range(8):
        start = 64 * (y % 4) + 32 * (y // 4)
        slab = back[start:start + 32]
        potential_out[y] = slab
        pot_ref[0, y] = slab[:, 0:128]
        pot_ref[1, y] = slab[:, 128:256]
    potential_copy = pltpu.make_async_copy(potential_out, potential_hbm_out, potential_sem.at[0])
    potential_copy.start()

    pltpu.make_async_copy(ask_in, ask_in, brick_sem.at[2]).wait()
    ask_copy = pltpu.make_async_copy(ask_in, ask_smem, brick_sem.at[3])
    ask_copy.start()
    lane_row = lane // 32

    def shuffle(bz, carry):
        for half in range(2):
            slabs = [pot_ref[half, y, pl.ds(8 * bz, 8), :] for y in range(8)]
            for quad in range(4):
                rows = []
                for u in range(2):
                    row = slabs[u]
                    if quad:
                        row = pltpu.roll(row, 128 - 32 * quad, 1)
                    for yg in range(1, 4):
                        move = 32 * ((yg - quad) % 4)
                        other = slabs[2 * yg + u]
                        other = pltpu.roll(other, move, 1) if move else other
                        row = jnp.where(lane_row == yg, other, row)
                    rows.append(row)
                shuffled[8 * bz + 4 * half + quad] = jnp.concatenate(rows, axis=0)
        return carry

    lax.fori_loop(0, 4, shuffle, 0)
    ask_copy.wait()
    lane_place = lax.rem(lane // BRICK, MOST)

    def answer(step, carry):
        other = lax.rem(px + step, PX)
        tile = jnp.zeros((16, 128), F32)
        for k in range(MOST):
            index = ask_smem[other, 0, k]
            moved = pltpu.roll(shuffled[index // 4], lax.rem(BRICK * (k - lax.rem(index, 4)) + 128, 128), 1)
            tile = jnp.where(lane_place == k, moved, tile)
        brick_out[other] = tile.astype(BF16)

        @pl.when(step > 0)
        def _():
            pltpu.make_async_remote_copy(
                src_ref=brick_out.at[other], dst_ref=brick_in.at[px],
                send_sem=brick_sem.at[4], recv_sem=brick_sem.at[5],
                device_id=(other, py), device_id_type=MESH,
            ).start()

        return carry

    lax.fori_loop(0, PX, answer, 0, unroll=4)
    pltpu.make_async_copy(brick_out.at[px], brick_in.at[px], brick_sem.at[5]).start()

    collect(b3, recv3, CENTRE_Y, yc, 3)
    packed = yc.reshape(PX * 48, 128)

    def z_backward(yp, carry):
        columns = []
        for u in range(2):
            parts = []
            for quad in range(2):
                rows = [packed[pl.ds(24 * quad + 8 * g + 2 * yp + u, PX, stride=48), :] for g in range(3)]
                parts += unpack(rows)
            columns.append(jnp.concatenate(parts, axis=0))
        back = z_inverse(columns)
        parts = []
        for u in range(2):
            rows = back[:, 128 * u:128 * u + 128].reshape(PY, 4, 8, 128)
            parts += [part.reshape(PY, 8, 128) for part in pack([rows[:, g].reshape(64, 128) for g in range(4)])]
        s4[yp] = encode(jnp.concatenate(parts, axis=1), CENTRE_BACK)
        pltpu.make_async_copy(s4.at[yp, py], b4.at[py, yp], recv4.at[yp]).start()

        def send(step, inner):
            other = lax.rem(py + step, PY)
            pltpu.make_async_remote_copy(
                src_ref=s4.at[yp, other], dst_ref=b4.at[py, yp],
                send_sem=send4.at[yp], recv_sem=recv4.at[yp],
                device_id=(px, other), device_id_type=MESH,
            ).start()
            return inner

        return lax.fori_loop(1, PY, send, carry)

    lax.fori_loop(0, 4, z_backward, 0)
    info_copy.wait()
    loads[14].wait()
    pltpu.make_async_copy(brick_in, brick_in, brick_sem.at[5]).wait()

    def take(slot, carry):
        tile = brick_in[info_smem[slot, 1]].astype(F32)
        tile = pltpu.roll(tile, lax.rem(128 - BRICK * info_smem[slot, 2], 128), 1)
        tiles[pl.ds(pl.multiple_of(16 * slot, 16), 16), :] = tile.astype(BF16)
        return carry

    lax.fori_loop(0, 32, take, 0, unroll=8)
    cell = lax.broadcasted_iota(jnp.int32, (128, 512), 1)
    origin = lax.broadcasted_iota(jnp.int32, (128, 512), 0)
    spread = (origin == 32 * (cell // 128) + lax.rem(cell, BRICK)).astype(F32).astype(BF16)
    wide = dot(tiles[...], spread)
    tile_row = lax.broadcasted_iota(jnp.int32, (512, 512), 0)
    tile_cell = lax.broadcasted_iota(jnp.int32, (512, 512), 1)
    wide = jnp.where(lax.rem(tile_row, 16) == lax.rem(tile_cell, 128) // BRICK, wide, 0.0).astype(BF16)
    slot_down = lax.broadcasted_iota(jnp.int32, (32, 512), 0)
    slot_cell = lax.broadcasted_iota(jnp.int32, (32, 512), 1)
    samples[...] = dot((slot_down == slot_cell // 16).astype(F32).astype(BF16), wide)

    def embed(group, carry):
        for item in range(4):
            slot = 4 * group + item
            fragment = info_smem[slot, 0]
            weighted = turned_basis[fragment] * samples[pl.ds(slot, 1), :].astype(BF16)
            fock_out[slot] = fock_ref[slot] + dot(weighted, basis_ref[fragment]).T
        slots = pl.ds(4 * group, 4)
        pltpu.make_async_copy(fock_out.at[slots], fock_hbm_out.at[slots], fock_sem.at[group]).start()
        return carry

    lax.fori_loop(0, 8, embed, 0)

    def x_backward(yp, carry):
        chunk = b4.at[:, yp]
        pltpu.make_async_copy(chunk, chunk, recv4.at[yp]).wait()
        wide = []
        for j in range(PY):
            rows = decode(b4[j, yp], CENTRE_BACK)
            parts = []
            for u in range(2):
                parts += unpack([rows[24 * u + 8 * g:24 * u + 8 * g + 8] for g in range(3)])
            wide.append(jnp.concatenate(parts, axis=0))
        back = x_inverse(jnp.concatenate(wide, axis=1), SITES)
        slabs = pl.ds(2 * yp, 2)
        for f in range(SITES):
            corr_out[f, slabs] = back[64 * f:64 * f + 64].reshape(2, 32, N)
        pltpu.make_async_copy(corr_out.at[:, slabs], corr_hbm_out.at[:, slabs], corr_sem.at[yp]).start()
        return carry

    lax.fori_loop(0, 4, x_backward, 0)
    potential_copy.wait()
    for part in range(4):
        slabs = pl.ds(2 * part, 2)
        pltpu.make_async_copy(corr_out.at[:, slabs], corr_hbm_out.at[:, slabs], corr_sem.at[part]).wait()
    for part in range(8):
        slots = pl.ds(4 * part, 4)
        pltpu.make_async_copy(fock_out.at[slots], fock_hbm_out.at[slots], fock_sem.at[part]).wait()

    for part in range(4):
        sent = s1.at[pl.ds(0, PY - 1), 0]
        pltpu.make_async_copy(sent, sent, send1.at[part]).wait()
        if part < 3:
            sent = s2.at[pl.ds(0, PX - 1), 0]
            pltpu.make_async_copy(sent, sent, send2.at[part]).wait()
            sent = s3.at[pl.ds(0, PX - 1), 0]
            pltpu.make_async_copy(sent, sent, send3.at[part]).wait()
        sent = s4.at[0, pl.ds(0, PY - 1)]
        pltpu.make_async_copy(sent, sent, send4.at[part]).wait()
    sent = s3p.at[pl.ds(0, PX - 1)]
    pltpu.make_async_copy(sent, sent, pot_sem.at[0]).wait()
    sent = s4p.at[:, pl.ds(0, 32 * (PY - 1))]
    pltpu.make_async_copy(sent, sent, pot_sem.at[2]).wait()
    sent = ask_out.at[pl.ds(0, PX - 1)]
    pltpu.make_async_copy(sent, sent, brick_sem.at[1]).wait()
    sent = brick_out.at[pl.ds(0, PX - 1)]
    pltpu.make_async_copy(sent, sent, brick_sem.at[4]).wait()


def store_kernel(*refs):
    sources, targets, held, in_sem, out_sem = refs[:3], refs[3:6], refs[6:9], refs[9], refs[10]
    loads, stores = [], []
    for i in range(3):
        count = (3, 1, 8)[i]
        step = sources[i].shape[0] // count
        for part in range(count):
            rows = pl.ds(part * step, step)
            sem = len(loads)
            loads.append(pltpu.make_async_copy(sources[i].at[rows], held[i].at[rows], in_sem.at[sem]))
            stores.append(pltpu.make_async_copy(held[i].at[rows], targets[i].at[rows], out_sem.at[sem]))
    for load in loads:
        load.start()
    for load, store in zip(loads, stores):
        load.wait()
        store.start()
    for store in stores:
        store.wait()


def shards(
    corr, solute_pot, chi, site_charge, home_slab, brick_index, block_slot, basis_values, fock_in
):
    hbm = pl.BlockSpec(memory_space=pltpu.HBM)
    dma = pltpu.SemaphoreType.DMA((4,))
    frags = home_slab.shape[0]
    results = pl.pallas_call(
        field_kernel,
        name="fields",
        out_shape=(
            jax.ShapeDtypeStruct((SITES, 8, 32, N), F32),
            jax.ShapeDtypeStruct((8, 32, N), F32),
            jax.ShapeDtypeStruct(fock_in.shape, F32),
        ),
        in_specs=[pl.BlockSpec(memory_space=pltpu.SMEM)] + [hbm] * 18,
        out_specs=(hbm,) * 3,
        scratch_shapes=[
            pltpu.VMEM(corr.shape, F32),
            pltpu.VMEM(corr.shape[1:], F32),
            pltpu.VMEM(fock_in.shape, F32),
            pltpu.VMEM(corr.shape, F32),
            pltpu.VMEM(solute_pot.shape, BF16),
            pltpu.VMEM((SITES, SITES, R, 8, N), F32),
            pltpu.VMEM((SITES, SITES, 8, N), F32),
            pltpu.VMEM((1, frags), jnp.int32),
            pltpu.VMEM((1, frags), jnp.int32),
            pltpu.VMEM((1, frags), jnp.int32),
            pltpu.VMEM(basis_values.shape, BF16),
            pltpu.VMEM(fock_in.shape, F32),
            pltpu.VMEM((N, PY * 128), BF16),
            pltpu.VMEM((N, PY * 128), BF16),
        ] + [pltpu.VMEM((N, N), BF16)] * 8 + [
            pltpu.VMEM((PY, 4, 48, 128), WIRE),
            pltpu.VMEM((PY, 4, 48, 128), WIRE),
            pltpu.VMEM((PX, 3, 16, 128), WIRE),
            pltpu.VMEM((PX, 3, 16, 128), WIRE),
            pltpu.VMEM((PX, 16, 128), F32),
            pltpu.VMEM((PX, 64, 128), F32),
            pltpu.VMEM((8, 128, N), F32),
            pltpu.VMEM((8, 128, N), F32),
            pltpu.VMEM((PX, 16, 128), WIRE),
            pltpu.VMEM((PX, 16, 128), WIRE),
            pltpu.VMEM((PX, 16, 128), F32),
            pltpu.VMEM((2, N, 128), WIRE),
            pltpu.VMEM((PY, 2, 32, 128), WIRE),
            pltpu.VMEM((PX, 3, 16, 128), WIRE),
            pltpu.VMEM((PX, 3, 16, 128), WIRE),
            pltpu.VMEM((PX, 48, 128), F32),
            pltpu.VMEM((4, PY, 48, 128), WIRE),
            pltpu.VMEM((PY, 4, 48, 128), WIRE),
            pltpu.VMEM((4, N, 128), F32),
            pltpu.VMEM((PX, 1, 128), jnp.int32),
            pltpu.VMEM((PX, 1, 128), jnp.int32),
            pltpu.SMEM((PX, 1, 128), jnp.int32),
            pltpu.VMEM((frags, 128), jnp.int32),
            pltpu.SMEM((frags, 128), jnp.int32),
            pltpu.VMEM((2, 8, 32, 128), F32),
            pltpu.VMEM((32, 16, 128), F32),
            pltpu.VMEM((PX, 16, 128), BF16),
            pltpu.VMEM((PX, 16, 128), BF16),
            pltpu.VMEM((frags, 128, 512), BF16),
            pltpu.VMEM((frags * 16, 128), BF16),
            pltpu.VMEM((frags, 512), F32),
            pltpu.SemaphoreType.DMA((19,)),
        ] + [dma] * 9 + [pltpu.SemaphoreType.DMA((6,)), dma, dma, pltpu.SemaphoreType.DMA((8,))],
        compiler_params=pltpu.CompilerParams(
            collective_id=0, has_side_effects=True, vmem_limit_bytes=60 * 2**20
        ),
    )(
        site_charge, corr, solute_pot, chi, home_slab.reshape(1, frags), brick_index.reshape(1, frags),
        block_slot, basis_values, fock_in, *[jnp.asarray(table) for table in tables()],
    )
    shapes = [jax.ShapeDtypeStruct(result.shape, F32) for result in results]
    return pl.pallas_call(
        store_kernel,
        name="store",
        out_shape=tuple(shapes),
        in_specs=[hbm] * 3,
        out_specs=(hbm,) * 3,
        scratch_shapes=[pltpu.VMEM(shape.shape, F32) for shape in shapes] + [pltpu.SemaphoreType.DMA((12,))] * 2,
        compiler_params=pltpu.CompilerParams(vmem_limit_bytes=60 * 2**20),
    )(*results)


def solution(mesh):
    return jax.shard_map(
        shards,
        mesh=mesh,
        in_specs=(
            P(None, "px", "py", None),
            P(None, "px", "py", None),
            P(None, None, None, "py", "px", None),
            P(),
            P(("px", "py"), None),
            P(("px", "py")),
            P(("px", "py"), None),
            P(("px", "py"), None, None),
            P(("px", "py"), None, None),
        ),
        out_specs=(P(None, "px", "py", None), P("px", "py", None), P(("px", "py"), None, None)),
        check_vma=False,
    )
```

```python
import functools
import jax
import jax.numpy as jnp
import numpy as np
from jax import lax
from jax.experimental import pallas as pl
from jax.experimental.pallas import tpu as pltpu
from jax.sharding import PartitionSpec as P

BRICK = 8
MOST = 4
N = 256
PX = 32
PY = 8
SITES = 3
FIELDS = 4
R = 16
MESH = pl.DeviceIdType.MESH
F32 = jnp.float32
BF16 = jnp.bfloat16
WIRE = jnp.bfloat16
FINE, STEEP, SLOPE = 11.0, 8.0, 3.0
CENTRE_X, CENTRE_Z, CENTRE_Y, CENTRE_BACK = 5.0, 9.0, -5.0, -1.0


def split(values):
    high = values.astype(BF16)
    return high, (values - high.astype(F32)).astype(BF16)


def np_split(values):
    high = values.astype(np.float32).astype(BF16)
    low = (values - high.astype(np.float64)).astype(np.float32).astype(BF16)
    return high, low


def tables():
    index = np.arange(N)
    angle = (index[:, None] * index[None, :] % N) * (2.0 * np.pi / N)
    cos, sin = np.cos(angle), np.sin(angle)
    half_re = cos[:, : N // 2].copy()
    half_im = -sin[:, : N // 2]
    half_im[:, 0] = cos[:, N // 2]
    halves = np.stack([half_re.reshape(N, PY, R), half_im.reshape(N, PY, R)], axis=2)
    spread = np.broadcast_to(halves[:, :, :, None, :], (N, PY, 2, FIELDS, R))
    spread = spread.reshape(N, PY * 128)
    order = index % PX * 8 + index // PX
    return np_split(spread) + np_split(cos) + np_split(sin) + np_split(cos[:, order]) + np_split(sin[:, order])


def encode(values, centre):
    power = jnp.log2(jnp.abs(values)) - centre
    power = SLOPE * power + (STEEP - SLOPE) * jnp.clip(power, -FINE, FINE)
    coded = jnp.exp2(power)
    return jnp.where(values < 0, -coded, coded).astype(WIRE)


def decode(coded, centre):
    coded = coded.astype(F32)
    power = jnp.log2(jnp.abs(coded))
    fine = jnp.clip(power, -FINE * STEEP, FINE * STEEP)
    values = jnp.exp2(power * (1.0 / SLOPE) + fine * (1.0 / STEEP - 1.0 / SLOPE) + centre)
    return jnp.where(coded < 0, -values, values)


def dot(left, right):
    return jnp.dot(left, right, preferred_element_type=F32)


def dot_nt(left, right):
    return lax.dot_general(left, right, (((1,), (1,)), ((), ())), preferred_element_type=F32)


def dot3(product, left, right):
    return product(left[0], right[0]) + product(left[0], right[1]) + product(left[1], right[0])


def closure(corr, solute_pot):
    excess = corr - solute_pot.astype(F32)
    low = jnp.minimum(excess, 0.0)
    series = jnp.full_like(low, 1.0 / 362880.0)
    for denominator in (40320.0, 5040.0, 720.0, 120.0, 24.0, 6.0, 2.0, 1.0):
        series = series * low + 1.0 / denominator
    grown = jnp.where(low > -0.5, series * low, jnp.exp(low) - 1.0)
    return jnp.where(excess > 0, excess, grown) - corr


def field_kernel(
    charge_ref, corr_hbm, solute_hbm, chi_hbm, home_hbm, brick_hbm, slot_hbm, basis_hbm, fock_hbm,
    xh_hbm, xl_hbm, ch_hbm, cl_hbm, sh_hbm, sl_hbm, och_hbm, ocl_hbm, osh_hbm, osl_hbm,
    corr_hbm_out, potential_hbm_out, fock_hbm_out,
    corr_out, potential_out, fock_out,
    corr_ref, solute_ref, chi0, chi1, home_ref, brick_ref, slot_ref, basis_ref, fock_ref,
    xh_ref, xl_ref, ch_ref, cl_ref, sh_ref, sl_ref, och_ref, ocl_ref, osh_ref, osl_ref,
    s1, b1, s2, b2, held, ys, plain_k, turned_k, s3p, b3p, ysp, s4p, b4p, s3, b3, yc, s4, b4, weights,
    ask_out, ask_in, ask_smem, info, info_smem, pot_ref, shuffled, brick_out, brick_in, turned_basis, tiles, samples,
    in_sem, send1, recv1, send2, recv2, send3, recv3, send4, recv4, pot_sem, brick_sem, corr_sem, potential_sem, fock_sem,
):
    px = lax.axis_index("px")
    py = lax.axis_index("py")
    barrier = pltpu.get_barrier_semaphore()

    def far(step):
        return lax.rem(px + PX // 2 + (step // 2) * (2 * lax.rem(step, 2) - 1) + PX, PX)

    def greet_px(step, carry):
        pl.semaphore_signal(barrier, inc=1, device_id=(lax.rem(px + step, PX), py), device_id_type=MESH)
        return carry

    def greet_py(step, carry):
        pl.semaphore_signal(barrier, inc=1, device_id=(px, lax.rem(py + step, PY)), device_id_type=MESH)
        return carry

    pairs = (
        (corr_hbm, corr_ref), (solute_hbm, solute_ref), (xh_hbm, xh_ref), (xl_hbm, xl_ref),
        (ch_hbm, ch_ref), (cl_hbm, cl_ref), (sh_hbm, sh_ref), (sl_hbm, sl_ref),
        (home_hbm, home_ref), (brick_hbm, brick_ref), (slot_hbm, slot_ref),
        (chi_hbm.at[:, :, 0], chi0), (chi_hbm.at[:, :, 1, 0], chi1),
        (basis_hbm, basis_ref), (fock_hbm, fock_ref),
        (och_hbm, och_ref), (ocl_hbm, ocl_ref), (osh_hbm, osh_ref), (osl_hbm, osl_ref),
    )
    loads = [pltpu.make_async_copy(source, to, in_sem.at[i]) for i, (source, to) in enumerate(pairs)]
    for load in loads[:11]:
        load.start()
    lax.fori_loop(1, PX, greet_px, 0)
    lax.fori_loop(1, PY, greet_py, 0)
    for load in loads[11:]:
        load.start()
    for load in loads[:4]:
        load.wait()

    lane = lax.broadcasted_iota(jnp.int32, (1, 128), 1)
    lane_re = lane < 64
    lane_field = lax.rem(lane // R, FIELDS)
    lane_spec = (lax.rem(lane, R) == 0) & (py == 0)

    def shift(data, slots):
        return pltpu.roll(data, 16 * slots % 128, 1) if slots else data

    def pack(parts):
        return [jnp.where(lane_field == 3, shift(parts[3], 3 - g), parts[g]) for g in range(3)]

    def unpack(parts):
        last = shift(parts[0], -3)
        for f in range(1, 3):
            last = jnp.where(lane_field == f, shift(parts[f], f - 3), last)
        return parts + [last]

    lane_site = jnp.concatenate([lane_field, lane_field], axis=1)

    def x_forward(turn, carry):
        yp = lax.rem(turn + 3, 4)
        parts = []
        for site in range(SITES):
            rows = closure(corr_ref[site, pl.ds(2 * yp, 2)], solute_ref[site, pl.ds(2 * yp, 2)])
            parts.append(rows.reshape(64, N))
        data = split(jnp.concatenate(parts, axis=0))
        for pair in range(PY // 2):
            wide = dot3(dot, data, (xh_ref[:, 256 * pair:256 * pair + 256], xl_ref[:, 256 * pair:256 * pair + 256]))
            rows = jnp.where(lane_site == 0, wide[0:64], jnp.where(lane_site == 1, wide[64:128], wide[128:192]))
            for half in range(2):
                part = rows[:, 128 * half:128 * half + 128]
                packed = pack([part[8 * g:8 * g + 8] for g in range(4)])
                packed += pack([part[32 + 8 * g:40 + 8 * g] for g in range(4)])
                s1[2 * pair + half, yp] = encode(jnp.concatenate(packed, axis=0), CENTRE_X)

        @pl.when(turn == 0)
        def _():
            pl.semaphore_wait(barrier, PX + PY - 2)

        pltpu.make_async_copy(
            s1.at[py, yp], b1.at[py, yp], recv1.at[yp]
        ).start()

        def send(step, inner):
            other = lax.rem(py + step, PY)
            pltpu.make_async_remote_copy(
                src_ref=s1.at[other, yp], dst_ref=b1.at[py, yp],
                send_sem=send1.at[yp], recv_sem=recv1.at[yp],
                device_id=(px, other), device_id_type=MESH,
            ).start()
            return inner

        return lax.fori_loop(1, PY, send, carry)

    lax.fori_loop(0, 4, x_forward, 0)

    for load in loads[8:11]:
        load.wait()
    home = home_ref[...]
    brick = brick_ref[...]
    down = lax.broadcasted_iota(jnp.int32, (32, 32), 0)
    across = lax.broadcasted_iota(jnp.int32, (32, 32), 1)
    home_down = jnp.sum(jnp.where(down == across, home, 0), axis=1, keepdims=True)
    place = jnp.sum(jnp.where((home_down == home) & (down < across), 1, 0), axis=0, keepdims=True)
    wide_lane = lax.broadcasted_iota(jnp.int32, (32, 128), 1)
    asked = jnp.zeros((32, 128), jnp.int32)
    for k in range(MOST):
        found = jnp.sum(jnp.where((home == down) & (place == k), brick, 0), axis=1, keepdims=True)
        asked = jnp.where(wide_lane == k, jnp.clip(found, 0, 127), asked)
    for other in range(PX):
        ask_out[other] = asked[other:other + 1]
    table = jnp.zeros((32, 128), jnp.int32)
    for k, (value, most) in enumerate(((across, 31), (home, PX - 1), (place, MOST - 1))):
        found = jnp.sum(jnp.where(slot_ref[...] == down, value, 0), axis=1, keepdims=True)
        table = jnp.where(wide_lane == k, jnp.clip(found, 0, most), table)
    info[...] = table
    info_copy = pltpu.make_async_copy(info, info_smem, brick_sem.at[0])
    info_copy.start()
    pltpu.make_async_copy(ask_out.at[px], ask_in.at[px], brick_sem.at[2]).start()

    def ask(step, carry):
        other = far(step)
        pltpu.make_async_remote_copy(
            src_ref=ask_out.at[other], dst_ref=ask_in.at[px],
            send_sem=brick_sem.at[1], recv_sem=brick_sem.at[2],
            device_id=(other, py), device_id_type=MESH,
        ).start()
        return carry

    lax.fori_loop(1, PX, ask, 0)
    for load in loads[4:8]:
        load.wait()

    cos = (ch_ref[...], cl_ref[...])
    sin = (sh_ref[...], sl_ref[...])
    wave = lax.broadcasted_iota(jnp.int32, (N, 1), 0)
    wave_edge = (wave == 0) | (wave == N // 2)
    wave_low = wave < N // 2
    wave_high = wave > N // 2

    def z_forward(yp):
        chunk = b1.at[:, yp]
        pltpu.make_async_copy(chunk, chunk, recv1.at[yp]).wait()
        columns = [[], []]
        for j in range(PY):
            rows = decode(b1[j, yp], CENTRE_X)
            for u in range(2):
                columns[u] += unpack([rows[24 * u + 8 * g:24 * u + 8 * g + 8] for g in range(3)])
        data = split(jnp.concatenate([jnp.concatenate(column, axis=0) for column in columns], axis=1))
        cos_data = dot3(dot, cos, data)
        sin_data = dot3(dot, sin, data)
        halves = []
        for u in range(2):
            cd = cos_data[:, 128 * u:128 * u + 128]
            sd = sin_data[:, 128 * u:128 * u + 128]
            cd_turn = pltpu.roll(cd, 64, 1)
            sd_turn = pltpu.roll(sd, 64, 1)
            usual = jnp.where(lane_re, cd + sd_turn, cd - sd_turn)
            packed_re = jnp.where(wave_high, cd_turn, cd)
            packed_im = jnp.where(wave_edge, cd, jnp.where(wave_low, -sd_turn, -sd))
            packed = jnp.where(lane_re, packed_re, packed_im)
            halves.append(jnp.where(lane_spec, packed, usual).reshape(PX, 8, 128))
        return jnp.concatenate(halves, axis=1)

    held[...] = z_forward(3)

    def z_send(yp, carry):
        rows = z_forward(yp).reshape(PX * 16, 128)
        moved = pltpu.roll(held[...].reshape(PX * 16, 128), 48 - 16 * yp, 1)
        s2[:, yp] = encode(jnp.where(lane_field == 3, moved, rows), CENTRE_Z).reshape(PX, 16, 128)
        pltpu.make_async_copy(s2.at[px, yp], b2.at[px, yp], recv2.at[yp]).start()

        def send(step, inner):
            other = far(step)
            pltpu.make_async_remote_copy(
                src_ref=s2.at[other, yp], dst_ref=b2.at[px, yp],
                send_sem=send2.at[yp], recv_sem=recv2.at[yp],
                device_id=(other, py), device_id_type=MESH,
            ).start()
            return inner

        return lax.fori_loop(1, PX, send, carry)

    lax.fori_loop(0, 3, z_send, 0)

    def collect(buffer, sem, centre, ys, parts):
        def body(part, carry):
            chunk = buffer.at[:, part]
            pltpu.make_async_copy(chunk, chunk, sem.at[part]).wait()

            def place(group, inner):
                sources = pl.ds(8 * group, 8)
                ys[sources, pl.ds(pl.multiple_of(16 * part, 16), 16), :] = decode(buffer[sources, part], centre)
                return inner

            return lax.fori_loop(0, PX // 8, place, carry)

        lax.fori_loop(0, parts, body, 0)

    pencils = ys.reshape(PX * 64, 128)

    def turn_basis(item, carry):
        turned_basis[item] = basis_ref[item].T
        return carry

    loads[13].wait()
    lax.fori_loop(0, 32, turn_basis, 0)
    collect(b2, recv2, CENTRE_Z, ys, 3)

    def unfold(group, carry):
        sources = pl.ds(8 * group, 8)
        rows = [ys[sources, 16 * part:16 * part + 16, :].reshape(128, 128) for part in range(3)]
        ys[sources, 48:64, :] = unpack(rows)[3].reshape(8, 16, 128)
        return carry

    lax.fori_loop(0, PX // 8, unfold, 0)
    loads[11].wait()
    loads[12].wait()

    row = lax.broadcasted_iota(jnp.int32, (R, 1), 0)
    first = (row == 0) & (py == 0)
    wave_y = lax.broadcasted_iota(jnp.int32, (1, N), 1)
    unit = 2.0 * np.pi / N

    def signed_square(index):
        shifted = (lax.rem(index + N // 2, N) - N // 2).astype(F32) * unit
        return shifted * shifted

    square_y = signed_square(wave_y)
    scale = jnp.where(first, 2.0 ** -24, 2.0 ** -23)

    def mix(chi_of, x_re, x_im, screened):
        out_re, out_im = [], []
        pot_re = pot_im = 0.0
        for a in range(SITES):
            t_re = t_im = 0.0
            for b in range(SITES):
                factor = chi_of(a, b)
                t_re = t_re + factor * x_re[b]
                t_im = t_im + factor * x_im[b]
            out_re.append((t_re - x_re[a]) * scale)
            out_im.append((t_im - x_im[a]) * scale)
            pot_re = pot_re + charge_ref[a] * t_re
            pot_im = pot_im + charge_ref[a] * t_im
        out_re.append(pot_re * (screened * scale))
        out_im.append(pot_im * (screened * scale))
        return out_re, out_im

    def y_forward(quad, carry):
        for pair in range(2):
            rows = jnp.concatenate(
                [pencils[pl.ds(4 * quad + 2 * pair + u, N, stride=8), :].T for u in range(2)], axis=0
            )
            data = split(rows)
            cos_data = dot3(dot, data, cos)
            sin_data = dot3(dot, data, sin)
            for u in range(2):
                k = 2 * pair + u
                kz = 4 * quad + k
                kz_all = px * 8 + kz
                base = 128 * u
                pick = lambda array, c, s: array[base + 64 * c + 16 * s:base + 64 * c + 16 * s + 16]
                c_re = [pick(cos_data, 0, s) for s in range(SITES)]
                c_im = [pick(cos_data, 1, s) for s in range(SITES)]
                s_re = [pick(sin_data, 0, s) for s in range(SITES)]
                s_im = [pick(sin_data, 1, s) for s in range(SITES)]
                x_re = [c_re[s] + s_im[s] for s in range(SITES)]
                x_im = [c_im[s] - s_re[s] for s in range(SITES)]
                upper = first & (kz_all > N // 2)
                kx = jnp.where(upper, N // 2, py * R + row)
                square_z = signed_square(jnp.full((1, 1), kz_all, jnp.int32))
                rest = square_z + square_y + 1.0
                screened = (4.0 * np.pi) / (signed_square(kx) + rest)
                chi_of = lambda a, b: jnp.where(upper, chi1[a, b, pl.ds(kz, 1), :], chi0[a, b, :, kz, :])
                if k == 0:
                    edge = first & ((kz_all == 0) | (kz_all == N // 2))
                    b_re = [c_im[s] for s in range(SITES)]
                    b_im = [-s_im[s] for s in range(SITES)]
                    x_re = [jnp.where(edge, c_re[s], x_re[s]) for s in range(SITES)]
                    x_im = [jnp.where(edge, -s_re[s], x_im[s]) for s in range(SITES)]
                    f_re, f_im = mix(chi_of, x_re, x_im, screened)
                    screened = (4.0 * np.pi) / (np.pi ** 2 + rest)
                    g_re, g_im = mix(lambda a, b: chi1[a, b, pl.ds(kz, 1), :], b_re, b_im, screened)
                    other_plain = [jnp.where(edge, g_re[f], f_im[f]) for f in range(FIELDS)]
                    other_turned = [jnp.where(edge, -g_im[f], f_re[f]) for f in range(FIELDS)]
                else:
                    f_re, f_im = mix(chi_of, x_re, x_im, screened)
                    other_plain, other_turned = f_im, f_re
                for f in range(FIELDS):
                    if f == SITES:
                        group, slot = 6 + quad, k
                    elif k < 3:
                        group, slot = 3 * quad + k, f
                    else:
                        group, slot = 3 * quad + f, 3
                    plain_k[group, pl.ds(16 * slot, 16), :] = f_re[f]
                    plain_k[group, pl.ds(64 + 16 * slot, 16), :] = other_plain[f]
                    turned_k[group, pl.ds(16 * slot, 16), :] = -f_im[f]
                    turned_k[group, pl.ds(64 + 16 * slot, 16), :] = other_turned[f]
        return carry

    lax.fori_loop(0, 2, y_forward, 0)

    def y_backward(unit):
        groups = pl.ds(2 * unit, 2)
        plain = split(plain_k[groups].reshape(256, N))
        turned = split(turned_k[groups].reshape(256, N))
        back = dot3(dot_nt, cos, plain) + dot3(dot_nt, sin, turned)
        return encode(
            jnp.concatenate([back[:, 128 * u:128 * u + 128].reshape(PX, 8, 128) for u in range(2)], axis=1),
            CENTRE_Y,
        )

    s3p[...] = y_backward(3)
    pltpu.make_async_copy(s3p.at[px], b3p.at[px], pot_sem.at[1]).start()

    def send_potential(step, carry):
        other = far(step)
        pltpu.make_async_remote_copy(
            src_ref=s3p.at[other], dst_ref=b3p.at[px],
            send_sem=pot_sem.at[0], recv_sem=pot_sem.at[1],
            device_id=(other, py), device_id_type=MESH,
        ).start()
        return carry

    lax.fori_loop(1, PX, send_potential, 0)

    def y_corr(unit, carry):
        s3[:, unit] = y_backward(unit)
        pltpu.make_async_copy(s3.at[px, unit], b3.at[px, unit], recv3.at[unit]).start()

        def send(step, inner):
            other = far(step)
            pltpu.make_async_remote_copy(
                src_ref=s3.at[other, unit], dst_ref=b3.at[px, unit],
                send_sem=send3.at[unit], recv_sem=recv3.at[unit],
                device_id=(other, py), device_id_type=MESH,
            ).start()
            return inner

        return lax.fori_loop(1, PX, send, carry)

    lax.fori_loop(0, 3, y_corr, 0)

    for load in loads[15:19]:
        load.wait()
    cos_order = (och_ref[...], ocl_ref[...])
    sin_order = (osh_ref[...], osl_ref[...])
    order = lax.rem(wave, PX) * 8 + wave // PX
    order_edge = (order == 0) | (order == N // 2)
    order_low = order < N // 2
    order_high = order > N // 2

    zero, one, two = jnp.zeros((N, 128), F32), jnp.ones((N, 128), F32), jnp.full((N, 128), 2.0, F32)
    packed_re = jnp.where(order_edge, one, jnp.where(order_low, two, zero))
    packed_im = jnp.where(order_edge, one, zero)
    weights[0] = jnp.where(lane_spec, jnp.where(lane_re, packed_re, packed_im), one)
    weights[1] = jnp.where(lane_spec & ~lane_re & order_high, two, zero)
    weights[2] = jnp.where(lane_spec & ~lane_re & order_high, -two, zero)
    usual = jnp.where(lane_re, -one, one)
    weights[3] = jnp.where(lane_spec, jnp.where(lane_re & order_low & ~order_edge, -two, zero), usual)

    def z_inverse(columns):
        plain, turned = [], []
        for data in columns:
            turn = pltpu.roll(data, 64, 1)
            plain.append(data * weights[0] + turn * weights[1])
            turned.append(data * weights[2] + turn * weights[3])
        plain = split(jnp.concatenate(plain, axis=1))
        turned = split(jnp.concatenate(turned, axis=1))
        return dot3(dot, cos_order, plain) + dot3(dot, sin_order, turned)

    def x_inverse(rows, count):
        field = jnp.concatenate([lane_field] * PY, axis=1)
        masks = [(field == f).astype(F32).astype(BF16) for f in range(count)]
        data = [jnp.concatenate([part * mask for mask in masks], axis=0) for part in split(rows)]
        return dot3(dot_nt, data, (xh_ref[...], xl_ref[...]))

    pltpu.make_async_copy(b3p, b3p, pot_sem.at[1]).wait()
    ysp[...] = decode(b3p[...], CENTRE_Y)
    tiles_in = ysp.reshape(PX * 16, 128)
    columns = []
    for yq in range(2):
        parts = []
        for quad in range(2):
            rows = [tiles_in[pl.ds(8 * quad + 4 * yq + j, PX, stride=16), :] for j in range(4)]
            for k in range(4):
                part = shift(rows[0], -k)
                for j in range(1, 4):
                    part = jnp.where(lane_field == j, shift(rows[j], j - k), part)
                parts.append(part)
        columns.append(jnp.concatenate(parts, axis=0))
    back = encode(z_inverse(columns), CENTRE_BACK)
    s4p[0] = back[:, 0:128]
    s4p[1] = back[:, 128:256]
    pltpu.make_async_copy(s4p.at[:, pl.ds(32 * py, 32)], b4p.at[py], pot_sem.at[3]).start()

    def send_rows(step, carry):
        other = lax.rem(py + step, PY)
        pltpu.make_async_remote_copy(
            src_ref=s4p.at[:, pl.ds(32 * other, 32)], dst_ref=b4p.at[py],
            send_sem=pot_sem.at[2], recv_sem=pot_sem.at[3],
            device_id=(px, other), device_id_type=MESH,
        ).start()
        return carry

    lax.fori_loop(1, PY, send_rows, 0)
    pltpu.make_async_copy(b4p, b4p, pot_sem.at[3]).wait()
    back = x_inverse(
        jnp.concatenate([decode(b4p[j], CENTRE_BACK).reshape(64, 128) for j in range(PY)], axis=1), FIELDS
    )
    for y in range(8):
        start = 64 * (y % 4) + 32 * (y // 4)
        slab = back[start:start + 32]
        potential_out[y] = slab
        pot_ref[0, y] = slab[:, 0:128]
        pot_ref[1, y] = slab[:, 128:256]
    potential_copy = pltpu.make_async_copy(potential_out, potential_hbm_out, potential_sem.at[0])
    potential_copy.start()

    pltpu.make_async_copy(ask_in, ask_in, brick_sem.at[2]).wait()
    ask_copy = pltpu.make_async_copy(ask_in, ask_smem, brick_sem.at[3])
    ask_copy.start()
    lane_row = lane // 32

    def shuffle(bz, carry):
        for half in range(2):
            slabs = [pot_ref[half, y, pl.ds(8 * bz, 8), :] for y in range(8)]
            for quad in range(4):
                rows = []
                for u in range(2):
                    row = slabs[u]
                    if quad:
                        row = pltpu.roll(row, 128 - 32 * quad, 1)
                    for yg in range(1, 4):
                        move = 32 * ((yg - quad) % 4)
                        other = slabs[2 * yg + u]
                        other = pltpu.roll(other, move, 1) if move else other
                        row = jnp.where(lane_row == yg, other, row)
                    rows.append(row)
                shuffled[8 * bz + 4 * half + quad] = jnp.concatenate(rows, axis=0)
        return carry

    lax.fori_loop(0, 4, shuffle, 0)
    ask_copy.wait()
    lane_place = lax.rem(lane // BRICK, MOST)

    def fill(other):
        tile = jnp.zeros((16, 128), F32)
        for k in range(MOST):
            index = ask_smem[other, 0, k]
            moved = pltpu.roll(shuffled[index // 4], lax.rem(BRICK * (k - lax.rem(index, 4)) + 128, 128), 1)
            tile = jnp.where(lane_place == k, moved, tile)
        brick_out[other] = tile.astype(BF16)

    def answer(step, carry):
        other = far(step)
        fill(other)
        pltpu.make_async_remote_copy(
            src_ref=brick_out.at[other], dst_ref=brick_in.at[px],
            send_sem=brick_sem.at[4], recv_sem=brick_sem.at[5],
            device_id=(other, py), device_id_type=MESH,
        ).start()
        return carry

    lax.fori_loop(1, PX, answer, 0, unroll=2)
    fill(px)
    pltpu.make_async_copy(brick_out.at[px], brick_in.at[px], brick_sem.at[5]).start()

    collect(b3, recv3, CENTRE_Y, yc, 3)
    packed = yc.reshape(PX * 48, 128)

    def z_backward(yp, carry):
        columns = []
        for u in range(2):
            parts = []
            for quad in range(2):
                rows = [packed[pl.ds(24 * quad + 8 * g + 2 * yp + u, PX, stride=48), :] for g in range(3)]
                parts += unpack(rows)
            columns.append(jnp.concatenate(parts, axis=0))
        back = z_inverse(columns)
        parts = []
        for u in range(2):
            rows = back[:, 128 * u:128 * u + 128].reshape(PY, 4, 8, 128)
            parts += [part.reshape(PY, 8, 128) for part in pack([rows[:, g].reshape(64, 128) for g in range(4)])]
        s4[yp] = encode(jnp.concatenate(parts, axis=1), CENTRE_BACK)
        pltpu.make_async_copy(s4.at[yp, py], b4.at[py, yp], recv4.at[yp]).start()

        def send(step, inner):
            other = lax.rem(py + step, PY)
            pltpu.make_async_remote_copy(
                src_ref=s4.at[yp, other], dst_ref=b4.at[py, yp],
                send_sem=send4.at[yp], recv_sem=recv4.at[yp],
                device_id=(px, other), device_id_type=MESH,
            ).start()
            return inner

        return lax.fori_loop(1, PY, send, carry)

    lax.fori_loop(0, 4, z_backward, 0)
    info_copy.wait()
    loads[14].wait()
    pltpu.make_async_copy(brick_in, brick_in, brick_sem.at[5]).wait()

    def take(slot, carry):
        tile = brick_in[info_smem[slot, 1]].astype(F32)
        tile = pltpu.roll(tile, lax.rem(128 - BRICK * info_smem[slot, 2], 128), 1)
        tiles[pl.ds(pl.multiple_of(16 * slot, 16), 16), :] = tile.astype(BF16)
        return carry

    lax.fori_loop(0, 32, take, 0, unroll=8)
    cell = lax.broadcasted_iota(jnp.int32, (128, 512), 1)
    origin = lax.broadcasted_iota(jnp.int32, (128, 512), 0)
    spread = (origin == 32 * (cell // 128) + lax.rem(cell, BRICK)).astype(F32).astype(BF16)
    wide = dot(tiles[...], spread)
    tile_row = lax.broadcasted_iota(jnp.int32, (512, 512), 0)
    tile_cell = lax.broadcasted_iota(jnp.int32, (512, 512), 1)
    wide = jnp.where(lax.rem(tile_row, 16) == lax.rem(tile_cell, 128) // BRICK, wide, 0.0).astype(BF16)
    slot_down = lax.broadcasted_iota(jnp.int32, (32, 512), 0)
    slot_cell = lax.broadcasted_iota(jnp.int32, (32, 512), 1)
    samples[...] = dot((slot_down == slot_cell // 16).astype(F32).astype(BF16), wide)

    def embed(group, carry):
        for item in range(4):
            slot = 4 * group + item
            fragment = info_smem[slot, 0]
            weighted = turned_basis[fragment] * samples[pl.ds(slot, 1), :].astype(BF16)
            fock_out[slot] = fock_ref[slot] + dot(weighted, basis_ref[fragment]).T
        slots = pl.ds(4 * group, 4)
        pltpu.make_async_copy(fock_out.at[slots], fock_hbm_out.at[slots], fock_sem.at[group]).start()
        return carry

    lax.fori_loop(0, 8, embed, 0)

    def x_backward(yp, carry):
        chunk = b4.at[:, yp]
        pltpu.make_async_copy(chunk, chunk, recv4.at[yp]).wait()
        wide = []
        for j in range(PY):
            rows = decode(b4[j, yp], CENTRE_BACK)
            parts = []
            for u in range(2):
                parts += unpack([rows[24 * u + 8 * g:24 * u + 8 * g + 8] for g in range(3)])
            wide.append(jnp.concatenate(parts, axis=0))
        back = x_inverse(jnp.concatenate(wide, axis=1), SITES)
        slabs = pl.ds(2 * yp, 2)
        for f in range(SITES):
            corr_out[f, slabs] = back[64 * f:64 * f + 64].reshape(2, 32, N)
        pltpu.make_async_copy(corr_out.at[:, slabs], corr_hbm_out.at[:, slabs], corr_sem.at[yp]).start()
        return carry

    lax.fori_loop(0, 4, x_backward, 0)
    potential_copy.wait()
    for part in range(4):
        slabs = pl.ds(2 * part, 2)
        pltpu.make_async_copy(corr_out.at[:, slabs], corr_hbm_out.at[:, slabs], corr_sem.at[part]).wait()
    for part in range(8):
        slots = pl.ds(4 * part, 4)
        pltpu.make_async_copy(fock_out.at[slots], fock_hbm_out.at[slots], fock_sem.at[part]).wait()

    for part in range(4):
        sent = s1.at[pl.ds(0, PY - 1), 0]
        pltpu.make_async_copy(sent, sent, send1.at[part]).wait()
        if part < 3:
            sent = s2.at[pl.ds(0, PX - 1), 0]
            pltpu.make_async_copy(sent, sent, send2.at[part]).wait()
            sent = s3.at[pl.ds(0, PX - 1), 0]
            pltpu.make_async_copy(sent, sent, send3.at[part]).wait()
        sent = s4.at[0, pl.ds(0, PY - 1)]
        pltpu.make_async_copy(sent, sent, send4.at[part]).wait()
    sent = s3p.at[pl.ds(0, PX - 1)]
    pltpu.make_async_copy(sent, sent, pot_sem.at[0]).wait()
    sent = s4p.at[:, pl.ds(0, 32 * (PY - 1))]
    pltpu.make_async_copy(sent, sent, pot_sem.at[2]).wait()
    sent = ask_out.at[pl.ds(0, PX - 1)]
    pltpu.make_async_copy(sent, sent, brick_sem.at[1]).wait()
    sent = brick_out.at[pl.ds(0, PX - 1)]
    pltpu.make_async_copy(sent, sent, brick_sem.at[4]).wait()


def store_kernel(*refs):
    sources, targets, held, in_sem, out_sem = refs[:3], refs[3:6], refs[6:9], refs[9], refs[10]
    loads, stores = [], []
    for i in range(3):
        count = (3, 1, 8)[i]
        step = sources[i].shape[0] // count
        for part in range(count):
            rows = pl.ds(part * step, step)
            sem = len(loads)
            loads.append(pltpu.make_async_copy(sources[i].at[rows], held[i].at[rows], in_sem.at[sem]))
            stores.append(pltpu.make_async_copy(held[i].at[rows], targets[i].at[rows], out_sem.at[sem]))
    for load in loads:
        load.start()
    for load, store in zip(loads, stores):
        load.wait()
        store.start()
    for store in stores:
        store.wait()


def shards(
    corr, solute_pot, chi, site_charge, home_slab, brick_index, block_slot, basis_values, fock_in
):
    hbm = pl.BlockSpec(memory_space=pltpu.HBM)
    dma = pltpu.SemaphoreType.DMA((4,))
    frags = home_slab.shape[0]
    results = pl.pallas_call(
        field_kernel,
        name="fields",
        out_shape=(
            jax.ShapeDtypeStruct((SITES, 8, 32, N), F32),
            jax.ShapeDtypeStruct((8, 32, N), F32),
            jax.ShapeDtypeStruct(fock_in.shape, F32),
        ),
        in_specs=[pl.BlockSpec(memory_space=pltpu.SMEM)] + [hbm] * 18,
        out_specs=(hbm,) * 3,
        scratch_shapes=[
            pltpu.VMEM(corr.shape, F32),
            pltpu.VMEM(corr.shape[1:], F32),
            pltpu.VMEM(fock_in.shape, F32),
            pltpu.VMEM(corr.shape, F32),
            pltpu.VMEM(solute_pot.shape, BF16),
            pltpu.VMEM((SITES, SITES, R, 8, N), F32),
            pltpu.VMEM((SITES, SITES, 8, N), F32),
            pltpu.VMEM((1, frags), jnp.int32),
            pltpu.VMEM((1, frags), jnp.int32),
            pltpu.VMEM((1, frags), jnp.int32),
            pltpu.VMEM(basis_values.shape, BF16),
            pltpu.VMEM(fock_in.shape, F32),
            pltpu.VMEM((N, PY * 128), BF16),
            pltpu.VMEM((N, PY * 128), BF16),
        ] + [pltpu.VMEM((N, N), BF16)] * 8 + [
            pltpu.VMEM((PY, 4, 48, 128), WIRE),
            pltpu.VMEM((PY, 4, 48, 128), WIRE),
            pltpu.VMEM((PX, 3, 16, 128), WIRE),
            pltpu.VMEM((PX, 3, 16, 128), WIRE),
            pltpu.VMEM((PX, 16, 128), F32),
            pltpu.VMEM((PX, 64, 128), F32),
            pltpu.VMEM((8, 128, N), F32),
            pltpu.VMEM((8, 128, N), F32),
            pltpu.VMEM((PX, 16, 128), WIRE),
            pltpu.VMEM((PX, 16, 128), WIRE),
            pltpu.VMEM((PX, 16, 128), F32),
            pltpu.VMEM((2, N, 128), WIRE),
            pltpu.VMEM((PY, 2, 32, 128), WIRE),
            pltpu.VMEM((PX, 3, 16, 128), WIRE),
            pltpu.VMEM((PX, 3, 16, 128), WIRE),
            pltpu.VMEM((PX, 48, 128), F32),
            pltpu.VMEM((4, PY, 48, 128), WIRE),
            pltpu.VMEM((PY, 4, 48, 128), WIRE),
            pltpu.VMEM((4, N, 128), F32),
            pltpu.VMEM((PX, 1, 128), jnp.int32),
            pltpu.VMEM((PX, 1, 128), jnp.int32),
            pltpu.SMEM((PX, 1, 128), jnp.int32),
            pltpu.VMEM((frags, 128), jnp.int32),
            pltpu.SMEM((frags, 128), jnp.int32),
            pltpu.VMEM((2, 8, 32, 128), F32),
            pltpu.VMEM((32, 16, 128), F32),
            pltpu.VMEM((PX, 16, 128), BF16),
            pltpu.VMEM((PX, 16, 128), BF16),
            pltpu.VMEM((frags, 128, 512), BF16),
            pltpu.VMEM((frags * 16, 128), BF16),
            pltpu.VMEM((frags, 512), F32),
            pltpu.SemaphoreType.DMA((19,)),
        ] + [dma] * 9 + [pltpu.SemaphoreType.DMA((6,)), dma, dma, pltpu.SemaphoreType.DMA((8,))],
        compiler_params=pltpu.CompilerParams(
            collective_id=0, has_side_effects=True, vmem_limit_bytes=60 * 2**20
        ),
    )(
        site_charge, corr, solute_pot, chi, home_slab.reshape(1, frags), brick_index.reshape(1, frags),
        block_slot, basis_values, fock_in, *[jnp.asarray(table) for table in tables()],
    )
    shapes = [jax.ShapeDtypeStruct(result.shape, F32) for result in results]
    return pl.pallas_call(
        store_kernel,
        name="store",
        out_shape=tuple(shapes),
        in_specs=[hbm] * 3,
        out_specs=(hbm,) * 3,
        scratch_shapes=[pltpu.VMEM(shape.shape, F32) for shape in shapes] + [pltpu.SemaphoreType.DMA((12,))] * 2,
        compiler_params=pltpu.CompilerParams(vmem_limit_bytes=60 * 2**20),
    )(*results)


def solution(mesh):
    return jax.shard_map(
        shards,
        mesh=mesh,
        in_specs=(
            P(None, "px", "py", None),
            P(None, "px", "py", None),
            P(None, None, None, "py", "px", None),
            P(),
            P(("px", "py"), None),
            P(("px", "py")),
            P(("px", "py"), None),
            P(("px", "py"), None, None),
            P(("px", "py"), None, None),
        ),
        out_specs=(P(None, "px", "py", None), P("px", "py", None), P(("px", "py"), None, None)),
        check_vma=False,
    )
```
